32 devices in a mesh: cases: 2 (over x), frdm: 16 (over z, y, core).
Axes of the slice: x: 2, y: 2, z: 4, core: 2. Of those that a mesh axis runs over, the one named last changes fastest.
Arguments:
- loads: bfloat16 [32768, 896], P(('cases', 'frdm')), parts along dimension 0, may hold values from -2 to 2
- shapes: bfloat16 [16384, 2048], P('frdm'), may hold values from -0.1875 to 0.1875
- mode_order: int32 [2048], replicated, may hold values from 0 to 2047, each once
- partner: int32 [2048], replicated, may hold values from 0 to 2047, as said below
- taps: float32 [2048, 513], replicated, may hold values from -0.25 to 0.25
- offsets: int32 [2048], replicated, may hold values from 0 to 128
- coef: bfloat16 [2, 2048], P(None, 'frdm'), may hold values from -1.5 to 1.5
Outputs:
- displacement: bfloat16 [32768, 256], P(('cases', 'frdm')), parts along dimension 0
The draws below stay inside these ranges and needn't reach their ends.
There are 2 independent parts, one for each index of `cases`. The reference program is written for one: setup_inputs(seed, part) draws one part's arguments, and reference() takes and returns one part's arrays. A program takes and returns all parts, laid end to end along the dimension named above; an argument that names none is the same for every part. Nothing has to cross between parts.
Inputs may be any that keep to these rules, and one draw needn't show every extreme that they name: `mode_order`: each mode appears once. partner[partner[m]] = m for every mode; exactly two modes are their own partners.
All inputs are finite; a program needn't handle non-finite values.
Results may differ from the reference program's by a relative error of at most 0.0057.
Values may be sent and summed in bfloat16 or wider, within the bound.
No kernel may reach another device: no remote copies, remote signals or barrier semaphores. Data moves between devices by JAX's collectives and lax.ppermute only.
A program may use at most 64 MiB of HBM per device.

```python
import jax
import jax.numpy as jnp
from jax import lax

M = 2048
K = 513
W = 256
DELAY = 128
FREEDOMS = 16384
HIST = 896


def draw_partner(key, part):
    shuffled = jax.random.permutation(key, M).astype(jnp.int32)
    position = jnp.arange(M, dtype=jnp.int32)
    mate_pos = jnp.where(position < 2, position, jnp.bitwise_xor(position, 1)).astype(jnp.int32)
    return jnp.zeros((M,), jnp.int32).at[shuffled].set(shuffled[mate_pos]).astype(jnp.int32)


def draw_offsets(key, part):
    base_values = jax.random.randint(jax.random.fold_in(key, 11), (M,), 0, DELAY + 1).astype(jnp.int32)
    top_spot = jax.random.randint(jax.random.fold_in(key, 12), (), 0, M).astype(jnp.int32)
    low_spot = ((top_spot + 1) % M).astype(jnp.int32)
    return base_values.at[top_spot].set(DELAY).at[low_spot].set(0).astype(jnp.int32)


def strengthened(drawn, key, source, target, parts, factor):
    def block_of(axis_at):
        return (jnp.arange(drawn.shape[axis_at]) // (drawn.shape[axis_at] // parts)).reshape((-1,) + (1,) * (drawn.ndim - 1 - axis_at))

    first = jax.random.permutation(key, parts)[block_of(target)]
    far = (block_of(target) + parts // 2) % parts
    return jnp.where((block_of(source) == first) | (block_of(source) == far), factor * drawn, drawn)


def shard_levels(stream_key, shape, pieces, smallest, largest):
    loudness = 1.0
    for dim, blocks in pieces:
        draws = jax.random.uniform(jax.random.fold_in(jax.random.fold_in(stream_key, 6), dim), (blocks,), jnp.float32, smallest / len(pieces), largest / len(pieces))
        loudness = loudness * jnp.repeat(jnp.exp(draws), shape[dim] // blocks).reshape((-1,) + (1,) * (len(shape) - 1 - dim))
    return loudness


def scatter_about(rng, dims, width, limit, cuts=(), kind=jnp.bfloat16):
    array = width * jax.random.normal(rng, dims, jnp.float32)
    if cuts:
        array = array * shard_levels(rng, dims, cuts, -0.22, 0.18)
    return jnp.clip(array, -limit, limit).astype(kind)


def heavy_noise(rng, dims, spread, bound, pieces, heavy, kind=jnp.bfloat16):
    array = spread * jax.random.normal(rng, dims, jnp.float32)
    if pieces:
        array = array * shard_levels(rng, dims, pieces, -0.22, 0.18)
    return jnp.clip(strengthened(array, jax.random.fold_in(rng, 3), *heavy), -bound, bound).astype(kind)


def setup_inputs(seed: int = 0, part: int = 0) -> dict:
    streams_of = jax.random.split(jax.random.key(seed), 8)
    part_splits = jax.random.split(jax.random.fold_in(streams_of[7], part), 8)
    return {
        "loads": scatter_about(part_splits[0], (FREEDOMS, HIST), ((M / FREEDOMS) ** 0.5), 2.0, ((0, 16),)),
        "shapes": heavy_noise(streams_of[1], (FREEDOMS, M), M ** -0.5, 0.1875, ((0, 16),), (0, 1, 16, 2.0)),
        "mode_order": jax.random.permutation(streams_of[2], M).astype(jnp.int32),
        "partner": draw_partner(jax.random.fold_in(streams_of[7], 71), part),
        "taps": scatter_about(streams_of[4], (M, K), K ** -0.5, 0.25, (), jnp.float32),
        "offsets": draw_offsets(jax.random.fold_in(streams_of[7], 71), part),
        "coef": jnp.clip(jax.random.uniform(streams_of[6], (2, M), jnp.float32, -1.5, 1.5) * shard_levels(streams_of[6], (2, M), ((1, 16),), -0.4, 0.0), -1.5, 1.5).astype(jnp.bfloat16),
    }


def convolve(modal_forces, tap_table, offset_table):
    mode_count = modal_forces.shape[0]
    block_size = min(32, mode_count)
    window_len = W + K - 1
    tap_index = (jnp.arange(W, dtype=jnp.int32)[:, None] + (K - 1) - jnp.arange(K, dtype=jnp.int32)[None, :]).astype(jnp.int32)

    def convolve_block(block_args):
        force_rows, tap_rows, offset_rows = block_args
        windows = jax.vmap(lambda r, o: lax.dynamic_slice(r, (o,), (window_len,)))(force_rows, offset_rows)
        toeplitz = windows[:, tap_index]
        return jnp.sum(toeplitz * tap_rows[:, None, :], axis=-1)

    results = lax.map(convolve_block, (modal_forces.reshape(mode_count // block_size, block_size, -1), tap_table.reshape(mode_count // block_size, block_size, K), offset_table.reshape(mode_count // block_size, block_size)))
    return results.reshape(mode_count, W)


def reference(loads, shapes, mode_order, partner, taps, offsets, coef):
    slot_of = jnp.zeros((M,), jnp.int32).at[mode_order].set(jnp.arange(M, dtype=jnp.int32))
    modal_mode = lax.dot_general(shapes, loads, (((0,), (0,)), ((), ())), preferred_element_type=jnp.float32)
    modal_forces = modal_mode[mode_order]
    response = convolve(modal_forces, taps, offsets.astype(jnp.int32)).astype(jnp.bfloat16)
    own_rows = response[slot_of].astype(jnp.float32)
    mate_rows = response[slot_of[partner]].astype(jnp.float32)
    direct = coef[0][slot_of].astype(jnp.float32)
    across = coef[1][slot_of].astype(jnp.float32)
    paired = (direct[:, None] * own_rows + across[:, None] * mate_rows).astype(jnp.bfloat16)
    return jnp.dot(shapes, paired, preferred_element_type=jnp.float32).astype(jnp.bfloat16)
```

```python
import functools

import jax
import jax.numpy as jnp
import numpy as np
from jax import lax
from jax.experimental import pallas as pl
from jax.experimental.pallas import tpu as pltpu
from jax.sharding import PartitionSpec as P

W = 256
BF = jnp.bfloat16
F32 = jnp.float32
VMEM_BYTES = 56 * 1024 * 1024
NT = (((1,), (1,)), ((), ()))
NN = (((1,), (0,)), ((), ()))


def dot(a, b, dims=NN):
    return lax.dot_general(a, b, dims, preferred_element_type=F32)


def split(table):
    high = table.astype(BF)
    low = (table - high.astype(np.float64)).astype(BF)
    return high, low


def tables(hist, taps):
    half = hist // 2
    odd = 2 * np.arange(half)[:, None] + 1

    def turn(n):
        angle = (odd * n[None, :]) % (2 * hist) * (np.pi / hist)
        return np.cos(angle), np.sin(angle)

    cos, sin = turn(np.arange(hist))
    forward = np.concatenate([cos, -sin])
    cos, sin = turn(np.arange(taps))
    tap_forward = np.concatenate([cos, -sin])
    delay = hist - W - taps + 1
    cos, sin = turn(np.arange(delay + 1))
    phase = np.concatenate([cos, sin])
    cos, sin = turn(np.arange(W) + taps - 1)
    inverse = np.concatenate([cos, -sin]).T * (2.0 / hist)
    return forward, tap_forward, phase, inverse


def params(**kw):
    return pltpu.CompilerParams(vmem_limit_bytes=VMEM_BYTES, **kw)


def once(shape):
    return pl.BlockSpec(shape, lambda *_: (0,) * len(shape), pipeline_mode=pl.Buffered(1))


def project_kernel(place, loads, fhi, flo, shapes, out, lft):
    @pl.when(pl.program_id(0) == 0)
    def _():
        rows = loads.shape[0]
        step = 256
        for r in range(0, rows, step):
            part = loads[r : r + step, :]
            lft[:, r : r + step] = (dot(fhi[...], part, NT) + dot(flo[...], part, NT)).astype(BF)

    out[...] = dot(lft[...], shapes[...]).astype(BF)


def project(place, loads, fhi, flo, shapes, tile=256):
    hist = loads.shape[1]
    rows, modes = shapes.shape
    half = modes // 2
    steps = half // tile
    return pl.pallas_call(
        project_kernel,
        grid_spec=pltpu.PrefetchScalarGridSpec(
            num_scalar_prefetch=1,
            grid=(steps,),
            in_specs=[
                once(loads.shape),
                once(fhi.shape),
                once(flo.shape),
                pl.BlockSpec((rows, tile), lambda i, s: (0, (1 - s[0]) * steps + i)),
            ],
            out_specs=[
                pl.BlockSpec((hist, tile), lambda i, s: (0, i)),
                pl.BlockSpec((hist, rows), lambda i, s: (0, 0)),
            ],
        ),
        out_shape=[
            jax.ShapeDtypeStruct((hist, half), BF),
            jax.ShapeDtypeStruct((hist, rows), BF),
        ],
        compiler_params=params(),
        name="project",
    )(place, loads, fhi, flo, shapes)


def spectrum_kernel(place, slots, offs, taps, thi, tlo, phi, plo, lft, shapes, spec, own, picked):
    tile = shapes.shape[1]
    half = spec.shape[0] // 2
    base = (place[0] * pl.num_programs(0) + pl.program_id(0)) * tile

    def pick(r, _):
        picked[pl.ds(r, 1), :] = taps[pl.ds(slots[base + r], 1), :]
        return _

    lax.fori_loop(0, tile, pick, 0, unroll=8)
    own[...] = dot(lft[...], shapes[...])
    row = picked[...]
    high = row.astype(BF)
    low = (row - high.astype(F32)).astype(BF)
    resp = dot(thi[...], high, NT) + dot(tlo[...], high, NT) + dot(thi[...], low, NT)
    hot = (lax.broadcasted_iota(jnp.int32, (phi.shape[1], tile), 0) == offs[...]).astype(F32).astype(BF)
    turn = dot(phi[...], hot) + dot(plo[...], hot)
    cos, sin = turn[:half], turn[half:]
    re, im = resp[:half], resp[half:]
    spec[:half, :] = cos * re - sin * im
    spec[half:, :] = sin * re + cos * im


def spectrum(place, slots, offs, taps, thi, tlo, phi, plo, lft, shapes, tile=256):
    hist = lft.shape[0]
    rows, modes = shapes.shape
    half = modes // 2
    steps = half // tile
    return pl.pallas_call(
        spectrum_kernel,
        grid_spec=pltpu.PrefetchScalarGridSpec(
            num_scalar_prefetch=2,
            grid=(steps,),
            in_specs=[
                pl.BlockSpec((1, tile), lambda i, s, _: (0, s[0] * steps + i)),
                once(taps.shape),
                once(thi.shape),
                once(tlo.shape),
                once(phi.shape),
                once(plo.shape),
                once(lft.shape),
                pl.BlockSpec((rows, tile), lambda i, s, _: (0, s[0] * steps + i)),
            ],
            out_specs=[
                pl.BlockSpec((hist, tile), lambda i, s, _: (0, i)),
                pl.BlockSpec((hist, tile), lambda i, s, _: (0, i)),
            ],
            scratch_shapes=[pltpu.VMEM((tile, taps.shape[1]), F32)],
        ),
        out_shape=[jax.ShapeDtypeStruct((hist, half), F32)] * 2,
        compiler_params=params(),
        name="spectrum",
    )(place, slots, offs, taps, thi, tlo, phi, plo, lft, shapes)


def respond_kernel(own, other, spec, ihi, ilo, out):
    half = spec.shape[0] // 2
    total = own[...] + other[...].astype(F32)
    re, im = total[:half], total[half:]
    tre, tim = spec[:half, :], spec[half:, :]
    product = jnp.concatenate([re * tre - im * tim, re * tim + im * tre], axis=0).astype(BF)
    out[...] = dot(ihi[...], product) + dot(ilo[...], product)


def respond(own, other, spec, ihi, ilo, tile=256):
    hist, half = own.shape
    block = pl.BlockSpec((hist, tile), lambda i: (0, i))
    return pl.pallas_call(
        respond_kernel,
        grid=(half // tile,),
        in_specs=[block, block, block, once(ihi.shape), once(ilo.shape)],
        out_specs=pl.BlockSpec((W, tile), lambda i: (0, i)),
        out_shape=jax.ShapeDtypeStruct((W, half), F32),
        compiler_params=params(),
        name="respond",
    )(own, other, spec, ihi, ilo)


def expand_kernel(place, resp, mate, coef, shapes, out, acc):
    step = pl.program_id(0)
    modes = resp.shape[1]
    tile = shapes.shape[1]
    hot = (lax.broadcasted_iota(jnp.int32, (modes, tile), 0) == mate[0:1, :]).astype(F32).astype(BF)
    self_hot = (lax.broadcasted_iota(jnp.int32, (modes, tile), 0) == mate[1:2, :]).astype(F32).astype(BF)
    across = dot(resp[...], hot)
    direct = dot(resp[...], self_hot)
    paired = (coef[0:1, :] * direct + coef[1:2, :] * across).astype(BF)
    part = dot(shapes[...], paired, NT)

    @pl.when(step == 0)
    def _():
        acc[...] = part

    @pl.when(step > 0)
    def _():
        acc[...] += part

    @pl.when(step == pl.num_programs(0) - 1)
    def _():
        out[...] = acc[...].astype(BF)


def expand(place, resp, mate, coef, shapes, tile=256):
    rows, modes = shapes.shape
    return pl.pallas_call(
        expand_kernel,
        grid_spec=pltpu.PrefetchScalarGridSpec(
            num_scalar_prefetch=1,
            grid=(modes // tile,),
            in_specs=[
                once(resp.shape),
                pl.BlockSpec((2, tile), lambda i, s: (0, i)),
                pl.BlockSpec((2, tile), lambda i, s: (0, i)),
                pl.BlockSpec((rows, tile), lambda i, s: (0, i)),
            ],
            out_specs=pl.BlockSpec((rows, W), lambda i, s: (0, 0)),
            scratch_shapes=[pltpu.VMEM((rows, W), F32)],
        ),
        out_shape=jax.ShapeDtypeStruct((rows, W), BF),
        compiler_params=params(),
        name="expand",
    )(place, resp, mate, coef, shapes)


def swap(x, devices, bits):
    return lax.ppermute(x, "frdm", [(i, i ^ bits) for i in range(devices)])


def columns(x, start, size):
    return lax.dynamic_slice_in_dim(x, start, size, 1)


def shards(devices, loads, shapes, mode_order, partner, taps, offsets, coef):
    modes = shapes.shape[1]
    half = modes // 2
    me = lax.axis_index("frdm")
    core = me & 1
    forward, tap_forward, phase, inverse = tables(loads.shape[1], taps.shape[1])
    pad = -phase.shape[1] % 128
    phase = np.pad(phase, ((0, 0), (0, pad)))
    place = core.reshape(1).astype(jnp.int32)

    all_coef = lax.all_gather(coef, "frdm", axis=1, tiled=True)
    slot_of = jnp.zeros((modes,), jnp.int32).at[mode_order].set(jnp.arange(modes, dtype=jnp.int32))
    mode_offsets = offsets[slot_of][None]
    mode_coef = all_coef[:, slot_of].astype(F32)

    sent, lft = project(place, loads, *split(forward), shapes)
    got = swap(sent, devices, 1)
    spec, own = spectrum(place, slot_of, mode_offsets, taps, *split(tap_forward), *split(phase), lft, shapes)
    resp = respond(own, got, spec, *split(inverse))
    if devices == 16:
        y, z = (me >> 1) & 1, me >> 2
        quarter, block = half // 2, half // 8
        got = swap(columns(resp, (1 - y) * quarter, quarter).astype(BF), devices, 2)
        resp = columns(resp, y * quarter, quarter) + got.astype(F32)
        parts = [columns(resp, (z ^ d) * block, block) for d in range(4)]
        total = parts[0]
        for d in (1, 2, 3):
            total = total + swap(parts[d].astype(BF), devices, 4 * d).astype(F32)
        total = total.astype(BF)
        resp = jnp.concatenate([total] + [swap(total, devices, 4 * d) for d in (1, 2, 3)], axis=1)
        resp = jnp.concatenate([resp, swap(resp, devices, 2)], axis=1)
        mask = ((core * 8 + y * 4 + z) * block).astype(jnp.int32)
    else:
        groups = [list(range(c, devices, 2)) for c in range(2)]
        resp = lax.psum(resp, "frdm", axis_index_groups=groups).astype(BF)
        mask = (core * half).astype(jnp.int32)
    resp = jnp.concatenate([resp, swap(resp, devices, 1)], axis=1)
    mate = jnp.stack([partner, jnp.arange(modes, dtype=jnp.int32)]) ^ mask
    return expand(place, resp, mate, mode_coef, shapes)


def solution(mesh):
    in_specs = (P(("cases", "frdm"), None), P("frdm", None), P(), P(), P(), P(), P(None, "frdm"))
    out_specs = P(("cases", "frdm"), None)
    body = functools.partial(shards, mesh.shape["frdm"])
    return jax.shard_map(body, mesh=mesh, in_specs=in_specs, out_specs=out_specs, check_vma=False)
```

```python
import functools

import jax
import jax.numpy as jnp
import numpy as np
from jax import lax
from jax.experimental import pallas as pl
from jax.experimental.pallas import tpu as pltpu
from jax.sharding import PartitionSpec as P

W = 256
LANES = 128
EXTRA = 16
BF = jnp.bfloat16
F32 = jnp.float32
I32 = jnp.int32
NT = (((1,), (1,)), ((), ()))
NN = (((1,), (0,)), ((), ()))


def dot(a, b, dims=NN):
    return lax.dot_general(a, b, dims, preferred_element_type=F32)


def split(table):
    high = table.astype(BF)
    low = (table - high.astype(np.float64)).astype(BF)
    return high, low


def turns(half, n):
    odd = 2 * np.arange(half)[:, None] + 1
    angle = (odd * n[None, :]) % (4 * half) * (np.pi / (2 * half))
    return np.cos(angle), np.sin(angle)


def forward_table(hist):
    cos, sin = turns(hist // 2, np.arange(hist))
    return np.concatenate(split(np.concatenate([cos, -sin])), axis=1)


def tap_table(hist, taps):
    cos, sin = turns(hist // 2, np.arange(taps))
    table = np.concatenate([cos, -sin])
    high, low = split(table[:, :-1])
    last = np.repeat(table[:, -1:], LANES, axis=1).astype(np.float32)
    return np.concatenate([high, low, high], axis=1), last


def phase_table(hist, delay):
    cos, sin = turns(hist // 2, np.arange(1, delay + 1))
    return np.concatenate(split(np.concatenate([cos - 1.0, sin])), axis=1)


def inverse_table(hist, taps):
    cos, sin = turns(hist // 2, np.arange(W) + taps - 1)
    return np.concatenate(split(np.concatenate([cos, -sin]).T * (2.0 / hist)), axis=1)


def call(kernel, name, out_shape, *args, scalars=1, scratch=(), limit=20):
    vmem = pl.BlockSpec(memory_space=pltpu.VMEM)
    smem = pl.BlockSpec(memory_space=pltpu.SMEM)
    return pl.pallas_call(
        kernel,
        in_specs=[smem] * scalars + [vmem] * (len(args) - scalars),
        out_specs=[vmem] * len(out_shape),
        out_shape=out_shape,
        scratch_shapes=list(scratch),
        compiler_params=pltpu.CompilerParams(vmem_limit_bytes=limit * 1024 * 1024),
        name=name,
    )(*args)


def array(*shape, dtype=BF):
    return jax.ShapeDtypeStruct(shape, dtype)


def block(start, size):
    return pl.ds(pl.multiple_of(start, LANES), size)


def hot(mask):
    return mask.astype(F32).astype(BF)


def project_kernel(place, loads, table, shapes, coef, sent, lft):
    rows, half = loads.shape[0], sent.shape[1]
    hist = lft.shape[0]
    for r in range(0, rows, 256):
        part = loads[r : r + 256, :]
        lft[:, r : r + 256] = dot(table[...], jnp.concatenate([part, part], axis=1), NT).astype(BF)
    base = (1 - place[0]) * half
    for c in range(0, half, 256):
        sent[:hist, c : c + 256] = dot(lft[...], shapes[:, block(base + c, 256)]).astype(BF)
    sent[hist:, :] = jnp.zeros((EXTRA, half), BF)
    per = coef.shape[1]
    sent[hist : hist + 2, :per] = coef[...]


def spectrum(base, taps, offsets, order, table, last, phase, stack, put, width):
    count = taps.shape[0] - 1
    half = table.shape[0] // 2
    for r in range(0, count, 64):
        row = taps[r : r + 64, :]
        high = row.astype(BF)
        stack[r : r + 64, :] = high
        stack[count + r : count + r + 64, :] = (row - high.astype(F32)).astype(BF)
    row = taps[count : count + 1, :]
    high = row.astype(BF).astype(F32)
    index = lax.broadcasted_iota(I32, (EXTRA, taps.shape[1]), 0)
    tail = jnp.where(index == 0, high, jnp.where(index == 1, row - high, jnp.where(index == 2, offsets[...].astype(F32), 0.0)))
    stack[2 * count :, :] = tail.astype(BF)
    delay = phase.shape[1] // 2
    for c in range(0, width, 256):
        mode = lax.broadcasted_iota(I32, (256, taps.shape[1]), 0) + (base + c)
        picked = dot(stack[...], hot(mode == order[...]), NT)
        main = picked[: 2 * count].astype(BF)
        tail = picked[2 * count :]
        end = tail[0:1] + tail[1:2]
        offset = tail[2:3].astype(I32)
        resp = dot(table[...], jnp.concatenate([main[:count], main], axis=0))
        resp = resp + jnp.tile(last[...], (1, 2)) * end
        which = hot(lax.broadcasted_iota(I32, (delay, 256), 0) + 1 == offset)
        turn = dot(phase[...], jnp.concatenate([which, which], axis=0))
        cos, sin = turn[:half] + 1.0, turn[half:]
        re, im = resp[:half], resp[half:]
        put(c, cos * re - sin * im, sin * re + cos * im)


def spectrum_kernel(place, taps, offsets, order, table, last, phase, lft, shapes, spec, own, stack):
    width = spec.shape[1]
    half = spec.shape[0] // 2
    base = place[0]
    for c in range(0, width, 256):
        own[:, c : c + 256] = dot(lft[...], shapes[:, block(base + c, 256)])

    def put(c, re, im):
        spec[:half, c : c + 256] = re
        spec[half:, c : c + 256] = im

    spectrum(base, taps, offsets, order, table, last, phase, stack, put, width)


def respond_kernel(place, own, other, spec, inverse, coef, out):
    hist, width = own.shape
    half = hist // 2
    start = place[0]
    for c in range(0, width, 256):
        total = own[:, c : c + 256] + other[:hist, block(start + c, 256)].astype(F32)
        re, im = total[:half], total[half:]
        tre, tim = spec[:half, c : c + 256], spec[half:, c : c + 256]
        product = jnp.concatenate([re * tre - im * tim, re * tim + im * tre], axis=0).astype(BF)
        result = dot(inverse[...], jnp.concatenate([product, product], axis=0))
        out[:W, c : c + 256] = result.astype(out.dtype)
    if out.shape[0] > W:
        out[W:, :] = jnp.zeros((EXTRA, width), BF)
        out[W : W + 2, :LANES] = coef[...]
        out[W + 2 : W + 4, :LANES] = other[hist : hist + 2, :LANES]


def fold_kernel(place, own, got, coef, other, keep, known, first, second, third):
    z = place[0]
    size = keep.shape[1]
    hist = other.shape[0] - EXTRA
    known[...] = jnp.zeros(known.shape, BF)
    known[0:2, :] = coef[...]
    known[2:4, :] = other[hist : hist + 2, :LANES]
    known[4:8, :] = got[W : W + 4, :LANES]
    for d, out in enumerate((keep, first, second, third)):
        where = block((z ^ d) * size, size)
        total = own[:, where] + got[:W, where].astype(F32)
        out[:W, :] = total.astype(out.dtype)
        if d:
            out[W:, :] = known[...]


def settle_kernel(keep, first, second, third, out):
    total = keep[...]
    for got in (first, second, third):
        total = total + got[:W, :].astype(F32)
    out[...] = total.astype(BF)


def mixers_kernel(place, order, partner, known, first, second, third, coef, pick, held):
    me, mask = place[0], place[1]
    modes = order.shape[1]
    held[...] = jnp.zeros(held.shape, F32)
    for z, rows in enumerate((known, first, second, third)):
        top = rows.shape[0] - EXTRA
        for low in range(4):
            where = block((me ^ (4 * z + low)) * LANES, LANES)
            held[0:2, where] = rows[top : top + EXTRA, :].astype(F32)[2 * low : 2 * low + 2]
    mixers(order, partner, mask, held, coef, pick)


def mixers(order, partner, mask, held, coef, pick):
    modes = order.shape[1]
    table = held[...].astype(BF)
    for c in range(0, modes, 256):
        mode = lax.broadcasted_iota(I32, (256, modes), 0) + c
        coef[:, c : c + 256] = dot(table, hot(mode == order[...]), NT)
        mode = lax.broadcasted_iota(I32, (256, modes), 0) + c
        pick[c : c + 256, :] = hot((mode ^ mask) == partner[...])


def plain_mixers_kernel(place, order, partner, every, coef, pick, held):
    held[...] = jnp.zeros(held.shape, F32)
    held[0:2, :] = every[...].astype(F32)
    mixers(order, partner, place[1], held, coef, pick)


def mate_kernel(resp, pick, out):
    for c in range(0, out.shape[1], 256):
        out[:, c : c + 256] = dot(resp[...], pick[: resp.shape[1], c : c + 256])


def expand_kernel(place, resp, other, mates, coef, pick, shapes, out, paired):
    half = resp.shape[1]
    mask = place[1]
    for c in range(0, 2 * half, 256):
        across = mates[:, c : c + 256] + dot(other[...], pick[half:, c : c + 256])
        for k in (c, c + LANES):
            start = mask ^ k
            mine = resp[:, block(start & (half - 1), LANES)].astype(F32)
            theirs = other[:, block(start & (half - 1), LANES)].astype(F32)
            direct = jnp.where(start < half, mine, theirs)
            mixed = coef[0:1, k : k + LANES] * direct + coef[1:2, k : k + LANES] * across[:, k - c : k - c + LANES]
            paired[:, k : k + LANES] = mixed.astype(BF)
    rows = out.shape[0]
    for r in range(0, rows, 256):
        out[r : r + 256, :] = dot(shapes[r : r + 256, :], paired[...], NT).astype(BF)


def swap(x, devices, bits):
    return lax.ppermute(x, "frdm", [(i, i ^ bits) for i in range(devices)])


def scalars(*values):
    return jnp.stack([jnp.asarray(v, I32) for v in values])


def shards(devices, loads, shapes, mode_order, partner, taps, offsets, coef):
    rows, modes = shapes.shape
    hist, count = loads.shape[1], taps.shape[1]
    half, quarter = modes // 2, modes // 4
    me = lax.axis_index("frdm").astype(I32)
    core = me & 1
    forward = forward_table(hist)
    tap_forward, last = tap_table(hist, count)
    phase = phase_table(hist, hist - W - count + 1)
    inverse = inverse_table(hist, count)
    order, mates, offsets, taps = mode_order[None], partner[None], offsets[None], taps.T

    sent, lft = call(
        project_kernel, "project", [array(hist + EXTRA, half), array(hist, rows)],
        scalars(core), loads, forward, shapes, coef,
    )
    got = swap(sent, devices, 1)

    def respond(index, out):
        spec, own = call(
            spectrum_kernel, "spectrum", [array(hist, quarter, dtype=F32)] * 2,
            scalars(core * half + index * quarter), taps, offsets, order, tap_forward, last, phase, lft, shapes,
            scratch=[pltpu.VMEM((2 * (count - 1) + EXTRA, modes), BF)],
        )
        return call(respond_kernel, "respond", [out], scalars(index * quarter), own, got, spec, inverse, coef)[0]

    if devices == 16:
        y, z = (me >> 1) & 1, me >> 2
        size = modes // devices
        away = swap(respond(1 - y, array(W + EXTRA, quarter)), devices, 2)
        mine = respond(y, array(W, quarter, dtype=F32))
        keep, known, *parts = call(
            fold_kernel, "fold", [array(W, size, dtype=F32), array(EXTRA, LANES)] + [array(W + EXTRA, size)] * 3,
            scalars(z), mine, away, coef, got,
        )
        parts = [swap(part, devices, 4 * d) for d, part in zip((1, 2, 3), parts)]
        total = call(settle_kernel, "settle", [array(W, size)], keep, *parts, scalars=0)[0]
        place = scalars(me, (core * 8 + y * 4 + z) * size)
        mode_coef, pick = call(
            mixers_kernel, "mixers", [array(8, modes, dtype=F32), array(modes, modes)],
            place, order, mates, known, *parts, scratch=[pltpu.VMEM((8, modes), F32)],
        )
        resp = jnp.concatenate([total] + [swap(total, devices, 4 * d) for d in (1, 2, 3)], axis=1)
        resp = jnp.concatenate([resp, swap(resp, devices, 2)], axis=1)
    else:
        place = scalars(me, core * half)
        mode_coef, pick = call(
            plain_mixers_kernel, "mixers", [array(8, modes, dtype=F32), array(modes, modes)],
            place, order, mates, lax.all_gather(coef, "frdm", axis=1, tiled=True), scratch=[pltpu.VMEM((8, modes), F32)],
        )
        resp = jnp.concatenate([respond(q, array(W, quarter, dtype=F32)) for q in (0, 1)], axis=1)
        groups = [list(range(c, devices, 2)) for c in range(2)]
        resp = lax.psum(resp, "frdm", axis_index_groups=groups).astype(BF)
    other = swap(resp, devices, 1)
    near = call(mate_kernel, "mate", [array(W, modes, dtype=F32)], resp, pick, scalars=0)[0]
    return call(
        expand_kernel, "expand", [array(rows, W)], place, resp, other, near, mode_coef, pick, shapes,
        scratch=[pltpu.VMEM((W, modes), BF)],
    )[0]


def solution(mesh):
    in_specs = (P(("cases", "frdm"), None), P("frdm", None), P(), P(), P(), P(), P(None, "frdm"))
    out_specs = P(("cases", "frdm"), None)
    body = functools.partial(shards, mesh.shape["frdm"])
    return jax.shard_map(body, mesh=mesh, in_specs=in_specs, out_specs=out_specs, check_vma=False)
```

```python
import functools

import jax
import jax.numpy as jnp
import numpy as np
from jax import lax
from jax.experimental import pallas as pl
from jax.experimental.pallas import tpu as pltpu
from jax.sharding import PartitionSpec as P

W = 256
LANES = 128
EXTRA = 16
BF = jnp.bfloat16
F32 = jnp.float32
I32 = jnp.int32
NT = (((1,), (1,)), ((), ()))
NN = (((1,), (0,)), ((), ()))


def dot(a, b, dims=NN):
    return lax.dot_general(a, b, dims, preferred_element_type=F32)


def split(table):
    high = table.astype(BF)
    low = (table - high.astype(np.float64)).astype(BF)
    return high, low


def turns(half, n):
    odd = 2 * np.arange(half)[:, None] + 1
    angle = (odd * n[None, :]) % (4 * half) * (np.pi / (2 * half))
    return np.cos(angle), np.sin(angle)


def forward_table(hist):
    cos, sin = turns(hist // 2, np.arange(hist))
    return np.concatenate(split(np.concatenate([cos, -sin])), axis=1)


def tap_table(hist, taps):
    cos, sin = turns(hist // 2, np.arange(taps))
    table = np.concatenate([cos, -sin])
    last = np.repeat(table[:, -1:], LANES, axis=1).astype(np.float32)
    return np.concatenate(split(table[:, :-1]), axis=1), last


def phase_table(hist, delay):
    cos, sin = turns(hist // 2, np.arange(1, delay + 1))
    return np.concatenate(split(np.concatenate([cos - 1.0, sin])), axis=1)


def inverse_table(hist, taps):
    cos, sin = turns(hist // 2, np.arange(W) + taps - 1)
    return np.concatenate(split(np.concatenate([cos, -sin]).T * (2.0 / hist)), axis=1)


def call(kernel, name, out_shape, *args, scalars=1, far=(), scratch=(), limit=16):
    vmem = pl.BlockSpec(memory_space=pltpu.VMEM)
    smem = pl.BlockSpec(memory_space=pltpu.SMEM)
    hbm = pl.BlockSpec(memory_space=pltpu.HBM)
    places = [smem] * scalars + [vmem] * (len(args) - scalars)
    args = list(args)
    for i in far:
        places[i] = hbm
        args[i] = pltpu.with_memory_space_constraint(jnp.asarray(args[i]), pltpu.HBM)
    return pl.pallas_call(
        kernel,
        in_specs=places,
        out_specs=[vmem] * len(out_shape),
        out_shape=out_shape,
        scratch_shapes=list(scratch),
        compiler_params=pltpu.CompilerParams(vmem_limit_bytes=limit * 1024 * 1024),
        name=name,
    )(*args)


def array(*shape, dtype=BF):
    return jax.ShapeDtypeStruct(shape, dtype)


def near(*shape, dtype=BF):
    return pltpu.VMEM(shape, dtype)


def block(start, size):
    return pl.ds(pl.multiple_of(start, LANES), size)


def hot(mask):
    return mask.astype(F32).astype(BF)


def project_kernel(
    place, loads_far, forward_far, shapes_far, taps_far, table_far, last_far, phase_far, inverse_far, offsets, coef,
    sent, lft, shapes, stack, table, last, phase, inverse, loads, forward, taps, sems,
):
    rows, half = loads.shape[0], sent.shape[1]
    hist = lft.shape[0]
    core = place[0]
    far, own = block((1 - core) * half, half), block(core * half, half)
    pairs = [
        (forward_far, forward),
        (loads_far, loads),
        (shapes_far.at[:, far], shapes.at[:, far]),
        (taps_far, taps),
        (table_far, table),
        (shapes_far.at[:, own], shapes.at[:, own]),
        (last_far, last),
        (phase_far, phase),
        (inverse_far, inverse),
    ]
    copies = [pltpu.make_async_copy(a, b, sems.at[i]) for i, (a, b) in enumerate(pairs)]
    for copy in copies:
        copy.start()
    copies[0].wait()
    copies[1].wait()
    for r in range(0, rows, 256):
        part = loads[r : r + 256, :]
        lft[:, r : r + 256] = dot(forward[...], jnp.concatenate([part, part], axis=1), NT).astype(BF)
    copies[2].wait()
    copies[3].wait()
    count = taps.shape[0] - 1
    for c in range(0, half, 256):
        sent[:hist, c : c + 256] = dot(lft[...], shapes[:, block((1 - core) * half + c, 256)]).astype(BF)
    sent[hist:, :] = jnp.zeros((EXTRA, half), BF)
    per = coef.shape[1]
    sent[hist : hist + 2, :per] = coef[...]
    for r in range(0, count, 64):
        stack[r : r + 64, :] = taps[r : r + 64, :].astype(BF)
    index = lax.broadcasted_iota(I32, (EXTRA, taps.shape[1]), 0)
    end = taps[count : count + 1, :]
    tail = jnp.where(index == 0, end, jnp.where(index == 1, offsets[...].astype(F32), 0.0))
    stack[count:, :] = tail.astype(BF)
    for copy in copies[4:]:
        copy.wait()


def spectrum(base, stack, order, table, last, phase, put, width):
    count = stack.shape[0] - EXTRA
    half = table.shape[0] // 2
    delay = phase.shape[1] // 2
    for c in range(0, width, 256):
        mode = lax.broadcasted_iota(I32, (256, stack.shape[1]), 0) + (base + c)
        picked = dot(stack[...], hot(mode == order[...]), NT)
        main = picked[:count].astype(BF)
        tail = picked[count:]
        end, offset = tail[0:1], tail[1:2].astype(I32)
        resp = dot(table[...], jnp.concatenate([main, main], axis=0))
        resp = resp + jnp.tile(last[...], (1, 2)) * end
        which = hot(lax.broadcasted_iota(I32, (delay, 256), 0) + 1 == offset)
        turn = dot(phase[...], jnp.concatenate([which, which], axis=0))
        cos, sin = turn[:half] + 1.0, turn[half:]
        re, im = resp[:half], resp[half:]
        put(c, cos * re - sin * im, sin * re + cos * im)


def spectrum_kernel(place, stack, order, table, last, phase, lft, shapes, spec, own):
    width = spec.shape[1]
    half = spec.shape[0] // 2
    base = place[0]
    for c in range(0, width, 256):
        own[:, c : c + 256] = dot(lft[...], shapes[:, block(base + c, 256)])

    def put(c, re, im):
        spec[:half, c : c + 256] = re
        spec[half:, c : c + 256] = im

    spectrum(base, stack, order, table, last, phase, put, width)


def impose(total, tre, tim, inverse):
    half = tre.shape[0]
    re, im = total[:half], total[half:]
    product = jnp.concatenate([re * tre - im * tim, re * tim + im * tre], axis=0).astype(BF)
    return dot(inverse[...], jnp.concatenate([product, product], axis=0))


def whole_kernel(place, stack, order, table, last, phase, lft, shapes, other, inverse, out):
    hist = lft.shape[0]
    base, start = place[0], place[1]

    def put(c, re, im):
        total = dot(lft[...], shapes[:, block(base + c, 256)]) + other[:hist, block(start + c, 256)].astype(F32)
        out[:, c : c + 256] = impose(total, re, im, inverse)

    spectrum(base, stack, order, table, last, phase, put, out.shape[1])


def respond_kernel(place, own, other, spec, inverse, coef, out):
    hist, width = own.shape
    half = hist // 2
    start = place[1]
    for c in range(0, width, 256):
        total = own[:, c : c + 256] + other[:hist, block(start + c, 256)].astype(F32)
        result = impose(total, spec[:half, c : c + 256], spec[half:, c : c + 256], inverse)
        out[:W, c : c + 256] = result.astype(BF)
    out[W:, :] = jnp.zeros((EXTRA, width), BF)
    out[W : W + 2, :LANES] = coef[...]
    out[W + 2 : W + 4, :LANES] = other[hist : hist + 2, :LANES]


def fold_kernel(place, own, got, coef, other, keep, known, first, second, third):
    z = place[0]
    size = keep.shape[1]
    hist = other.shape[0] - EXTRA
    known[...] = jnp.zeros(known.shape, BF)
    known[0:2, :] = coef[...]
    known[2:4, :] = other[hist : hist + 2, :LANES]
    known[4:8, :] = got[W : W + 4, :LANES]
    for d, out in enumerate((keep, first, second, third)):
        where = block((z ^ d) * size, size)
        total = own[:, where] + got[:W, where].astype(F32)
        out[:W, :] = total.astype(out.dtype)
        if d:
            out[W:, :] = known[...]


def settle_kernel(keep, first, second, third, out):
    total = keep[...]
    for got in (first, second, third):
        total = total + got[:W, :].astype(F32)
    out[...] = total.astype(BF)


def mixers_kernel(place, order, partner, known, first, second, third, after, coef, pick, held):
    me, mask = place[0], place[1]
    modes = order.shape[1]
    held[...] = jnp.zeros(held.shape, F32)
    for z, rows in enumerate((known, first, second, third)):
        top = rows.shape[0] - EXTRA
        for low in range(4):
            where = block((me ^ (4 * z + low)) * LANES, LANES)
            held[0:2, where] = rows[top : top + EXTRA, :].astype(F32)[2 * low : 2 * low + 2]
    mixers(order, partner, mask, held, coef, pick)


def mixers(order, partner, mask, held, coef, pick):
    modes = order.shape[1]
    table = held[...].astype(BF)
    for c in range(0, modes, 256):
        mode = lax.broadcasted_iota(I32, (256, modes), 0) + c
        coef[:, c : c + 256] = dot(table, hot(mode == order[...]), NT)
        mode = lax.broadcasted_iota(I32, (256, modes), 0) + c
        pick[c : c + 256, :] = hot((mode ^ mask) == partner[...])


def plain_mixers_kernel(place, order, partner, every, coef, pick, held):
    held[...] = jnp.zeros(held.shape, F32)
    held[0:2, :] = every[...].astype(F32)
    mixers(order, partner, place[1], held, coef, pick)


def join_kernel(quarter, got, before, out):
    width = quarter.shape[1]
    out[:, :width] = quarter[...]
    out[:, width:] = got[...]


def mate_kernel(resp, pick, out):
    for c in range(0, out.shape[1], 256):
        out[:, c : c + 256] = dot(resp[...], pick[: resp.shape[1], c : c + 256])


def expand_kernel(place, resp, other, mates, coef, pick, shapes, out, paired):
    half = resp.shape[1]
    mask = place[1]
    for c in range(0, 2 * half, 256):
        across = mates[:, c : c + 256] + dot(other[...], pick[half:, c : c + 256])
        for k in (c, c + LANES):
            start = mask ^ k
            mine = resp[:, block(start & (half - 1), LANES)].astype(F32)
            theirs = other[:, block(start & (half - 1), LANES)].astype(F32)
            direct = jnp.where(start < half, mine, theirs)
            mixed = coef[0:1, k : k + LANES] * direct + coef[1:2, k : k + LANES] * across[:, k - c : k - c + LANES]
            paired[:, k : k + LANES] = mixed.astype(BF)
    rows = out.shape[0]
    for r in range(0, rows, 256):
        out[r : r + 256, :] = dot(shapes[r : r + 256, :], paired[...], NT).astype(BF)


def swap(x, devices, bits):
    return lax.ppermute(x, "frdm", [(i, i ^ bits) for i in range(devices)])


def scalars(*values):
    return jnp.stack([jnp.asarray(v, I32) for v in values])


def shards(devices, loads, shapes, mode_order, partner, taps, offsets, coef):
    rows, modes = shapes.shape
    hist, count = loads.shape[1], taps.shape[1]
    half, quarter = modes // 2, modes // 4
    me = lax.axis_index("frdm").astype(I32)
    core = me & 1
    forward = forward_table(hist)
    tap_forward, last = tap_table(hist, count)
    phase = phase_table(hist, hist - W - count + 1)
    inverse = inverse_table(hist, count)
    order, mates, offsets, taps = mode_order[None], partner[None], offsets[None], taps.T

    sent, lft, shapes, stack, tap_forward, last, phase, inverse = call(
        project_kernel, "project",
        [near(hist + EXTRA, half), near(hist, rows), near(rows, modes), near(count - 1 + EXTRA, modes)]
        + [near(*tap_forward.shape), near(*last.shape, dtype=F32), near(*phase.shape), near(*inverse.shape)],
        scalars(core), loads, forward, shapes, taps, tap_forward, last, phase, inverse, offsets, coef,
        far=range(1, 9),
        scratch=[
            pltpu.VMEM(loads.shape, BF), pltpu.VMEM(forward.shape, BF), pltpu.VMEM(taps.shape, F32),
            pltpu.SemaphoreType.DMA((9,)),
        ],
        limit=24,
    )
    got = swap(sent, devices, 1)
    common = (stack, order, tap_forward, last, phase, lft, shapes)

    def quarter_of(index):
        return scalars(core * half + index * quarter, index * quarter)

    def respond(index):
        return call(whole_kernel, "whole", [array(W, quarter, dtype=F32)], quarter_of(index), *common, got, inverse)[0]

    if devices == 16:
        y, z = (me >> 1) & 1, me >> 2
        size = modes // devices
        spec, own = call(
            spectrum_kernel, "spectrum", [near(hist, quarter, dtype=F32)] * 2, quarter_of(1 - y), *common
        )
        away = call(
            respond_kernel, "respond", [array(W + EXTRA, quarter)], quarter_of(1 - y), own, got, spec, inverse, coef
        )[0]
        away = swap(away, devices, 2)
        keep, known, *parts = call(
            fold_kernel, "fold", [array(W, size, dtype=F32), array(EXTRA, LANES)] + [array(W + EXTRA, size)] * 3,
            scalars(z), respond(y), away, coef, got,
        )
        parts = [swap(part, devices, 4 * d) for d, part in zip((1, 2, 3), parts)]
        total = call(settle_kernel, "settle", [array(W, size)], keep, *parts, scalars=0)[0]
        resp = jnp.concatenate([total] + [swap(total, devices, 4 * d) for d in (1, 2, 3)], axis=1)
        place = scalars(me, (core * 8 + y * 4 + z) * size)
        mode_coef, pick = call(
            mixers_kernel, "mixers", [array(8, modes, dtype=F32), near(modes, modes)],
            place, order, mates, known, *parts, resp, scratch=[pltpu.VMEM((8, modes), F32)],
        )
        resp = call(join_kernel, "join", [array(W, half)], resp, swap(resp, devices, 2), mode_coef, scalars=0)[0]
    else:
        place = scalars(me, core * half)
        mode_coef, pick = call(
            plain_mixers_kernel, "mixers", [array(8, modes, dtype=F32), near(modes, modes)],
            place, order, mates, lax.all_gather(coef, "frdm", axis=1, tiled=True), scratch=[pltpu.VMEM((8, modes), F32)],
        )
        resp = jnp.concatenate([respond(q) for q in (0, 1)], axis=1)
        groups = [list(range(c, devices, 2)) for c in range(2)]
        resp = lax.psum(resp, "frdm", axis_index_groups=groups).astype(BF)
    other = swap(resp, devices, 1)
    mine = call(mate_kernel, "mate", [array(W, modes, dtype=F32)], resp, pick, scalars=0)[0]
    return call(
        expand_kernel, "expand", [array(rows, W)], place, resp, other, mine, mode_coef, pick, shapes,
        scratch=[pltpu.VMEM((W, modes), BF)],
    )[0]


def solution(mesh):
    in_specs = (P(("cases", "frdm"), None), P("frdm", None), P(), P(), P(), P(), P(None, "frdm"))
    out_specs = P(("cases", "frdm"), None)
    body = functools.partial(shards, mesh.shape["frdm"])
    return jax.shard_map(body, mesh=mesh, in_specs=in_specs, out_specs=out_specs, check_vma=False)
```

```python
import functools

import jax
import jax.numpy as jnp
import numpy as np
from jax import lax
from jax.experimental import pallas as pl
from jax.experimental.pallas import tpu as pltpu
from jax.sharding import PartitionSpec as P

W = 256
LANES = 128
EXTRA = 16
BF = jnp.bfloat16
F32 = jnp.float32
I32 = jnp.int32
NT = (((1,), (1,)), ((), ()))
NN = (((1,), (0,)), ((), ()))


def dot(a, b, dims=NN):
    return lax.dot_general(a, b, dims, preferred_element_type=F32)


def split(table):
    high = table.astype(BF)
    low = (table - high.astype(np.float64)).astype(BF)
    return high, low


def turns(half, n):
    odd = 2 * np.arange(half)[:, None] + 1
    angle = (odd * n[None, :]) % (4 * half) * (np.pi / (2 * half))
    return np.cos(angle), np.sin(angle)


def forward_table(hist):
    cos, sin = turns(hist // 2, np.arange(hist))
    return np.concatenate(split(np.concatenate([cos, -sin])), axis=1)


def tap_table(hist, taps):
    cos, sin = turns(hist // 2, np.arange(taps))
    table = np.concatenate([cos, -sin])
    last = np.repeat(table[:, -1:], LANES, axis=1).astype(np.float32)
    return np.concatenate(split(table[:, :-1]), axis=1), last


def phase_table(hist, delay):
    cos, sin = turns(hist // 2, np.arange(1, delay + 1))
    return np.concatenate(split(np.concatenate([cos - 1.0, sin])), axis=1)


def inverse_table(hist, taps):
    cos, sin = turns(hist // 2, np.arange(W) + taps - 1)
    return np.concatenate(split(np.concatenate([cos, -sin]).T * (2.0 / hist)), axis=1)


def call(kernel, name, out_shape, *args, scalars=1, far=(), scratch=(), limit=16):
    vmem = pl.BlockSpec(memory_space=pltpu.VMEM)
    smem = pl.BlockSpec(memory_space=pltpu.SMEM)
    hbm = pl.BlockSpec(memory_space=pltpu.HBM)
    places = [smem] * scalars + [vmem] * (len(args) - scalars)
    args = list(args)
    for i in far:
        places[i] = hbm
        args[i] = pltpu.with_memory_space_constraint(jnp.asarray(args[i]), pltpu.HBM)
    return pl.pallas_call(
        kernel,
        in_specs=places,
        out_specs=[vmem] * len(out_shape),
        out_shape=out_shape,
        scratch_shapes=list(scratch),
        compiler_params=pltpu.CompilerParams(vmem_limit_bytes=limit * 1024 * 1024),
        name=name,
    )(*args)


def array(*shape, dtype=BF):
    return jax.ShapeDtypeStruct(shape, dtype)


def near(*shape, dtype=BF):
    return pltpu.VMEM(shape, dtype)


def block(start, size):
    return pl.ds(pl.multiple_of(start, LANES), size)


def hot(mask):
    return mask.astype(F32).astype(BF)


def project_kernel(
    place, loads_far, forward_far, shapes_far, taps_far, table_far, last_far, phase_far, inverse_far, offsets, coef,
    sent, lft, shapes, stack, table, last, phase, inverse, loads, forward, taps, sems,
):
    rows, half = loads.shape[0], sent.shape[1]
    hist = lft.shape[0]
    core = place[0] & 1
    far, own = block((1 - core) * half, half), block(core * half, half)
    pairs = [
        (forward_far, forward),
        (loads_far, loads),
        (shapes_far.at[:, far], shapes.at[:, far]),
        (taps_far, taps),
        (table_far, table),
        (shapes_far.at[:, own], shapes.at[:, own]),
        (last_far, last),
        (phase_far, phase),
        (inverse_far, inverse),
    ]
    copies = [pltpu.make_async_copy(a, b, sems.at[i]) for i, (a, b) in enumerate(pairs)]
    for copy in copies:
        copy.start()
    copies[0].wait()
    copies[1].wait()
    for r in range(0, rows, 256):
        part = loads[r : r + 256, :]
        lft[:, r : r + 256] = dot(forward[...], jnp.concatenate([part, part], axis=1), NT).astype(BF)
    copies[2].wait()
    copies[3].wait()
    count = taps.shape[0] - 1
    for c in range(0, half, 256):
        sent[:hist, c : c + 256] = dot(lft[...], shapes[:, block((1 - core) * half + c, 256)]).astype(BF)
    sent[hist:, :] = jnp.zeros((EXTRA, half), BF)
    per = coef.shape[1]
    sent[hist : hist + 2, :per] = coef[...]
    for r in range(0, count, 64):
        stack[r : r + 64, :] = taps[r : r + 64, :].astype(BF)
    index = lax.broadcasted_iota(I32, (EXTRA, taps.shape[1]), 0)
    end = taps[count : count + 1, :]
    tail = jnp.where(index == 0, end, jnp.where(index == 1, offsets[...].astype(F32), 0.0))
    stack[count:, :] = tail.astype(BF)
    for copy in copies[4:]:
        copy.wait()


def quarter_base(place, which, modes):
    me = place[0]
    index = which - 2 if which > 1 else ((me >> 1) & 1) ^ which
    start = index * (modes // 4)
    return (me & 1) * (modes // 2) + start, start


def spectrum(base, stack, order, table, last, phase, put, width):
    count = stack.shape[0] - EXTRA
    half = table.shape[0] // 2
    delay = phase.shape[1] // 2
    for c in range(0, width, 256):
        mode = lax.broadcasted_iota(I32, (256, stack.shape[1]), 0) + (base + c)
        picked = dot(stack[...], hot(mode == order[...]), NT)
        main = picked[:count].astype(BF)
        tail = picked[count:]
        end, offset = tail[0:1], tail[1:2].astype(I32)
        resp = dot(table[...], jnp.concatenate([main, main], axis=0))
        resp = resp + jnp.tile(last[...], (1, 2)) * end
        which = hot(lax.broadcasted_iota(I32, (delay, 256), 0) + 1 == offset)
        turn = dot(phase[...], jnp.concatenate([which, which], axis=0))
        cos, sin = turn[:half] + 1.0, turn[half:]
        re, im = resp[:half], resp[half:]
        put(c, cos * re - sin * im, sin * re + cos * im)


def spectrum_kernel(place, stack, order, table, last, phase, lft, shapes, spec, own):
    width = spec.shape[1]
    half = spec.shape[0] // 2
    base = quarter_base(place, 1, shapes.shape[1])[0]
    for c in range(0, width, 256):
        own[:, c : c + 256] = dot(lft[...], shapes[:, block(base + c, 256)])

    def put(c, re, im):
        spec[:half, c : c + 256] = re
        spec[half:, c : c + 256] = im

    spectrum(base, stack, order, table, last, phase, put, width)


def impose(total, tre, tim, inverse):
    half = tre.shape[0]
    re, im = total[:half], total[half:]
    product = jnp.concatenate([re * tre - im * tim, re * tim + im * tre], axis=0).astype(BF)
    return dot(inverse[...], jnp.concatenate([product, product], axis=0))


def whole_kernel(which, place, stack, order, table, last, phase, lft, shapes, other, inverse, out):
    hist = lft.shape[0]
    base, start = quarter_base(place, which, shapes.shape[1])

    def put(c, re, im):
        total = dot(lft[...], shapes[:, block(base + c, 256)]) + other[:hist, block(start + c, 256)].astype(F32)
        out[:, c : c + 256] = impose(total, re, im, inverse)

    spectrum(base, stack, order, table, last, phase, put, out.shape[1])


def respond_kernel(place, own, other, spec, inverse, coef, out):
    hist, width = own.shape
    half = hist // 2
    start = quarter_base(place, 1, 4 * width)[1]
    for c in range(0, width, 256):
        total = own[:, c : c + 256] + other[:hist, block(start + c, 256)].astype(F32)
        result = impose(total, spec[:half, c : c + 256], spec[half:, c : c + 256], inverse)
        out[:W, c : c + 256] = result.astype(BF)
    out[W:, :] = jnp.zeros((EXTRA, width), BF)
    out[W : W + 2, :LANES] = coef[...]
    out[W + 2 : W + 4, :LANES] = other[hist : hist + 2, :LANES]


def fold_kernel(place, own, got, coef, other, keep, known, first, second, third):
    z = place[0] >> 2
    size = keep.shape[1]
    hist = other.shape[0] - EXTRA
    known[...] = jnp.zeros(known.shape, BF)
    known[0:2, :] = coef[...]
    known[2:4, :] = other[hist : hist + 2, :LANES]
    known[4:8, :] = got[W : W + 4, :LANES]
    for d, out in enumerate((keep, first, second, third)):
        where = block((z ^ d) * size, size)
        total = own[:, where] + got[:W, where].astype(F32)
        out[:W, :] = total.astype(out.dtype)
        if d:
            out[W:, :] = known[...]


def settle_kernel(keep, first, second, third, out):
    total = keep[...]
    for got in (first, second, third):
        total = total + got[:W, :].astype(F32)
    out[...] = total.astype(BF)


def mask_of(place, devices, modes):
    me = place[0]
    if devices == 16:
        return ((me & 1) * 8 + (me & 2) * 2 + (me >> 2)) * (modes // 16)
    return (me & 1) * (modes // 2)


def mixers_kernel(place, order, partner, known, first, second, third, after, coef, pick, held):
    me, mask = place[0], mask_of(place, 16, order.shape[1])
    held[...] = jnp.zeros(held.shape, F32)
    for z, rows in enumerate((known, first, second, third)):
        top = rows.shape[0] - EXTRA
        for low in range(4):
            where = block((me ^ (4 * z + low)) * LANES, LANES)
            held[0:2, where] = rows[top : top + EXTRA, :].astype(F32)[2 * low : 2 * low + 2]
    mixers(order, partner, mask, held, coef, pick)


def mixers(order, partner, mask, held, coef, pick):
    modes = order.shape[1]
    table = held[...].astype(BF)
    for c in range(0, modes, 256):
        mode = lax.broadcasted_iota(I32, (256, modes), 0) + c
        coef[:, c : c + 256] = dot(table, hot(mode == order[...]), NT)
        mode = lax.broadcasted_iota(I32, (256, modes), 0) + c
        pick[c : c + 256, :] = hot((mode ^ mask) == partner[...])


def plain_mixers_kernel(devices, place, order, partner, every, coef, pick, held):
    held[...] = jnp.zeros(held.shape, F32)
    held[0:2, :] = every[...].astype(F32)
    mixers(order, partner, mask_of(place, devices, order.shape[1]), held, coef, pick)


def join_kernel(quarter, got, before, out):
    width = quarter.shape[1]
    out[:, :width] = quarter[...]
    out[:, width:] = got[...]


def mate_kernel(resp, pick, out):
    for c in range(0, out.shape[1], 256):
        out[:, c : c + 256] = dot(resp[...], pick[: resp.shape[1], c : c + 256])


def expand_kernel(devices, place, resp, other, mates, coef, pick, shapes, out, paired):
    half = resp.shape[1]
    mask = mask_of(place, devices, shapes.shape[1])
    for c in range(0, 2 * half, 256):
        across = mates[:, c : c + 256] + dot(other[...], pick[half:, c : c + 256])
        for k in (c, c + LANES):
            start = mask ^ k
            mine = resp[:, block(start & (half - 1), LANES)].astype(F32)
            theirs = other[:, block(start & (half - 1), LANES)].astype(F32)
            direct = jnp.where(start < half, mine, theirs)
            mixed = coef[0:1, k : k + LANES] * direct + coef[1:2, k : k + LANES] * across[:, k - c : k - c + LANES]
            paired[:, k : k + LANES] = mixed.astype(BF)
    rows = out.shape[0]
    for r in range(0, rows, 256):
        out[r : r + 256, :] = dot(shapes[r : r + 256, :], paired[...], NT).astype(BF)


def swap(x, devices, bits):
    return lax.ppermute(x, "frdm", [(i, i ^ bits) for i in range(devices)])


def shards(devices, loads, shapes, mode_order, partner, taps, offsets, coef):
    rows, modes = shapes.shape
    hist, count = loads.shape[1], taps.shape[1]
    half, quarter = modes // 2, modes // 4
    place = lax.axis_index("frdm").astype(I32).reshape(1)
    forward = forward_table(hist)
    tap_forward, last = tap_table(hist, count)
    phase = phase_table(hist, hist - W - count + 1)
    inverse = inverse_table(hist, count)
    order, mates, offsets, taps = mode_order[None], partner[None], offsets[None], taps.T

    sent, lft, shapes, stack, tap_forward, last, phase, inverse = call(
        project_kernel, "project",
        [near(hist + EXTRA, half), near(hist, rows), near(rows, modes), near(count - 1 + EXTRA, modes)]
        + [near(*tap_forward.shape), near(*last.shape, dtype=F32), near(*phase.shape), near(*inverse.shape)],
        place, loads, forward, shapes, taps, tap_forward, last, phase, inverse, offsets, coef,
        far=range(1, 9),
        scratch=[
            pltpu.VMEM(loads.shape, BF), pltpu.VMEM(forward.shape, BF), pltpu.VMEM(taps.shape, F32),
            pltpu.SemaphoreType.DMA((9,)),
        ],
        limit=24,
    )
    got = swap(sent, devices, 1)
    common = (stack, order, tap_forward, last, phase, lft, shapes)

    def respond(which):
        kernel = functools.partial(whole_kernel, which)
        return call(kernel, "whole", [array(W, quarter, dtype=F32)], place, *common, got, inverse)[0]

    if devices == 16:
        size = modes // devices
        spec, own = call(
            spectrum_kernel, "spectrum", [near(hist, quarter, dtype=F32)] * 2, place, *common
        )
        away = call(
            respond_kernel, "respond", [array(W + EXTRA, quarter)], place, own, got, spec, inverse, coef
        )[0]
        away = swap(away, devices, 2)
        keep, known, *parts = call(
            fold_kernel, "fold", [array(W, size, dtype=F32), array(EXTRA, LANES)] + [array(W + EXTRA, size)] * 3,
            place, respond(0), away, coef, got,
        )
        parts = [swap(part, devices, 4 * d) for d, part in zip((1, 2, 3), parts)]
        total = call(settle_kernel, "settle", [array(W, size)], keep, *parts, scalars=0)[0]
        resp = jnp.concatenate([total] + [swap(total, devices, 4 * d) for d in (1, 2, 3)], axis=1)
        mode_coef, pick = call(
            mixers_kernel, "mixers", [array(8, modes, dtype=F32), near(modes, modes)],
            place, order, mates, known, *parts, resp, scratch=[pltpu.VMEM((8, modes), F32)],
        )
        resp = call(join_kernel, "join", [array(W, half)], resp, swap(resp, devices, 2), mode_coef, scalars=0)[0]
    else:
        mode_coef, pick = call(
            functools.partial(plain_mixers_kernel, devices), "mixers", [array(8, modes, dtype=F32), near(modes, modes)],
            place, order, mates, lax.all_gather(coef, "frdm", axis=1, tiled=True), scratch=[pltpu.VMEM((8, modes), F32)],
        )
        resp = jnp.concatenate([respond(q) for q in (2, 3)], axis=1)
        groups = [list(range(c, devices, 2)) for c in range(2)]
        resp = lax.psum(resp, "frdm", axis_index_groups=groups).astype(BF)
    other = swap(resp, devices, 1)
    mine = call(mate_kernel, "mate", [array(W, modes, dtype=F32)], resp, pick, scalars=0)[0]
    return call(
        functools.partial(expand_kernel, devices), "expand", [array(rows, W)], place, resp, other, mine, mode_coef, pick, shapes,
        scratch=[pltpu.VMEM((W, modes), BF)],
    )[0]


def solution(mesh):
    in_specs = (P(("cases", "frdm"), None), P("frdm", None), P(), P(), P(), P(), P(None, "frdm"))
    out_specs = P(("cases", "frdm"), None)
    body = functools.partial(shards, mesh.shape["frdm"])
    return jax.shard_map(body, mesh=mesh, in_specs=in_specs, out_specs=out_specs, check_vma=False)
```

```python
import functools

import jax
import jax.numpy as jnp
import numpy as np
from jax import lax
from jax.experimental import pallas as pl
from jax.experimental.pallas import tpu as pltpu
from jax.sharding import PartitionSpec as P

W = 256
LANES = 128
EXTRA = 16
BF = jnp.bfloat16
F32 = jnp.float32
I32 = jnp.int32
NT = (((1,), (1,)), ((), ()))
NN = (((1,), (0,)), ((), ()))


def dot(a, b, dims=NN):
    return lax.dot_general(a, b, dims, preferred_element_type=F32)


def split(table):
    high = table.astype(BF)
    low = (table - high.astype(np.float64)).astype(BF)
    return high, low


def turns(half, n):
    odd = 2 * np.arange(half)[:, None] + 1
    angle = (odd * n[None, :]) % (4 * half) * (np.pi / (2 * half))
    return np.cos(angle), np.sin(angle)


def forward_table(hist):
    cos, sin = turns(hist // 2, np.arange(hist))
    return np.concatenate([cos, -sin]).astype(BF)


def tap_table(hist, taps):
    cos, sin = turns(hist // 2, np.arange(taps))
    table = np.concatenate([cos, -sin])
    last = np.repeat(table[:, -1:], LANES, axis=1).astype(np.float32)
    return np.concatenate(split(table[:, :-1]), axis=1), last


def phase_table(hist, delay):
    cos, sin = turns(hist // 2, np.arange(1, delay + 1))
    return np.concatenate(split(np.concatenate([cos - 1.0, sin])), axis=1)


def inverse_table(hist, taps):
    cos, sin = turns(hist // 2, np.arange(W) + taps - 1)
    high, low = split(np.concatenate([cos, -sin]).T * (2.0 / hist))
    return np.concatenate([high, high, low], axis=1)


def call(kernel, name, out_shape, *args, scalars=1, far=(), scratch=(), limit=16):
    vmem = pl.BlockSpec(memory_space=pltpu.VMEM)
    smem = pl.BlockSpec(memory_space=pltpu.SMEM)
    hbm = pl.BlockSpec(memory_space=pltpu.HBM)
    places = [smem] * scalars + [vmem] * (len(args) - scalars)
    args = list(args)
    for i in far:
        places[i] = hbm
        args[i] = pltpu.with_memory_space_constraint(jnp.asarray(args[i]), pltpu.HBM)
    return pl.pallas_call(
        kernel,
        in_specs=places,
        out_specs=[vmem] * len(out_shape),
        out_shape=out_shape,
        scratch_shapes=list(scratch),
        compiler_params=pltpu.CompilerParams(vmem_limit_bytes=limit * 1024 * 1024),
        name=name,
    )(*args)


def array(*shape, dtype=BF):
    return jax.ShapeDtypeStruct(shape, dtype)


def near(*shape, dtype=BF):
    return pltpu.VMEM(shape, dtype)


def block(start, size):
    return pl.ds(pl.multiple_of(start, LANES), size)


def hot(mask):
    return mask.astype(F32).astype(BF)


def project_kernel(
    place, loads_far, forward_far, shapes_far, taps_far, table_far, last_far, phase_far, inverse_far, offsets_far, coef_far,
    sent, lft, shapes, stack, table, last, phase, inverse, coef, loads, forward, taps, offsets, sems,
):
    rows, half = loads.shape[0], sent.shape[1]
    hist = lft.shape[0]
    core = place[0] & 1
    far, own = block((1 - core) * half, half), block(core * half, half)
    step = 256
    chunks = [pl.ds(r, step) for r in range(0, rows, step)]
    pairs = [(forward_far, forward)] + [(loads_far.at[r, :], loads.at[r, :]) for r in chunks]
    first = len(pairs)
    pairs += [
        (coef_far, coef),
        (offsets_far, offsets),
        (shapes_far.at[:, far], shapes.at[:, far]),
        (taps_far, taps),
        (table_far, table),
        (shapes_far.at[:, own], shapes.at[:, own]),
        (last_far, last),
        (phase_far, phase),
        (inverse_far, inverse),
    ]
    copies = [pltpu.make_async_copy(a, b, sems.at[i]) for i, (a, b) in enumerate(pairs)]
    for copy in copies[:first]:
        copy.start()
    copies[0].wait()
    copies[1].wait()
    for copy in copies[first:]:
        copy.start()
    for i, r in enumerate(chunks):
        if i:
            copies[1 + i].wait()
        lft[:, i * step : (i + 1) * step] = dot(forward[...], loads[r, :], NT).astype(BF)
    for copy in copies[first : first + 4]:
        copy.wait()
    count = taps.shape[0] - 1
    for c in range(0, half, 256):
        sent[:hist, c : c + 256] = dot(lft[...], shapes[:, block((1 - core) * half + c, 256)]).astype(BF)
    sent[hist:, :] = jnp.zeros((EXTRA, half), BF)
    per = coef.shape[1]
    sent[hist : hist + 2, :per] = coef[...]
    for r in range(0, count, 64):
        stack[r : r + 64, :] = taps[r : r + 64, :].astype(BF)
    index = lax.broadcasted_iota(I32, (EXTRA, taps.shape[1]), 0)
    end = taps[count : count + 1, :]
    tail = jnp.where(index == 0, end, jnp.where(index == 1, offsets[...].astype(F32), 0.0))
    stack[count:, :] = tail.astype(BF)
    for copy in copies[first + 4 :]:
        copy.wait()


def quarter_base(place, which, modes):
    me = place[0]
    index = which - 2 if which > 1 else ((me >> 1) & 1) ^ which
    start = index * (modes // 4)
    return (me & 1) * (modes // 2) + start, start


def spectrum(base, stack, order, table, last, phase, put, width):
    count = stack.shape[0] - EXTRA
    half = table.shape[0] // 2
    delay = phase.shape[1] // 2
    for c in range(0, width, 256):
        mode = lax.broadcasted_iota(I32, (256, stack.shape[1]), 0) + (base + c)
        picked = dot(stack[...], hot(mode == order[...]), NT)
        main = picked[:count].astype(BF)
        tail = picked[count:]
        end, offset = tail[0:1], tail[1:2].astype(I32)
        resp = dot(table[...], jnp.concatenate([main, main], axis=0))
        resp = resp + jnp.tile(last[...], (1, 2)) * end
        which = hot(lax.broadcasted_iota(I32, (delay, 256), 0) + 1 == offset)
        turn = dot(phase[...], jnp.concatenate([which, which], axis=0))
        cos, sin = turn[:half] + 1.0, turn[half:]
        re, im = resp[:half], resp[half:]
        put(c, cos * re - sin * im, sin * re + cos * im)


def spectrum_kernel(place, stack, order, table, last, phase, lft, shapes, spec, own):
    width = spec.shape[1]
    half = spec.shape[0] // 2
    base = quarter_base(place, 1, shapes.shape[1])[0]
    for c in range(0, width, 256):
        own[:, c : c + 256] = dot(lft[...], shapes[:, block(base + c, 256)])

    def put(c, re, im):
        spec[:half, c : c + 256] = re
        spec[half:, c : c + 256] = im

    spectrum(base, stack, order, table, last, phase, put, width)


def impose(total, tre, tim, inverse):
    half = tre.shape[0]
    re, im = total[:half], total[half:]
    product = jnp.concatenate([re * tre - im * tim, re * tim + im * tre], axis=0)
    high = product.astype(BF)
    low = (product - high.astype(F32)).astype(BF)
    return dot(inverse[...], jnp.concatenate([high, low, high], axis=0))


def whole_kernel(which, place, stack, order, table, last, phase, lft, shapes, other, inverse, out):
    hist = lft.shape[0]
    base, start = quarter_base(place, which, shapes.shape[1])

    def put(c, re, im):
        total = dot(lft[...], shapes[:, block(base + c, 256)]) + other[:hist, block(start + c, 256)].astype(F32)
        out[:, c : c + 256] = impose(total, re, im, inverse)

    spectrum(base, stack, order, table, last, phase, put, out.shape[1])


def respond_kernel(place, own, other, spec, inverse, coef, out):
    hist, width = own.shape
    half = hist // 2
    start = quarter_base(place, 1, 4 * width)[1]
    for c in range(0, width, 256):
        total = own[:, c : c + 256] + other[:hist, block(start + c, 256)].astype(F32)
        result = impose(total, spec[:half, c : c + 256], spec[half:, c : c + 256], inverse)
        out[:W, c : c + 256] = result.astype(BF)
    out[W:, :] = jnp.zeros((EXTRA, width), BF)
    out[W : W + 2, :LANES] = coef[...]
    out[W + 2 : W + 4, :LANES] = other[hist : hist + 2, :LANES]


def fold_kernel(place, own, got, coef, other, keep, known, first, second, third):
    z = place[0] >> 2
    size = keep.shape[1]
    hist = other.shape[0] - EXTRA
    known[...] = jnp.zeros(known.shape, BF)
    known[0:2, :] = coef[...]
    known[2:4, :] = other[hist : hist + 2, :LANES]
    known[4:8, :] = got[W : W + 4, :LANES]
    for d, out in enumerate((keep, first, second, third)):
        where = block((z ^ d) * size, size)
        total = own[:, where] + got[:W, where].astype(F32)
        out[:W, :] = total.astype(out.dtype)
        if d:
            out[W:, :] = known[...]


def settle_kernel(after, keep, first, second, third, out):
    total = keep[...]
    for got in (first, second, third):
        total = total + got[:W, :].astype(F32)
    out[...] = total.astype(BF)


def mask_of(place, devices, modes):
    me = place[0]
    if devices == 16:
        return ((me & 1) * 8 + (me & 2) * 2 + (me >> 2)) * (modes // 16)
    return (me & 1) * (modes // 2)


def pick_kernel(devices, place, partner, after, pick):
    modes = partner.shape[1]
    mask = mask_of(place, devices, modes)
    for c in range(0, modes, 256):
        mode = lax.broadcasted_iota(I32, (256, modes), 0) + c
        pick[c : c + 256, :] = hot((mode ^ mask) == partner[...])


def mixers_kernel(place, order, known, third, second, first, after, coef, held):
    me = place[0]
    held[...] = jnp.zeros(held.shape, F32)
    for z, rows in enumerate((known, first, second, third)):
        top = rows.shape[0] - EXTRA
        for low in range(4):
            where = block((me ^ (4 * z + low)) * LANES, LANES)
            held[0:2, where] = rows[top : top + EXTRA, :].astype(F32)[2 * low : 2 * low + 2]
    mixers(order, held, coef)


def mixers(order, held, coef):
    modes = order.shape[1]
    table = held[...].astype(BF)
    for c in range(0, modes, 256):
        mode = lax.broadcasted_iota(I32, (256, modes), 0) + c
        coef[:, c : c + 256] = dot(table, hot(mode == order[...]), NT)


def plain_mixers_kernel(order, every, coef, held):
    held[...] = jnp.zeros(held.shape, F32)
    held[0:2, :] = every[...].astype(F32)
    mixers(order, held, coef)


def join_kernel(*refs):
    *parts, out = refs
    start = 0
    for part in parts:
        out[:, start : start + part.shape[1]] = part[...]
        start += part.shape[1]


def join(*parts, after=None):
    width = sum(part.shape[1] for part in parts)
    kernel = join_kernel if after is None else lambda _, *refs: join_kernel(*refs)
    first = () if after is None else (after,)
    return call(kernel, "join", [array(parts[0].shape[0], width)], *first, *parts, scalars=0)[0]


def mate_kernel(resp, pick, out):
    for c in range(0, out.shape[1], 256):
        out[:, c : c + 256] = dot(resp[...], pick[: resp.shape[1], c : c + 256])


def expand_kernel(devices, place, resp, other, mates, coef, pick, shapes, out, paired):
    half = resp.shape[1]
    mask = mask_of(place, devices, shapes.shape[1])
    for c in range(0, 2 * half, 256):
        across = mates[:, c : c + 256] + dot(other[...], pick[half:, c : c + 256])
        for k in (c, c + LANES):
            start = mask ^ k
            mine = resp[:, block(start & (half - 1), LANES)].astype(F32)
            theirs = other[:, block(start & (half - 1), LANES)].astype(F32)
            direct = jnp.where(start < half, mine, theirs)
            mixed = coef[0:1, k : k + LANES] * direct + coef[1:2, k : k + LANES] * across[:, k - c : k - c + LANES]
            paired[:, k : k + LANES] = mixed.astype(BF)
    rows = out.shape[0]
    for r in range(0, rows, 256):
        out[r : r + 256, :] = dot(shapes[r : r + 256, :], paired[...], NT).astype(BF)


def swap(x, devices, bits):
    return lax.ppermute(x, "frdm", [(i, i ^ bits) for i in range(devices)])


def shards(devices, loads, shapes, mode_order, partner, taps, offsets, coef):
    rows, modes = shapes.shape
    hist, count = loads.shape[1], taps.shape[1]
    half, quarter = modes // 2, modes // 4
    place = lax.axis_index("frdm").astype(I32).reshape(1)
    forward = forward_table(hist)
    tap_forward, last = tap_table(hist, count)
    phase = phase_table(hist, hist - W - count + 1)
    inverse = inverse_table(hist, count)
    order, mates, offsets, taps = mode_order[None], partner[None], offsets[None], taps.T

    sent, lft, shapes, stack, tap_forward, last, phase, inverse, coef_near = call(
        project_kernel, "project",
        [near(hist + EXTRA, half), near(hist, rows), near(rows, modes), near(count - 1 + EXTRA, modes)]
        + [near(*tap_forward.shape), near(*last.shape, dtype=F32), near(*phase.shape), near(*inverse.shape), near(*coef.shape)],
        place, loads, forward, shapes, taps, tap_forward, last, phase, inverse, offsets, coef,
        far=range(1, 11),
        scratch=[
            pltpu.VMEM(loads.shape, BF), pltpu.VMEM(forward.shape, BF), pltpu.VMEM(taps.shape, F32),
            pltpu.VMEM(offsets.shape, I32), pltpu.SemaphoreType.DMA((10 + rows // 256,)),
        ],
        limit=24,
    )
    got = swap(sent, devices, 1)
    common = (stack, order, tap_forward, last, phase, lft, shapes)

    def respond(which):
        kernel = functools.partial(whole_kernel, which)
        return call(kernel, "whole", [array(W, quarter, dtype=F32)], place, *common, got, inverse)[0]

    if devices == 16:
        size = modes // devices
        spec, own = call(
            spectrum_kernel, "spectrum", [near(hist, quarter, dtype=F32)] * 2, place, *common
        )
        away = call(
            respond_kernel, "respond", [array(W + EXTRA, quarter)], place, own, got, spec, inverse, coef_near
        )[0]
        away = swap(away, devices, 2)
        keep, known, *parts = call(
            fold_kernel, "fold", [array(W, size, dtype=F32), array(EXTRA, LANES)] + [array(W + EXTRA, size)] * 3,
            place, respond(0), away, coef_near, got,
        )
        parts = [swap(part, devices, 4 * d) for d, part in reversed(list(zip((1, 2, 3), parts)))]
        pick = call(functools.partial(pick_kernel, devices), "pick", [near(modes, modes)], place, mates, keep)[0]
        total = call(settle_kernel, "settle", [array(W, size)], pick, keep, *parts, scalars=0)[0]
        spread = [swap(total, devices, 4 * d) for d in (1, 2, 3)]
        ends = join(total, spread[0])
        mode_coef = call(
            mixers_kernel, "mixers", [array(8, modes, dtype=F32)],
            place, order, known, *parts, ends, scratch=[pltpu.VMEM((8, modes), F32)],
        )[0]
        halves = [swap(ends, devices, 2), join(*spread[1:], after=mode_coef)]
        halves = [ends, halves[1], halves[0], swap(halves[1], devices, 2)]
        resp = join(*halves)
    else:
        pick = call(functools.partial(pick_kernel, devices), "pick", [near(modes, modes)], place, mates, mates)[0]
        mode_coef = call(
            plain_mixers_kernel, "mixers", [array(8, modes, dtype=F32)],
            order, lax.all_gather(coef, "frdm", axis=1, tiled=True), scalars=0, scratch=[pltpu.VMEM((8, modes), F32)],
        )[0]
        resp = jnp.concatenate([respond(q) for q in (2, 3)], axis=1)
        groups = [list(range(c, devices, 2)) for c in range(2)]
        resp = lax.psum(resp, "frdm", axis_index_groups=groups).astype(BF)
    other = swap(resp, devices, 1)
    mine = call(mate_kernel, "mate", [array(W, modes, dtype=F32)], resp, pick, scalars=0)[0]
    return call(
        functools.partial(expand_kernel, devices), "expand", [array(rows, W)], place, resp, other, mine, mode_coef, pick, shapes,
        scratch=[pltpu.VMEM((W, modes), BF)],
    )[0]


def solution(mesh):
    in_specs = (P(("cases", "frdm"), None), P("frdm", None), P(), P(), P(), P(), P(None, "frdm"))
    out_specs = P(("cases", "frdm"), None)
    body = functools.partial(shards, mesh.shape["frdm"])
    return jax.shard_map(body, mesh=mesh, in_specs=in_specs, out_specs=out_specs, check_vma=False)
```

```python
import functools

import jax
import jax.numpy as jnp
import numpy as np
from jax import lax
from jax.experimental import pallas as pl
from jax.experimental.pallas import tpu as pltpu
from jax.sharding import PartitionSpec as P

W = 256
LANES = 128
EXTRA = 16
BF = jnp.bfloat16
F32 = jnp.float32
I32 = jnp.int32
NT = (((1,), (1,)), ((), ()))
NN = (((1,), (0,)), ((), ()))


def dot(a, b, dims=NN):
    return lax.dot_general(a, b, dims, preferred_element_type=F32)


def split(table):
    high = table.astype(BF)
    low = (table - high.astype(np.float64)).astype(BF)
    return high, low


def turns(half, n):
    odd = 2 * np.arange(half)[:, None] + 1
    angle = (odd * n[None, :]) % (4 * half) * (np.pi / (2 * half))
    return np.cos(angle), np.sin(angle)


def forward_table(hist):
    cos, sin = turns(hist // 2, np.arange(hist))
    return np.concatenate([cos, -sin]).astype(BF)


def tap_table(hist, taps):
    cos, sin = turns(hist // 2, np.arange(taps))
    table = np.concatenate([cos, -sin])
    last = np.repeat(table[:, -1:], LANES, axis=1).astype(BF)
    return np.concatenate(split(table[:, :-1]), axis=1), last


def phase_table(hist, delay):
    cos, sin = turns(hist // 2, np.arange(1, delay + 1))
    return np.concatenate(split(np.concatenate([cos - 1.0, sin])), axis=1)


def inverse_table(hist, taps):
    cos, sin = turns(hist // 2, np.arange(W) + taps - 1)
    return np.concatenate(split(np.concatenate([cos, -sin]).T * (2.0 / hist)), axis=1)


def call(kernel, name, out_shape, *args, scalars=1, far=(), scratch=(), limit=16):
    vmem = pl.BlockSpec(memory_space=pltpu.VMEM)
    smem = pl.BlockSpec(memory_space=pltpu.SMEM)
    hbm = pl.BlockSpec(memory_space=pltpu.HBM)
    places = [smem] * scalars + [vmem] * (len(args) - scalars)
    args = list(args)
    for i in far:
        places[i] = hbm
        args[i] = pltpu.with_memory_space_constraint(jnp.asarray(args[i]), pltpu.HBM)
    return pl.pallas_call(
        kernel,
        in_specs=places,
        out_specs=[vmem] * len(out_shape),
        out_shape=out_shape,
        scratch_shapes=list(scratch),
        compiler_params=pltpu.CompilerParams(vmem_limit_bytes=limit * 1024 * 1024),
        name=name,
    )(*args)


def array(*shape, dtype=BF):
    return jax.ShapeDtypeStruct(shape, dtype)


def near(*shape, dtype=BF):
    return pltpu.VMEM(shape, dtype)


def block(start, size):
    return pl.ds(pl.multiple_of(start, LANES), size)


def hot(mask):
    return mask.astype(F32).astype(BF)


def fetch(pairs, sems):
    return [pltpu.make_async_copy(a, b, sems.at[i]) for i, (a, b) in enumerate(pairs)]


def project_kernel(
    place, loads_far, forward_far, shapes_far, taps_far, offsets_far, coef_far,
    sent, lft, shapes, stack, coef, loads, forward, taps, offsets, sems,
):
    rows, half = loads.shape[0], sent.shape[1]
    hist = lft.shape[0]
    start = (1 - (place[0] & 1)) * half
    step = 256
    chunks = [pl.ds(r, step) for r in range(0, rows, step)]
    pairs = [(forward_far, forward)] + [(loads_far.at[r, :], loads.at[r, :]) for r in chunks]
    first = len(pairs)
    pairs += [
        (coef_far, coef),
        (offsets_far, offsets),
        (shapes_far.at[:, block(start, half)], shapes),
        (taps_far, taps),
    ]
    copies = fetch(pairs, sems)
    for copy in copies:
        copy.start()
    copies[0].wait()
    for i, r in enumerate(chunks):
        copies[1 + i].wait()
        lft[:, i * step : (i + 1) * step] = dot(forward[...], loads[r, :], NT).astype(BF)
    for copy in copies[first : first + 3]:
        copy.wait()
    count = taps.shape[0] - 1
    for c in range(0, half, step):
        sent[:hist, c : c + step] = dot(lft[...], shapes[:, c : c + step]).astype(BF)
    sent[hist:, :] = jnp.zeros((EXTRA, half), BF)
    sent[hist : hist + 2, : coef.shape[1]] = coef[...]
    copies[first + 3].wait()
    for r in range(0, count, 64):
        stack[r : r + 64, :] = taps[r : r + 64, :].astype(BF)
    index = lax.broadcasted_iota(I32, (EXTRA, taps.shape[1]), 0)
    end = taps[count : count + 1, :]
    tail = jnp.where(index == 0, end, jnp.where(index == 1, offsets[...].astype(F32), 0.0))
    stack[count:, :] = tail.astype(BF)


def quarter_start(place, which, modes):
    return (((place[0] >> 1) & 1) ^ which) * (modes // 4)


def gather_taps(base, stack, order):
    count = stack.shape[0] - EXTRA
    mode = lax.broadcasted_iota(I32, (256, stack.shape[1]), 0) + base
    picked = dot(stack[...], hot(mode == order[...]), NT)
    tail = picked[count:]
    return picked[:count].astype(BF), tail[0:1], tail[1:2].astype(I32)


def spectrum_of(main, end, offset, table, last, phase):
    half = table.shape[0] // 2
    delay = phase.shape[1] // 2
    resp = dot(table[...], jnp.concatenate([main, main], axis=0))
    resp = resp + jnp.tile(last[...].astype(F32), (1, 2)) * end
    which = hot(lax.broadcasted_iota(I32, (delay, 256), 0) + 1 == offset)
    turn = dot(phase[...], jnp.concatenate([which, which], axis=0))
    cos, sin = turn[:half] + 1.0, turn[half:]
    re, im = resp[:half], resp[half:]
    return cos * re - sin * im, sin * re + cos * im


def spectrum_kernel(
    place, stack, order, lft, shapes_far, table_far, last_far, phase_far, inverse_far,
    spec, own, shapes, table, last, phase, inverse, sems,
):
    width = spec.shape[1]
    half = spec.shape[0] // 2
    modes = shapes_far.shape[1]
    core = place[0] & 1
    start, later = quarter_start(place, 1, modes), quarter_start(place, 0, modes)
    near = core * 2 * width
    copies = fetch(
        [
            (shapes_far.at[:, block(near + start, width)], shapes.at[:, block(start, width)]),
            (table_far, table),
            (last_far, last),
            (phase_far, phase),
            (inverse_far, inverse),
            (shapes_far.at[:, block(near + later, width)], shapes.at[:, block(later, width)]),
        ],
        sems,
    )
    for copy in copies:
        copy.start()
    tiles = range(0, width, 256)
    picked = [gather_taps(near + start + c, stack, order) for c in tiles]
    copies[0].wait()
    for c in tiles:
        own[:, c : c + 256] = dot(lft[...], shapes[:, block(start + c, 256)])
    for copy in copies[1:4]:
        copy.wait()
    for c, parts in zip(tiles, picked):
        spec[:half, c : c + 256], spec[half:, c : c + 256] = spectrum_of(*parts, table, last, phase)
    for copy in copies[4:]:
        copy.wait()


def impose(total, tre, tim, inverse):
    half = tre.shape[0]
    re, im = total[:half], total[half:]
    product = jnp.concatenate([re * tre - im * tim, re * tim + im * tre], axis=0)
    high = product.astype(BF)
    low = (product - high.astype(F32)).astype(BF)
    both = dot(inverse[...], jnp.concatenate([high, high], axis=0))
    return both + dot(inverse[:, : 2 * half], low)


def whole_kernel(place, stack, order, lft, other, shapes, table, last, phase, inverse, out):
    hist, modes = lft.shape[0], order.shape[1]
    start = quarter_start(place, 0, modes)
    near = (place[0] & 1) * (modes // 2) + start
    for c in range(0, out.shape[1], 256):
        spec = spectrum_of(*gather_taps(near + c, stack, order), table, last, phase)
        here = block(start + c, 256)
        total = dot(lft[...], shapes[:, here]) + other[:hist, here].astype(F32)
        out[:, c : c + 256] = impose(total, *spec, inverse)


def respond_kernel(place, own, other, spec, inverse, coef, out):
    hist, width = own.shape
    half = hist // 2
    start = quarter_start(place, 1, 4 * width)
    for c in range(0, width, 256):
        total = own[:, c : c + 256] + other[:hist, block(start + c, 256)].astype(F32)
        result = impose(total, spec[:half, c : c + 256], spec[half:, c : c + 256], inverse)
        out[:W, c : c + 256] = result.astype(BF)
    out[W:, :] = jnp.zeros((EXTRA, width), BF)
    out[W : W + 2, : coef.shape[1]] = coef[...]
    out[W + 2 : W + 4, :LANES] = other[hist : hist + 2, :LANES]


def fold_kernel(place, own, got, coef, other, keep, known, first, second, third):
    z = place[0] >> 2
    size = keep.shape[1]
    hist = other.shape[0] - EXTRA
    known[...] = jnp.zeros(known.shape, BF)
    known[0:2, :] = coef[...]
    known[2:4, :] = other[hist : hist + 2, :LANES]
    known[4:8, :] = got[W : W + 4, :LANES]
    for d, out in enumerate((keep, first, second, third)):
        where = block((z ^ d) * size, size)
        total = own[:, where] + got[:W, where].astype(F32)
        out[:W, :] = total.astype(out.dtype)
        if d:
            out[W:, :] = known[...]


def settle_kernel(after, keep, first, second, third, out):
    total = keep[...]
    for got in (first, second, third):
        total = total + got[:W, :].astype(F32)
    out[...] = total.astype(BF)


def mask_of(place, devices, modes):
    me = place[0]
    if devices == 16:
        return ((me & 1) * 8 + (me & 2) * 2 + (me >> 2)) * (modes // 16)
    return (me & 1) * (modes // 2)


def pick_kernel(devices, place, partner, after, pick):
    modes = partner.shape[1]
    mask = mask_of(place, devices, modes)
    mates = [partner[:, block(c ^ mask, LANES)] ^ mask for c in range(0, modes, LANES)]
    mates = jnp.concatenate(mates, axis=1)
    for c in range(0, modes, 256):
        pick[c : c + 256, :] = hot(lax.broadcasted_iota(I32, (256, modes), 0) + c == mates)


def mixers_kernel(place, order, known, third, second, first, after, coef, held):
    me = place[0]
    held[...] = jnp.zeros(held.shape, F32)
    for z, rows in enumerate((known, first, second, third)):
        top = rows.shape[0] - EXTRA
        for low in range(4):
            where = block((me ^ (4 * z + low)) * LANES, LANES)
            held[0:2, where] = rows[top : top + EXTRA, :].astype(F32)[2 * low : 2 * low + 2]
    mixers(order, mask_of(place, 16, order.shape[1]), held, coef)


def mixers(order, mask, held, coef):
    modes = order.shape[1]
    table = held[...].astype(BF)
    slots = order[...] ^ mask
    for c in range(0, modes, 256):
        coef[:, c : c + 256] = dot(table, hot(lax.broadcasted_iota(I32, (256, modes), 0) + c == slots), NT)


def plain_mixers_kernel(devices, place, order, every, coef, held):
    held[...] = jnp.zeros(held.shape, F32)
    held[0:2, :] = every[...].astype(F32)
    mixers(order, mask_of(place, devices, order.shape[1]), held, coef)


def join_kernel(*refs):
    *parts, out = refs
    start = 0
    for part in parts:
        out[:, start : start + part.shape[1]] = part[...]
        start += part.shape[1]


def join(*parts, after=None):
    width = sum(part.shape[1] for part in parts)
    kernel = join_kernel if after is None else lambda _, *refs: join_kernel(*refs)
    first = () if after is None else (after,)
    return call(kernel, "join", [array(parts[0].shape[0], width)], *first, *parts, scalars=0)[0]


def mate_kernel(mine, theirs, pick, out):
    width = mine.shape[1]
    resp = jnp.concatenate([mine[...], theirs[...]], axis=1)
    for c in range(0, out.shape[1], 256):
        here = slice(c, c + 256)
        out[:, here] = dot(resp, jnp.concatenate([pick[:width, here], pick[2 * width : 3 * width, here]], axis=0))


def more_kernel(mates, got, pick, out):
    width = got.shape[1]
    for c in range(0, out.shape[1], 256):
        out[:, c : c + 256] = mates[:, c : c + 256] + dot(got[...], pick[width : 2 * width, c : c + 256])


def expand_kernel(devices, place, mine, got, theirs, other, mates, pick, coef, near, far, out, near_pair, far_pair):
    width = mine.shape[1]
    half = 2 * width
    mask = mask_of(place, devices, 2 * half)
    for q, direct in enumerate((mine, got, theirs, other)):
        pair = near_pair if q < 2 else far_pair
        for c in range(0, width, 256):
            k = q * width + c
            across = mates[:, k : k + 256] + dot(other[...], pick[3 * width :, k : k + 256])
            mixed = coef[0:1, k : k + 256] * direct[:, c : c + 256].astype(F32) + coef[1:2, k : k + 256] * across
            for d in (0, LANES):
                pair[:, block((mask ^ (k + d)) & (half - 1), LANES)] = mixed[:, d : d + LANES].astype(BF)
    rows = out.shape[0]
    for r in range(0, rows, 256):
        total = dot(near[r : r + 256, :], near_pair[...], NT) + dot(far[r : r + 256, :], far_pair[...], NT)
        out[r : r + 256, :] = total.astype(BF)


def swap(x, devices, bits):
    return lax.ppermute(x, "frdm", [(i, i ^ bits) for i in range(devices)])


def shards(devices, loads, shapes, mode_order, partner, taps, offsets, coef):
    rows, modes = shapes.shape
    hist, count = loads.shape[1], taps.shape[1]
    half, quarter = modes // 2, modes // 4
    place = lax.axis_index("frdm").astype(I32).reshape(1)
    forward = forward_table(hist)
    tap_forward, last = tap_table(hist, count)
    phase = phase_table(hist, hist - W - count + 1)
    inverse = inverse_table(hist, count)
    order, mates, offsets, taps = mode_order[None], partner[None], offsets[None], taps.T

    sent, lft, far, stack, coef_near = call(
        project_kernel, "project",
        [near(hist + EXTRA, half), near(hist, rows), near(rows, half), near(count - 1 + EXTRA, modes), near(*coef.shape)],
        place, loads, forward, shapes, taps, offsets, coef, far=range(1, 7),
        scratch=[
            pltpu.VMEM(loads.shape, BF), pltpu.VMEM(forward.shape, BF), pltpu.VMEM(taps.shape, F32),
            pltpu.VMEM(offsets.shape, I32), pltpu.SemaphoreType.DMA((5 + rows // 256,)),
        ],
        limit=24,
    )
    got = swap(sent, devices, 1)
    spec, own, shapes, *held = call(
        spectrum_kernel, "spectrum",
        [near(hist, quarter, dtype=F32)] * 2 + [near(rows, half)]
        + [near(*t.shape) for t in (tap_forward, last, phase, inverse)],
        place, stack, order, lft, shapes, tap_forward, last, phase, inverse, far=range(4, 9),
        scratch=[pltpu.SemaphoreType.DMA((6,))],
    )
    inverse = held[-1]
    away = call(respond_kernel, "respond", [array(W + EXTRA, quarter)], place, own, got, spec, inverse, coef_near)[0]

    def respond_own():
        return call(
            whole_kernel, "whole", [array(W, quarter, dtype=F32)], place, stack, order, lft, got, shapes, *held
        )[0]

    pair = functools.partial(pick_kernel, devices)
    if devices == 16:
        size = modes // devices
        away = swap(away, devices, 2)
        keep, known, *parts = call(
            fold_kernel, "fold", [array(W, size, dtype=F32), array(EXTRA, LANES)] + [array(W + EXTRA, size)] * 3,
            place, respond_own(), away, coef_near, got,
        )
        parts = [swap(part, devices, 4 * d) for d, part in reversed(list(zip((1, 2, 3), parts)))]
        pick = call(pair, "pick", [near(modes, modes)], place, mates, keep)[0]
        total = call(settle_kernel, "settle", [array(W, size)], pick, keep, *parts, scalars=0)[0]
        spread = [swap(total, devices, 4 * d) for d in (3, 2, 1)]
        mode_coef = call(
            mixers_kernel, "mixers", [array(8, modes, dtype=F32)],
            place, order, known, *parts, total, scratch=[pltpu.VMEM((8, modes), F32)],
        )[0]
        mine = join(total, *reversed(spread), after=mode_coef)
        resp = swap(mine, devices, 2)
        theirs = swap(mine, devices, 1)
        first = call(mate_kernel, "mate", [array(W, modes, dtype=F32)], mine, theirs, pick, scalars=0)[0]
        resp = join(resp, after=first)
    else:
        pick = call(pair, "pick", [near(modes, modes)], place, mates, mates)[0]
        mode_coef = call(
            functools.partial(plain_mixers_kernel, devices), "mixers", [array(8, modes, dtype=F32)],
            place, order, lax.all_gather(coef, "frdm", axis=1, tiled=True), scratch=[pltpu.VMEM((8, modes), F32)],
        )[0]
        away, resp = away[:W].astype(F32), respond_own()
        resp = jnp.where(place[0] & 2, jnp.concatenate([away, resp], axis=1), jnp.concatenate([resp, away], axis=1))
        groups = [list(range(c, devices, 2)) for c in range(2)]
        resp = lax.psum(resp, "frdm", axis_index_groups=groups).astype(BF)
        mine, resp = resp[:, :quarter], resp[:, quarter:]
        theirs = swap(mine, devices, 1)
        first = call(mate_kernel, "mate", [array(W, modes, dtype=F32)], mine, theirs, pick, scalars=0)[0]
    other = swap(resp, devices, 1)
    most = call(more_kernel, "more", [array(W, modes, dtype=F32)], first, resp, pick, scalars=0)[0]
    return call(
        functools.partial(expand_kernel, devices), "expand", [array(rows, W)],
        place, mine, resp, theirs, other, most, pick, mode_coef, shapes, far,
        scratch=[pltpu.VMEM((W, half), BF)] * 2,
    )[0]


def solution(mesh):
    in_specs = (P(("cases", "frdm"), None), P("frdm", None), P(), P(), P(), P(), P(None, "frdm"))
    out_specs = P(("cases", "frdm"), None)
    body = functools.partial(shards, mesh.shape["frdm"])
    return jax.shard_map(body, mesh=mesh, in_specs=in_specs, out_specs=out_specs, check_vma=False)
```

```python
import functools

import jax
import jax.numpy as jnp
import numpy as np
from jax import lax
from jax.experimental import pallas as pl
from jax.experimental.pallas import tpu as pltpu
from jax.sharding import PartitionSpec as P

W = 256
LANES = 128
EXTRA = 16
BF = jnp.bfloat16
F32 = jnp.float32
I32 = jnp.int32
NT = (((1,), (1,)), ((), ()))
NN = (((1,), (0,)), ((), ()))


def dot(a, b, dims=NN):
    return lax.dot_general(a, b, dims, preferred_element_type=F32)


def split(table):
    high = table.astype(BF)
    low = (table - high.astype(np.float64)).astype(BF)
    return high, low


def turns(half, n):
    odd = 2 * np.arange(half)[:, None] + 1
    angle = (odd * n[None, :]) % (4 * half) * (np.pi / (2 * half))
    return np.cos(angle), np.sin(angle)


def forward_table(hist):
    cos, sin = turns(hist // 2, np.arange(hist))
    return np.concatenate([cos, -sin]).astype(BF)


def tap_table(hist, taps):
    cos, sin = turns(hist // 2, np.arange(taps))
    table = np.concatenate([cos, -sin])
    last = np.repeat(table[:, -1:], LANES, axis=1).astype(BF)
    return np.concatenate(split(table[:, :-1]), axis=1), last


def phase_table(hist, delay):
    cos, sin = turns(hist // 2, np.arange(1, delay + 1))
    return np.concatenate(split(np.concatenate([cos - 1.0, sin])), axis=1)


def inverse_table(hist, taps):
    cos, sin = turns(hist // 2, np.arange(W) + taps - 1)
    return np.concatenate(split(np.concatenate([cos, -sin]).T * (2.0 / hist)), axis=1)


def call(kernel, name, out_shape, *args, scalars=1, far=(), scratch=(), limit=16):
    vmem = pl.BlockSpec(memory_space=pltpu.VMEM)
    smem = pl.BlockSpec(memory_space=pltpu.SMEM)
    hbm = pl.BlockSpec(memory_space=pltpu.HBM)
    places = [smem] * scalars + [vmem] * (len(args) - scalars)
    args = list(args)
    for i in far:
        places[i] = hbm
        args[i] = pltpu.with_memory_space_constraint(jnp.asarray(args[i]), pltpu.HBM)
    return pl.pallas_call(
        kernel,
        in_specs=places,
        out_specs=[vmem] * len(out_shape),
        out_shape=out_shape,
        scratch_shapes=list(scratch),
        compiler_params=pltpu.CompilerParams(vmem_limit_bytes=limit * 1024 * 1024),
        name=name,
    )(*args)


def array(*shape, dtype=BF):
    return jax.ShapeDtypeStruct(shape, dtype)


def near(*shape, dtype=BF):
    return pltpu.VMEM(shape, dtype)


def block(start, size):
    return pl.ds(pl.multiple_of(start, LANES), size)


def hot(mask):
    return mask.astype(F32).astype(BF)


def fetch(pairs, sems):
    return [pltpu.make_async_copy(a, b, sems.at[i]) for i, (a, b) in enumerate(pairs)]


def project_kernel(
    place, loads_far, forward_far, shapes_far, taps_far, offsets_far, coef_far,
    sent, lft, shapes, stack, coef, loads, forward, taps, offsets, sems,
):
    rows, half = loads.shape[0], sent.shape[1]
    hist = lft.shape[0]
    start = (1 - (place[0] & 1)) * half
    step = 256
    chunks = [pl.ds(r, step) for r in range(0, rows, step)]
    pairs = [(forward_far, forward)] + [(loads_far.at[r, :], loads.at[r, :]) for r in chunks]
    first = len(pairs)
    pairs += [
        (coef_far, coef),
        (offsets_far, offsets),
        (shapes_far.at[:, block(start, half)], shapes),
        (taps_far, taps),
    ]
    copies = fetch(pairs, sems)
    for copy in copies[:first]:
        copy.start()
    copies[0].wait()
    for i, r in enumerate(chunks):
        copies[1 + i].wait()
        if i == 0:
            for copy in copies[first:]:
                copy.start()
        lft[:, i * step : (i + 1) * step] = dot(forward[...], loads[r, :], NT).astype(BF)
    for copy in copies[first : first + 3]:
        copy.wait()
    count = taps.shape[0] - 1
    for c in range(0, half, step):
        sent[:hist, c : c + step] = dot(lft[...], shapes[:, c : c + step]).astype(BF)
    sent[hist:, :] = jnp.zeros((EXTRA, half), BF)
    sent[hist : hist + 2, : coef.shape[1]] = coef[...]
    copies[first + 3].wait()
    for r in range(0, count, 64):
        stack[r : r + 64, :] = taps[r : r + 64, :].astype(BF)
    index = lax.broadcasted_iota(I32, (EXTRA, taps.shape[1]), 0)
    end = taps[count : count + 1, :]
    tail = jnp.where(index == 0, end, jnp.where(index == 1, offsets[...].astype(F32), 0.0))
    stack[count:, :] = tail.astype(BF)


def quarter_start(place, which, modes):
    return (((place[0] >> 1) & 1) ^ which) * (modes // 4)


def gather_taps(base, stack, order):
    count = stack.shape[0] - EXTRA
    mode = lax.broadcasted_iota(I32, (256, stack.shape[1]), 0) + base
    picked = dot(stack[...], hot(mode == order[...]), NT)
    tail = picked[count:]
    return picked[:count].astype(BF), tail[0:1], tail[1:2].astype(I32)


def spectrum_of(main, end, offset, table, last, phase):
    half = table.shape[0] // 2
    delay = phase.shape[1] // 2
    resp = dot(table[...], jnp.concatenate([main, main], axis=0))
    resp = resp + jnp.tile(last[...].astype(F32), (1, 2)) * end
    which = hot(lax.broadcasted_iota(I32, (delay, 256), 0) + 1 == offset)
    turn = dot(phase[...], jnp.concatenate([which, which], axis=0))
    cos, sin = turn[:half] + 1.0, turn[half:]
    re, im = resp[:half], resp[half:]
    return cos * re - sin * im, sin * re + cos * im


def spectrum_kernel(
    place, stack, order, lft, shapes_far, table_far, last_far, phase_far, inverse_far,
    spec, own, shapes, table, last, phase, inverse, sems,
):
    width = spec.shape[1]
    half = spec.shape[0] // 2
    modes = shapes_far.shape[1]
    core = place[0] & 1
    start, later = quarter_start(place, 1, modes), quarter_start(place, 0, modes)
    near = core * 2 * width
    copies = fetch(
        [
            (shapes_far.at[:, block(near + start, width)], shapes.at[:, block(start, width)]),
            (table_far, table),
            (last_far, last),
            (phase_far, phase),
            (inverse_far, inverse),
            (shapes_far.at[:, block(near + later, width)], shapes.at[:, block(later, width)]),
        ],
        sems,
    )
    for copy in copies:
        copy.start()
    tiles = range(0, width, 256)
    picked = [gather_taps(near + start + c, stack, order) for c in tiles]
    copies[0].wait()
    for c in tiles:
        own[:, c : c + 256] = dot(lft[...], shapes[:, block(start + c, 256)])
    for copy in copies[1:4]:
        copy.wait()
    for c, parts in zip(tiles, picked):
        spec[:half, c : c + 256], spec[half:, c : c + 256] = spectrum_of(*parts, table, last, phase)
    for copy in copies[4:]:
        copy.wait()


def impose(total, tre, tim, inverse):
    half = tre.shape[0]
    re, im = total[:half], total[half:]
    product = jnp.concatenate([re * tre - im * tim, re * tim + im * tre], axis=0)
    high = product.astype(BF)
    low = (product - high.astype(F32)).astype(BF)
    both = dot(inverse[...], jnp.concatenate([high, high], axis=0))
    return both + dot(inverse[:, : 2 * half], low)


def whole_kernel(place, stack, order, lft, other, shapes, table, last, phase, inverse, out):
    hist, modes = lft.shape[0], order.shape[1]
    start = quarter_start(place, 0, modes)
    near = (place[0] & 1) * (modes // 2) + start
    for c in range(0, out.shape[1], 256):
        spec = spectrum_of(*gather_taps(near + c, stack, order), table, last, phase)
        here = block(start + c, 256)
        total = dot(lft[...], shapes[:, here]) + other[:hist, here].astype(F32)
        out[:, c : c + 256] = impose(total, *spec, inverse)


def respond_kernel(place, own, other, spec, inverse, coef, out):
    hist, width = own.shape
    half = hist // 2
    start = quarter_start(place, 1, 4 * width)
    for c in range(0, width, 256):
        total = own[:, c : c + 256] + other[:hist, block(start + c, 256)].astype(F32)
        result = impose(total, spec[:half, c : c + 256], spec[half:, c : c + 256], inverse)
        out[:W, c : c + 256] = result.astype(BF)
    out[W:, :] = jnp.zeros((EXTRA, width), BF)
    out[W : W + 2, : coef.shape[1]] = coef[...]
    out[W + 2 : W + 4, :LANES] = other[hist : hist + 2, :LANES]


def fold_kernel(place, own, got, coef, other, keep, known, first, second, third):
    z = place[0] >> 2
    size = keep.shape[1]
    hist = other.shape[0] - EXTRA
    known[...] = jnp.zeros(known.shape, BF)
    known[0:2, :] = coef[...]
    known[2:4, :] = other[hist : hist + 2, :LANES]
    known[4:8, :] = got[W : W + 4, :LANES]
    for d, out in enumerate((keep, first, second, third)):
        where = block((z ^ d) * size, size)
        total = own[:, where] + got[:W, where].astype(F32)
        out[:W, :] = total.astype(out.dtype)
        if d:
            out[W:, :] = known[...]


def settle_kernel(after, keep, first, second, third, out):
    total = keep[...]
    for got in (first, second, third):
        total = total + got[:W, :].astype(F32)
    out[...] = total.astype(BF)


def mask_of(place, devices, modes):
    me = place[0]
    if devices == 16:
        return ((me & 1) * 8 + (me & 2) * 2 + (me >> 2)) * (modes // 16)
    return (me & 1) * (modes // 2)


def pick_kernel(devices, place, partner, after, pick):
    modes = partner.shape[1]
    mask = mask_of(place, devices, modes)
    mates = [partner[:, block(c ^ mask, LANES)] ^ mask for c in range(0, modes, LANES)]
    mates = jnp.concatenate(mates, axis=1)
    for c in range(0, modes, 256):
        pick[c : c + 256, :] = hot(lax.broadcasted_iota(I32, (256, modes), 0) + c == mates)


def mixers_kernel(place, order, known, third, second, first, after, coef, held):
    me = place[0]
    held[...] = jnp.zeros(held.shape, F32)
    for z, rows in enumerate((known, first, second, third)):
        top = rows.shape[0] - EXTRA
        for low in range(4):
            where = block((me ^ (4 * z + low)) * LANES, LANES)
            held[0:2, where] = rows[top : top + EXTRA, :].astype(F32)[2 * low : 2 * low + 2]
    mixers(order, mask_of(place, 16, order.shape[1]), held, coef)


def mixers(order, mask, held, coef):
    modes = order.shape[1]
    table = held[...].astype(BF)
    slots = order[...] ^ mask
    for c in range(0, modes, 256):
        coef[:, c : c + 256] = dot(table, hot(lax.broadcasted_iota(I32, (256, modes), 0) + c == slots), NT)


def plain_mixers_kernel(devices, place, order, every, coef, held):
    held[...] = jnp.zeros(held.shape, F32)
    held[0:2, :] = every[...].astype(F32)
    mixers(order, mask_of(place, devices, order.shape[1]), held, coef)


def join_kernel(*refs):
    *parts, out = refs
    start = 0
    for part in parts:
        out[:, start : start + part.shape[1]] = part[...]
        start += part.shape[1]


def join(*parts, after=None):
    width = sum(part.shape[1] for part in parts)
    kernel = join_kernel if after is None else lambda _, *refs: join_kernel(*refs)
    first = () if after is None else (after,)
    return call(kernel, "join", [array(parts[0].shape[0], width)], *first, *parts, scalars=0)[0]


def mate_kernel(mine, pick, out):
    half = mine.shape[1]
    for c in range(0, 2 * half, 256):
        out[:, c : c + 256] = dot(mine[...], pick[:half, c : c + 256])


def expand_kernel(devices, place, mine, theirs, mates, pick, coef, near, far, out, near_pair, far_pair):
    half = mine.shape[1]
    mask = mask_of(place, devices, 2 * half)
    for q, (direct, pair) in enumerate(((mine, near_pair), (theirs, far_pair))):
        for c in range(0, half, 256):
            k = q * half + c
            across = mates[:, k : k + 256] + dot(theirs[...], pick[half:, k : k + 256])
            mixed = coef[0:1, k : k + 256] * direct[:, c : c + 256].astype(F32) + coef[1:2, k : k + 256] * across
            for d in (0, LANES):
                pair[:, block((mask ^ (k + d)) & (half - 1), LANES)] = mixed[:, d : d + LANES].astype(BF)
    rows = out.shape[0]
    for r in range(0, rows, 256):
        total = dot(near[r : r + 256, :], near_pair[...], NT) + dot(far[r : r + 256, :], far_pair[...], NT)
        out[r : r + 256, :] = total.astype(BF)


def swap(x, devices, bits):
    return lax.ppermute(x, "frdm", [(i, i ^ bits) for i in range(devices)])


def shards(devices, loads, shapes, mode_order, partner, taps, offsets, coef):
    rows, modes = shapes.shape
    hist, count = loads.shape[1], taps.shape[1]
    half, quarter = modes // 2, modes // 4
    place = lax.axis_index("frdm").astype(I32).reshape(1)
    forward = forward_table(hist)
    tap_forward, last = tap_table(hist, count)
    phase = phase_table(hist, hist - W - count + 1)
    inverse = inverse_table(hist, count)
    order, mates, offsets, taps = mode_order[None], partner[None], offsets[None], taps.T

    sent, lft, far, stack, coef_near = call(
        project_kernel, "project",
        [near(hist + EXTRA, half), near(hist, rows), near(rows, half), near(count - 1 + EXTRA, modes), near(*coef.shape)],
        place, loads, forward, shapes, taps, offsets, coef, far=range(1, 7),
        scratch=[
            pltpu.VMEM(loads.shape, BF), pltpu.VMEM(forward.shape, BF), pltpu.VMEM(taps.shape, F32),
            pltpu.VMEM(offsets.shape, I32), pltpu.SemaphoreType.DMA((5 + rows // 256,)),
        ],
        limit=24,
    )
    got = swap(sent, devices, 1)
    spec, own, shapes, *held = call(
        spectrum_kernel, "spectrum",
        [near(hist, quarter, dtype=F32)] * 2 + [near(rows, half)]
        + [near(*t.shape) for t in (tap_forward, last, phase, inverse)],
        place, stack, order, lft, shapes, tap_forward, last, phase, inverse, far=range(4, 9),
        scratch=[pltpu.SemaphoreType.DMA((6,))],
    )
    inverse = held[-1]
    away = call(respond_kernel, "respond", [array(W + EXTRA, quarter)], place, own, got, spec, inverse, coef_near)[0]

    def respond_own():
        return call(
            whole_kernel, "whole", [array(W, quarter, dtype=F32)], place, stack, order, lft, got, shapes, *held
        )[0]

    pair = functools.partial(pick_kernel, devices)
    if devices == 16:
        size = modes // devices
        away = swap(away, devices, 2)
        keep, known, *parts = call(
            fold_kernel, "fold", [array(W, size, dtype=F32), array(EXTRA, LANES)] + [array(W + EXTRA, size)] * 3,
            place, respond_own(), away, coef_near, got,
        )
        parts = [swap(part, devices, 4 * d) for d, part in reversed(list(zip((1, 2, 3), parts)))]
        pick = call(pair, "pick", [near(modes, modes)], place, mates, keep)[0]
        total = call(settle_kernel, "settle", [array(W, size)], pick, keep, *parts, scalars=0)[0]
        spread = [swap(total, devices, 4 * d) for d in (3, 2, 1)]
        mode_coef = call(
            mixers_kernel, "mixers", [array(8, modes, dtype=F32)],
            place, order, known, *parts, total, scratch=[pltpu.VMEM((8, modes), F32)],
        )[0]
        resp = join(total, *reversed(spread), after=mode_coef)
        mine = join(resp, swap(resp, devices, 2))
    else:
        pick = call(pair, "pick", [near(modes, modes)], place, mates, mates)[0]
        mode_coef = call(
            functools.partial(plain_mixers_kernel, devices), "mixers", [array(8, modes, dtype=F32)],
            place, order, lax.all_gather(coef, "frdm", axis=1, tiled=True), scratch=[pltpu.VMEM((8, modes), F32)],
        )[0]
        away, resp = away[:W].astype(F32), respond_own()
        resp = jnp.where(place[0] & 2, jnp.concatenate([away, resp], axis=1), jnp.concatenate([resp, away], axis=1))
        groups = [list(range(c, devices, 2)) for c in range(2)]
        mine = lax.psum(resp, "frdm", axis_index_groups=groups).astype(BF)
    theirs = swap(mine, devices, 1)
    first = call(mate_kernel, "mate", [array(W, modes, dtype=F32)], mine, pick, scalars=0)[0]
    return call(
        functools.partial(expand_kernel, devices), "expand", [array(rows, W)],
        place, mine, theirs, first, pick, mode_coef, shapes, far,
        scratch=[pltpu.VMEM((W, half), BF)] * 2,
    )[0]


def solution(mesh):
    in_specs = (P(("cases", "frdm"), None), P("frdm", None), P(), P(), P(), P(), P(None, "frdm"))
    out_specs = P(("cases", "frdm"), None)
    body = functools.partial(shards, mesh.shape["frdm"])
    return jax.shard_map(body, mesh=mesh, in_specs=in_specs, out_specs=out_specs, check_vma=False)
```

```python
import functools

import jax
import jax.numpy as jnp
import numpy as np
from jax import lax
from jax.experimental import pallas as pl
from jax.experimental.pallas import tpu as pltpu
from jax.sharding import PartitionSpec as P

W = 256
LANES = 128
TILE = 512
EXTRA = 16
BF = jnp.bfloat16
F32 = jnp.float32
I32 = jnp.int32
NT = (((1,), (1,)), ((), ()))
NN = (((1,), (0,)), ((), ()))


def dot(a, b, dims=NN):
    return lax.dot_general(a, b, dims, preferred_element_type=F32)


def split(table):
    high = table.astype(BF)
    low = (table - high.astype(np.float64)).astype(BF)
    return high, low


def turns(half, n):
    odd = 2 * np.arange(half)[:, None] + 1
    angle = (odd * n[None, :]) % (4 * half) * (np.pi / (2 * half))
    return np.cos(angle), np.sin(angle)


def forward_table(hist):
    cos, sin = turns(hist // 2, np.arange(hist))
    return np.concatenate([cos, -sin]).astype(BF)


def tap_table(hist, taps):
    cos, sin = turns(hist // 2, np.arange(taps))
    table = np.concatenate([cos, -sin])
    last = np.repeat(table[:, -1:], LANES, axis=1).astype(BF)
    return np.concatenate(split(table[:, :-1]), axis=1), last


def phase_table(hist, delay):
    cos, sin = turns(hist // 2, np.arange(1, delay + 1))
    return np.concatenate(split(np.concatenate([cos - 1.0, sin])), axis=1)


def inverse_table(hist, taps):
    cos, sin = turns(hist // 2, np.arange(W) + taps - 1)
    return np.concatenate(split(np.concatenate([cos, -sin]).T * (2.0 / hist)), axis=1)


def call(kernel, name, out_shape, *args, scalars=1, far=(), scratch=(), limit=16):
    vmem = pl.BlockSpec(memory_space=pltpu.VMEM)
    smem = pl.BlockSpec(memory_space=pltpu.SMEM)
    hbm = pl.BlockSpec(memory_space=pltpu.HBM)
    places = [smem] * scalars + [vmem] * (len(args) - scalars)
    args = list(args)
    for i in far:
        places[i] = hbm
        args[i] = pltpu.with_memory_space_constraint(jnp.asarray(args[i]), pltpu.HBM)
    return pl.pallas_call(
        kernel,
        in_specs=places,
        out_specs=[vmem] * len(out_shape),
        out_shape=out_shape,
        scratch_shapes=list(scratch),
        compiler_params=pltpu.CompilerParams(vmem_limit_bytes=limit * 1024 * 1024),
        name=name,
    )(*args)


def array(*shape, dtype=BF):
    return jax.ShapeDtypeStruct(shape, dtype)


def near(*shape, dtype=BF):
    return pltpu.VMEM(shape, dtype)


def block(start, size):
    return pl.ds(pl.multiple_of(start, LANES), size)


def hot(mask):
    return mask.astype(F32).astype(BF)


def fetch(pairs, sems):
    return [pltpu.make_async_copy(a, b, sems.at[i]) for i, (a, b) in enumerate(pairs)]


def project_kernel(
    place, loads_far, forward_far, shapes_far, taps_far, offsets_far, coef_far,
    sent, lft, shapes, stack, coef, loads, forward, taps, offsets, sems,
):
    rows, half = loads.shape[0], sent.shape[1]
    hist = lft.shape[0]
    start = (1 - (place[0] & 1)) * half
    step = TILE
    pairs = [(forward_far, forward), (loads_far, loads)]
    first = len(pairs)
    pairs += [
        (coef_far, coef),
        (offsets_far, offsets),
        (shapes_far.at[:, block(start, half)], shapes),
        (taps_far, taps),
    ]
    copies = fetch(pairs, sems)
    for copy in copies[:first]:
        copy.start()
    copies[0].wait()
    for copy in copies[1:first]:
        copy.wait()
    for copy in copies[first:]:
        copy.start()

    @pl.loop(0, rows // step)
    def _(j):
        here = block(j * step, step)
        lft[:, here] = dot(forward[...], loads[here, :], NT).astype(BF)

    for copy in copies[first : first + 3]:
        copy.wait()
    count = taps.shape[0] - 1
    for c in range(0, half, step):
        sent[:hist, c : c + step] = dot(lft[...], shapes[:, c : c + step]).astype(BF)
    sent[hist:, :] = jnp.zeros((EXTRA, half), BF)
    sent[hist : hist + 2, : coef.shape[1]] = coef[...]
    copies[first + 3].wait()
    for r in range(0, count, 64):
        stack[r : r + 64, :] = taps[r : r + 64, :].astype(BF)
    index = lax.broadcasted_iota(I32, (EXTRA, taps.shape[1]), 0)
    end = taps[count : count + 1, :]
    tail = jnp.where(index == 0, end, jnp.where(index == 1, offsets[...].astype(F32), 0.0))
    stack[count:, :] = tail.astype(BF)


def quarter_start(place, which, modes):
    return (((place[0] >> 1) & 1) ^ which) * (modes // 4)


def gather_taps(base, stack, order):
    count = stack.shape[0] - EXTRA
    mode = lax.broadcasted_iota(I32, (TILE, stack.shape[1]), 0) + base
    picked = dot(stack[...], hot(mode == order[...]), NT)
    tail = picked[count:]
    return picked[:count].astype(BF), tail[0:1], tail[1:2].astype(I32)


def spectrum_of(main, end, offset, table, last, phase):
    half = table.shape[0] // 2
    delay = phase.shape[1] // 2
    resp = dot(table[...], jnp.concatenate([main, main], axis=0))
    resp = resp + jnp.tile(last[...].astype(F32), (1, TILE // LANES)) * end
    which = hot(lax.broadcasted_iota(I32, (delay, TILE), 0) + 1 == offset)
    turn = dot(phase[...], jnp.concatenate([which, which], axis=0))
    cos, sin = turn[:half] + 1.0, turn[half:]
    re, im = resp[:half], resp[half:]
    return cos * re - sin * im, sin * re + cos * im


def spectrum_kernel(
    place, stack, order, lft, shapes_far, table_far, last_far, phase_far, inverse_far,
    spec, own, shapes, table, last, phase, inverse, sems,
):
    width = spec.shape[1]
    half = spec.shape[0] // 2
    modes = shapes_far.shape[1]
    core = place[0] & 1
    start, later = quarter_start(place, 1, modes), quarter_start(place, 0, modes)
    near = core * 2 * width
    copies = fetch(
        [
            (shapes_far.at[:, block(near + start, width)], shapes.at[:, block(start, width)]),
            (table_far, table),
            (last_far, last),
            (phase_far, phase),
            (inverse_far, inverse),
            (shapes_far.at[:, block(near + later, width)], shapes.at[:, block(later, width)]),
        ],
        sems,
    )
    for copy in copies:
        copy.start()
    tiles = range(0, width, TILE)
    picked = [gather_taps(near + start + c, stack, order) for c in tiles]
    copies[0].wait()
    for c in tiles:
        own[:, c : c + TILE] = dot(lft[...], shapes[:, block(start + c, TILE)])
    for copy in copies[1:4]:
        copy.wait()
    for c, parts in zip(tiles, picked):
        spec[:half, c : c + TILE], spec[half:, c : c + TILE] = spectrum_of(*parts, table, last, phase)
    for copy in copies[4:]:
        copy.wait()


def impose(total, tre, tim, inverse):
    half = tre.shape[0]
    re, im = total[:half], total[half:]
    product = jnp.concatenate([re * tre - im * tim, re * tim + im * tre], axis=0)
    high = product.astype(BF)
    low = (product - high.astype(F32)).astype(BF)
    both = dot(inverse[...], jnp.concatenate([high, high], axis=0))
    return both + dot(inverse[:, : 2 * half], low)


def whole_kernel(place, stack, order, lft, other, shapes, table, last, phase, inverse, out):
    hist, modes = lft.shape[0], order.shape[1]
    start = quarter_start(place, 0, modes)
    near = (place[0] & 1) * (modes // 2) + start
    for c in range(0, out.shape[1], TILE):
        spec = spectrum_of(*gather_taps(near + c, stack, order), table, last, phase)
        here = block(start + c, TILE)
        total = dot(lft[...], shapes[:, here]) + other[:hist, here].astype(F32)
        out[:, c : c + TILE] = impose(total, *spec, inverse)


def respond_kernel(place, own, other, spec, inverse, coef, out):
    hist, width = own.shape
    half = hist // 2
    start = quarter_start(place, 1, 4 * width)
    for c in range(0, width, TILE):
        total = own[:, c : c + TILE] + other[:hist, block(start + c, TILE)].astype(F32)
        result = impose(total, spec[:half, c : c + TILE], spec[half:, c : c + TILE], inverse)
        out[:W, c : c + TILE] = result.astype(BF)
    out[W:, :] = jnp.zeros((EXTRA, width), BF)
    out[W : W + 2, : coef.shape[1]] = coef[...]
    out[W + 2 : W + 4, :LANES] = other[hist : hist + 2, :LANES]


def fold_kernel(place, own, got, coef, other, before, keep, known, first, second, third):
    z = place[0] >> 2
    size = keep.shape[1]
    hist = other.shape[0] - EXTRA
    known[...] = jnp.zeros(known.shape, BF)
    known[0:2, :] = coef[...]
    known[2:4, :] = other[hist : hist + 2, :LANES]
    known[4:8, :] = got[W : W + 4, :LANES]
    for d, out in enumerate((keep, first, second, third)):
        where = block((z ^ d) * size, size)
        total = own[:, where] + got[:W, where].astype(F32)
        out[:W, :] = total.astype(out.dtype)
        if d:
            out[W:, :] = known[...]


def settle_kernel(keep, first, second, third, out):
    total = keep[...]
    for got in (first, second, third):
        total = total + got[:W, :].astype(F32)
    out[...] = total.astype(BF)


def mask_of(place, devices, modes):
    me = place[0]
    if devices == 16:
        return ((me & 1) * 8 + (me & 2) * 2 + (me >> 2)) * (modes // 16)
    return (me & 1) * (modes // 2)


def pick_kernel(devices, place, partner, after, pick):
    modes = partner.shape[1]
    mask = mask_of(place, devices, modes)
    mates = [partner[:, block(c ^ mask, LANES)] ^ mask for c in range(0, modes, LANES)]
    mates = jnp.concatenate(mates, axis=1)
    for c in range(0, modes, 256):
        pick[c : c + 256, :] = hot(lax.broadcasted_iota(I32, (256, modes), 0) + c == mates)


def mixers_kernel(place, order, known, third, second, first, after, coef, held):
    me = place[0]
    held[...] = jnp.zeros(held.shape, F32)
    for z, rows in enumerate((known, first, second, third)):
        top = rows.shape[0] - EXTRA
        for low in range(4):
            where = block((me ^ (4 * z + low)) * LANES, LANES)
            held[0:2, where] = rows[top : top + EXTRA, :].astype(F32)[2 * low : 2 * low + 2]
    mixers(order, mask_of(place, 16, order.shape[1]), held, coef)


def mixers(order, mask, held, coef):
    modes = order.shape[1]
    table = held[...].astype(BF)
    slots = order[...] ^ mask
    for c in range(0, modes, TILE):
        coef[:, c : c + TILE] = dot(table, hot(lax.broadcasted_iota(I32, (TILE, modes), 0) + c == slots), NT)


def plain_mixers_kernel(devices, place, order, every, coef, held):
    held[...] = jnp.zeros(held.shape, F32)
    held[0:2, :] = every[...].astype(F32)
    mixers(order, mask_of(place, devices, order.shape[1]), held, coef)


def join_kernel(*refs):
    *parts, out = refs
    start = 0
    for part in parts:
        out[:, start : start + part.shape[1]] = part[...]
        start += part.shape[1]


def join(*parts, after=None):
    width = sum(part.shape[1] for part in parts)
    kernel = join_kernel if after is None else lambda _, *refs: join_kernel(*refs)
    first = () if after is None else (after,)
    return call(kernel, "join", [array(parts[0].shape[0], width)], *first, *parts, scalars=0)[0]


def mate_kernel(mine, pick, out):
    half = mine.shape[1]
    for c in range(0, 2 * half, TILE):
        out[:, c : c + TILE] = dot(mine[...], pick[:half, c : c + TILE])


def expand_kernel(devices, place, mine, theirs, mates, pick, coef, near, far, out, near_pair, far_pair):
    half = mine.shape[1]
    mask = mask_of(place, devices, 2 * half)
    for q, (direct, pair) in enumerate(((mine, near_pair), (theirs, far_pair))):
        for c in range(0, half, TILE):
            k = q * half + c
            here = slice(k, k + TILE)
            across = mates[:, here] + dot(theirs[...], pick[half:, here])
            mixed = coef[0:1, here] * direct[:, c : c + TILE].astype(F32) + coef[1:2, here] * across
            for d in range(0, TILE, LANES):
                pair[:, block((mask ^ (k + d)) & (half - 1), LANES)] = mixed[:, d : d + LANES].astype(BF)
    rows = out.shape[0]
    for r in range(0, rows, TILE):
        total = dot(near[r : r + TILE, :], near_pair[...], NT) + dot(far[r : r + TILE, :], far_pair[...], NT)
        out[r : r + TILE, :] = total.astype(BF)


def swap(x, devices, bits):
    return lax.ppermute(x, "frdm", [(i, i ^ bits) for i in range(devices)])


def shards(devices, loads, shapes, mode_order, partner, taps, offsets, coef):
    rows, modes = shapes.shape
    hist, count = loads.shape[1], taps.shape[1]
    half, quarter = modes // 2, modes // 4
    place = lax.axis_index("frdm").astype(I32).reshape(1)
    forward = forward_table(hist)
    tap_forward, last = tap_table(hist, count)
    phase = phase_table(hist, hist - W - count + 1)
    inverse = inverse_table(hist, count)
    order, mates, offsets, taps = mode_order[None], partner[None], offsets[None], taps.T

    sent, lft, far, stack, coef_near = call(
        project_kernel, "project",
        [near(hist + EXTRA, half), near(hist, rows), near(rows, half), near(count - 1 + EXTRA, modes), near(*coef.shape)],
        place, loads, forward, shapes, taps, offsets, coef, far=range(1, 7),
        scratch=[
            pltpu.VMEM(loads.shape, BF), pltpu.VMEM(forward.shape, BF), pltpu.VMEM(taps.shape, F32),
            pltpu.VMEM(offsets.shape, I32), pltpu.SemaphoreType.DMA((6,)),
        ],
        limit=24,
    )
    got = swap(sent, devices, 1)
    spec, own, shapes, *held = call(
        spectrum_kernel, "spectrum",
        [near(hist, quarter, dtype=F32)] * 2 + [near(rows, half)]
        + [near(*t.shape) for t in (tap_forward, last, phase, inverse)],
        place, stack, order, lft, shapes, tap_forward, last, phase, inverse, far=range(4, 9),
        scratch=[pltpu.SemaphoreType.DMA((6,))],
    )
    inverse = held[-1]
    away = call(respond_kernel, "respond", [array(W + EXTRA, quarter)], place, own, got, spec, inverse, coef_near)[0]

    def respond_own():
        return call(
            whole_kernel, "whole", [array(W, quarter, dtype=F32)], place, stack, order, lft, got, shapes, *held
        )[0]

    pair = functools.partial(pick_kernel, devices)
    if devices == 16:
        size = modes // devices
        pick = call(pair, "pick", [near(modes, modes)], place, mates, away)[0]
        away = swap(away, devices, 2)
        keep, known, *parts = call(
            fold_kernel, "fold", [array(W, size, dtype=F32), array(EXTRA, LANES)] + [array(W + EXTRA, size)] * 3,
            place, respond_own(), away, coef_near, got, pick,
        )
        parts = [swap(part, devices, 4 * d) for d, part in reversed(list(zip((1, 2, 3), parts)))]
        total = call(settle_kernel, "settle", [array(W, size)], keep, *parts, scalars=0)[0]
        spread = [swap(total, devices, 4 * d) for d in (1, 2, 3)]
        resp = join(total, *spread)
        mode_coef = call(
            mixers_kernel, "mixers", [array(8, modes, dtype=F32)],
            place, order, known, *parts, resp, scratch=[pltpu.VMEM((8, modes), F32)],
        )[0]
        mine = join(resp, swap(resp, devices, 2), after=mode_coef)
    else:
        pick = call(pair, "pick", [near(modes, modes)], place, mates, mates)[0]
        mode_coef = call(
            functools.partial(plain_mixers_kernel, devices), "mixers", [array(8, modes, dtype=F32)],
            place, order, lax.all_gather(coef, "frdm", axis=1, tiled=True), scratch=[pltpu.VMEM((8, modes), F32)],
        )[0]
        away, resp = away[:W].astype(F32), respond_own()
        resp = jnp.where(place[0] & 2, jnp.concatenate([away, resp], axis=1), jnp.concatenate([resp, away], axis=1))
        groups = [list(range(c, devices, 2)) for c in range(2)]
        mine = lax.psum(resp, "frdm", axis_index_groups=groups).astype(BF)
    theirs = swap(mine, devices, 1)
    first = call(mate_kernel, "mate", [array(W, modes, dtype=F32)], mine, pick, scalars=0)[0]
    return call(
        functools.partial(expand_kernel, devices), "expand", [array(rows, W)],
        place, mine, theirs, first, pick, mode_coef, shapes, far,
        scratch=[pltpu.VMEM((W, half), BF)] * 2,
    )[0]


def solution(mesh):
    in_specs = (P(("cases", "frdm"), None), P("frdm", None), P(), P(), P(), P(), P(None, "frdm"))
    out_specs = P(("cases", "frdm"), None)
    body = functools.partial(shards, mesh.shape["frdm"])
    return jax.shard_map(body, mesh=mesh, in_specs=in_specs, out_specs=out_specs, check_vma=False)
```

```python
import functools

import jax
import jax.numpy as jnp
import numpy as np
from jax import lax
from jax.experimental import pallas as pl
from jax.experimental.pallas import tpu as pltpu
from jax.sharding import PartitionSpec as P

W = 256
LANES = 128
TILE = 512
EXTRA = 16
BF = jnp.bfloat16
F32 = jnp.float32
I32 = jnp.int32
NT = (((1,), (1,)), ((), ()))
NN = (((1,), (0,)), ((), ()))


def dot(a, b, dims=NN):
    return lax.dot_general(a, b, dims, preferred_element_type=F32)


def split(table):
    high = table.astype(BF)
    low = (table - high.astype(np.float64)).astype(BF)
    return high, low


def turns(half, n):
    odd = 2 * np.arange(half)[:, None] + 1
    angle = (odd * n[None, :]) % (4 * half) * (np.pi / (2 * half))
    return np.cos(angle), np.sin(angle)


def forward_table(hist):
    cos, sin = turns(hist // 2, np.arange(hist))
    return np.concatenate([cos, -sin]).astype(BF)


def tap_table(hist, taps):
    cos, sin = turns(hist // 2, np.arange(taps))
    table = np.concatenate([cos, -sin])
    last = np.repeat(table[:, -1:], LANES, axis=1).astype(BF)
    return np.concatenate(split(table[:, :-1]), axis=1), last


def phase_table(hist, delay):
    cos, sin = turns(hist // 2, np.arange(1, delay + 1))
    return np.concatenate(split(np.concatenate([cos - 1.0, sin])), axis=1)


def inverse_table(hist, taps):
    cos, sin = turns(hist // 2, np.arange(W) + taps - 1)
    return np.concatenate(split(np.concatenate([cos, -sin]).T * (2.0 / hist)), axis=1)


def call(kernel, name, out_shape, *args, scalars=1, far=(), scratch=(), limit=16, alias=None):
    vmem = pl.BlockSpec(memory_space=pltpu.VMEM)
    smem = pl.BlockSpec(memory_space=pltpu.SMEM)
    hbm = pl.BlockSpec(memory_space=pltpu.HBM)
    places = [smem] * scalars + [vmem] * (len(args) - scalars)
    args = list(args)
    for i in far:
        places[i] = hbm
        args[i] = pltpu.with_memory_space_constraint(jnp.asarray(args[i]), pltpu.HBM)
    return pl.pallas_call(
        kernel,
        in_specs=places,
        out_specs=[vmem] * len(out_shape),
        out_shape=out_shape,
        input_output_aliases=alias or {},
        scratch_shapes=list(scratch),
        compiler_params=pltpu.CompilerParams(vmem_limit_bytes=limit * 1024 * 1024),
        name=name,
    )(*args)


def array(*shape, dtype=BF):
    return jax.ShapeDtypeStruct(shape, dtype)


def near(*shape, dtype=BF):
    return pltpu.VMEM(shape, dtype)


def block(start, size):
    return pl.ds(pl.multiple_of(start, LANES), size)


def hot(mask):
    return mask.astype(F32).astype(BF)


def fetch(pairs, sems):
    return [pltpu.make_async_copy(a, b, sems.at[i]) for i, (a, b) in enumerate(pairs)]


def project_kernel(
    place, loads_far, forward_far, shapes_far, taps_far, offsets_far, coef_far,
    sent, lft, shapes, stack, coef, loads, forward, taps, offsets, sems,
):
    rows, half = loads.shape[0], sent.shape[1]
    hist = lft.shape[0]
    start = (1 - (place[0] & 1)) * half
    step = TILE
    pairs = [(forward_far, forward), (loads_far, loads)]
    first = len(pairs)
    pairs += [
        (coef_far, coef),
        (offsets_far, offsets),
        (shapes_far.at[:, block(start, half)], shapes),
        (taps_far, taps),
    ]
    copies = fetch(pairs, sems)
    for copy in copies[:first]:
        copy.start()
    copies[0].wait()
    for copy in copies[1:first]:
        copy.wait()
    for copy in copies[first:]:
        copy.start()

    @pl.loop(0, rows // step)
    def _(j):
        here = block(j * step, step)
        lft[:, here] = dot(forward[...], loads[here, :], NT).astype(BF)

    for copy in copies[first : first + 3]:
        copy.wait()
    count = taps.shape[0] - 1
    for c in range(0, half, step):
        sent[:hist, c : c + step] = dot(lft[...], shapes[:, c : c + step]).astype(BF)
    sent[hist:, :] = jnp.zeros((EXTRA, half), BF)
    sent[hist : hist + 2, : coef.shape[1]] = coef[...]
    copies[first + 3].wait()
    for r in range(0, count, 64):
        stack[r : r + 64, :] = taps[r : r + 64, :].astype(BF)
    index = lax.broadcasted_iota(I32, (EXTRA, taps.shape[1]), 0)
    end = taps[count : count + 1, :]
    tail = jnp.where(index == 0, end, jnp.where(index == 1, offsets[...].astype(F32), 0.0))
    stack[count:, :] = tail.astype(BF)


def quarter_start(place, which, modes):
    return (((place[0] >> 1) & 1) ^ which) * (modes // 4)


def gather_taps(base, stack, order):
    count = stack.shape[0] - EXTRA
    mode = lax.broadcasted_iota(I32, (TILE, stack.shape[1]), 0) + base
    picked = dot(stack[...], hot(mode == order[...]), NT)
    tail = picked[count:]
    return picked[:count].astype(BF), tail[0:1], tail[1:2].astype(I32)


def spectrum_of(main, end, offset, table, last, phase):
    half = table.shape[0] // 2
    delay = phase.shape[1] // 2
    resp = dot(table[...], jnp.concatenate([main, main], axis=0))
    resp = resp + jnp.tile(last[...].astype(F32), (1, TILE // LANES)) * end
    which = hot(lax.broadcasted_iota(I32, (delay, TILE), 0) + 1 == offset)
    turn = dot(phase[...], jnp.concatenate([which, which], axis=0))
    cos, sin = turn[:half] + 1.0, turn[half:]
    re, im = resp[:half], resp[half:]
    return cos * re - sin * im, sin * re + cos * im


def spectrum_kernel(
    place, stack, order, lft, shapes_far, table_far, last_far, phase_far, inverse_far,
    spec, own, shapes, table, last, phase, inverse, sems,
):
    width = spec.shape[1]
    half = spec.shape[0] // 2
    modes = shapes_far.shape[1]
    core = place[0] & 1
    start, later = quarter_start(place, 1, modes), quarter_start(place, 0, modes)
    near = core * 2 * width
    copies = fetch(
        [
            (shapes_far.at[:, block(near + start, width)], shapes.at[:, block(start, width)]),
            (table_far, table),
            (last_far, last),
            (phase_far, phase),
            (inverse_far, inverse),
            (shapes_far.at[:, block(near + later, width)], shapes.at[:, block(later, width)]),
        ],
        sems,
    )
    for copy in copies:
        copy.start()
    tiles = range(0, width, TILE)
    picked = [gather_taps(near + start + c, stack, order) for c in tiles]
    copies[0].wait()
    for c in tiles:
        own[:, c : c + TILE] = dot(lft[...], shapes[:, block(start + c, TILE)])
    for copy in copies[1:4]:
        copy.wait()
    for c, parts in zip(tiles, picked):
        spec[:half, c : c + TILE], spec[half:, c : c + TILE] = spectrum_of(*parts, table, last, phase)
    for copy in copies[4:]:
        copy.wait()


def impose(total, tre, tim, inverse):
    half = tre.shape[0]
    re, im = total[:half], total[half:]
    product = jnp.concatenate([re * tre - im * tim, re * tim + im * tre], axis=0)
    high = product.astype(BF)
    low = (product - high.astype(F32)).astype(BF)
    both = dot(inverse[...], jnp.concatenate([high, high], axis=0))
    return both + dot(inverse[:, : 2 * half], low)


def whole_kernel(place, stack, order, lft, other, shapes, table, last, phase, inverse, out):
    hist, modes = lft.shape[0], order.shape[1]
    start = quarter_start(place, 0, modes)
    near = (place[0] & 1) * (modes // 2) + start
    for c in range(0, out.shape[1], TILE):
        spec = spectrum_of(*gather_taps(near + c, stack, order), table, last, phase)
        here = block(start + c, TILE)
        total = dot(lft[...], shapes[:, here]) + other[:hist, here].astype(F32)
        out[:, c : c + TILE] = impose(total, *spec, inverse)


def respond_kernel(place, own, other, spec, inverse, coef, before, out):
    hist, width = own.shape
    half = hist // 2
    start = quarter_start(place, 1, 4 * width)
    for c in range(0, width, TILE):
        total = own[:, c : c + TILE] + other[:hist, block(start + c, TILE)].astype(F32)
        result = impose(total, spec[:half, c : c + TILE], spec[half:, c : c + TILE], inverse)
        out[:W, c : c + TILE] = result.astype(BF)
    out[W:, :] = jnp.zeros((EXTRA, width), BF)
    out[W : W + 2, : coef.shape[1]] = coef[...]
    out[W + 2 : W + 4, :LANES] = other[hist : hist + 2, :LANES]


def fold_kernel(place, own, got, coef, other, keep, known, first, second, third):
    z = place[0] >> 2
    size = keep.shape[1]
    hist = other.shape[0] - EXTRA
    known[...] = jnp.zeros(known.shape, BF)
    known[0:2, :] = coef[...]
    known[2:4, :] = other[hist : hist + 2, :LANES]
    known[4:8, :] = got[W : W + 4, :LANES]
    for d, out in enumerate((keep, first, second, third)):
        where = block((z ^ d) * size, size)
        total = own[:, where] + got[:W, where].astype(F32)
        out[:W, :] = total.astype(out.dtype)
        if d:
            out[W:, :] = known[...]


def settle_kernel(keep, first, second, third, out):
    total = keep[...]
    for got in (first, second, third):
        total = total + got[:W, :].astype(F32)
    out[...] = total.astype(BF)


def mask_of(place, devices, modes):
    me = place[0]
    if devices == 16:
        return ((me & 1) * 8 + (me & 2) * 2 + (me >> 2)) * (modes // 16)
    return (me & 1) * (modes // 2)


def pick_kernel(devices, turn, place, partner, after, *refs):
    pick = refs[-1]
    modes = partner.shape[1]
    mask = mask_of(place, devices, modes)

    @pl.when(place[0] & 1 == turn)
    def _():
        mates = [partner[:, block(c ^ mask, LANES)] ^ mask for c in range(0, modes, LANES)]
        mates = jnp.concatenate(mates, axis=1)
        for c in range(0, modes, 256):
            pick[c : c + 256, :] = hot(lax.broadcasted_iota(I32, (256, modes), 0) + c == mates)


def mixers_kernel(place, order, known, first, second, third, after, coef, held):
    me = place[0]
    held[...] = jnp.zeros(held.shape, F32)
    for z, rows in enumerate((known, first, second, third)):
        top = rows.shape[0] - EXTRA
        for low in range(4):
            where = block((me ^ (4 * z + low)) * LANES, LANES)
            held[0:2, where] = rows[top : top + EXTRA, :].astype(F32)[2 * low : 2 * low + 2]
    mixers(order, mask_of(place, 16, order.shape[1]), held, coef)


def mixers(order, mask, held, coef):
    modes = order.shape[1]
    table = held[...].astype(BF)
    slots = order[...] ^ mask
    for c in range(0, modes, TILE):
        coef[:, c : c + TILE] = dot(table, hot(lax.broadcasted_iota(I32, (TILE, modes), 0) + c == slots), NT)


def plain_mixers_kernel(devices, place, order, every, coef, held):
    held[...] = jnp.zeros(held.shape, F32)
    held[0:2, :] = every[...].astype(F32)
    mixers(order, mask_of(place, devices, order.shape[1]), held, coef)


def join_kernel(*refs):
    *parts, out = refs
    start = 0
    for part in parts:
        out[:, start : start + part.shape[1]] = part[...]
        start += part.shape[1]


def join(*parts, after=None):
    width = sum(part.shape[1] for part in parts)
    kernel = join_kernel if after is None else lambda _, *refs: join_kernel(*refs)
    first = () if after is None else (after,)
    return call(kernel, "join", [array(parts[0].shape[0], width)], *first, *parts, scalars=0)[0]


def mate_kernel(mine, pick, out):
    half = mine.shape[1]
    for c in range(0, 2 * half, TILE):
        out[:, c : c + TILE] = dot(mine[...], pick[:half, c : c + TILE])


def expand_kernel(devices, place, mine, theirs, mates, pick, coef, near, far, out, near_pair, far_pair):
    half = mine.shape[1]
    mask = mask_of(place, devices, 2 * half)
    for q, (direct, pair) in enumerate(((mine, near_pair), (theirs, far_pair))):
        for c in range(0, half, TILE):
            k = q * half + c
            here = slice(k, k + TILE)
            across = mates[:, here] + dot(theirs[...], pick[half:, here])
            mixed = coef[0:1, here] * direct[:, c : c + TILE].astype(F32) + coef[1:2, here] * across
            for d in range(0, TILE, LANES):
                pair[:, block((mask ^ (k + d)) & (half - 1), LANES)] = mixed[:, d : d + LANES].astype(BF)
    rows = out.shape[0]
    for r in range(0, rows, TILE):
        total = dot(near[r : r + TILE, :], near_pair[...], NT) + dot(far[r : r + TILE, :], far_pair[...], NT)
        out[r : r + TILE, :] = total.astype(BF)


def swap(x, devices, bits):
    return lax.ppermute(x, "frdm", [(i, i ^ bits) for i in range(devices)])


def shards(devices, loads, shapes, mode_order, partner, taps, offsets, coef):
    rows, modes = shapes.shape
    hist, count = loads.shape[1], taps.shape[1]
    half, quarter = modes // 2, modes // 4
    place = lax.axis_index("frdm").astype(I32).reshape(1)
    forward = forward_table(hist)
    tap_forward, last = tap_table(hist, count)
    phase = phase_table(hist, hist - W - count + 1)
    inverse = inverse_table(hist, count)
    order, mates, offsets, taps = mode_order[None], partner[None], offsets[None], taps.T

    sent, lft, far, stack, coef_near = call(
        project_kernel, "project",
        [near(hist + EXTRA, half), near(hist, rows), near(rows, half), near(count - 1 + EXTRA, modes), near(*coef.shape)],
        place, loads, forward, shapes, taps, offsets, coef, far=range(1, 7),
        scratch=[
            pltpu.VMEM(loads.shape, BF), pltpu.VMEM(forward.shape, BF), pltpu.VMEM(taps.shape, F32),
            pltpu.VMEM(offsets.shape, I32), pltpu.SemaphoreType.DMA((6,)),
        ],
        limit=24,
    )
    got = swap(sent, devices, 1)
    spec, own, shapes, *held = call(
        spectrum_kernel, "spectrum",
        [near(hist, quarter, dtype=F32)] * 2 + [near(rows, half)]
        + [near(*t.shape) for t in (tap_forward, last, phase, inverse)],
        place, stack, order, lft, shapes, tap_forward, last, phase, inverse, far=range(4, 9),
        scratch=[pltpu.SemaphoreType.DMA((6,))],
    )
    inverse = held[-1]
    def pair(turn, after, *pick):
        return call(
            functools.partial(pick_kernel, devices, turn), "pick", [near(modes, modes)], place, mates, after, *pick,
            alias={3: 0} if pick else None,
        )[0]

    pick = pair(0, spec)
    away = call(
        respond_kernel, "respond", [array(W + EXTRA, quarter)], place, own, got, spec, inverse, coef_near, pick
    )[0]

    def respond_own():
        return call(
            whole_kernel, "whole", [array(W, quarter, dtype=F32)], place, stack, order, lft, got, shapes, *held
        )[0]

    if devices == 16:
        size = modes // devices
        away = swap(away, devices, 2)
        keep, known, *parts = call(
            fold_kernel, "fold", [array(W, size, dtype=F32), array(EXTRA, LANES)] + [array(W + EXTRA, size)] * 3,
            place, respond_own(), away, coef_near, got,
        )
        parts = [swap(part, devices, 4 * d) for d, part in zip((1, 2, 3), parts)]
        total = call(settle_kernel, "settle", [array(W, size)], keep, *parts, scalars=0)[0]
        spread = [swap(total, devices, 4 * d) for d in (1, 2, 3)]
        resp = join(total, *spread)
        mode_coef = call(
            mixers_kernel, "mixers", [array(8, modes, dtype=F32)],
            place, order, known, *parts, resp, scratch=[pltpu.VMEM((8, modes), F32)],
        )[0]
        pick = pair(1, mode_coef, pick)
        mine = join(resp, swap(resp, devices, 2), after=pick)
    else:
        pick = pair(1, mates, pick)
        mode_coef = call(
            functools.partial(plain_mixers_kernel, devices), "mixers", [array(8, modes, dtype=F32)],
            place, order, lax.all_gather(coef, "frdm", axis=1, tiled=True), scratch=[pltpu.VMEM((8, modes), F32)],
        )[0]
        away, resp = away[:W].astype(F32), respond_own()
        resp = jnp.where(place[0] & 2, jnp.concatenate([away, resp], axis=1), jnp.concatenate([resp, away], axis=1))
        groups = [list(range(c, devices, 2)) for c in range(2)]
        mine = lax.psum(resp, "frdm", axis_index_groups=groups).astype(BF)
    theirs = swap(mine, devices, 1)
    first = call(mate_kernel, "mate", [array(W, modes, dtype=F32)], mine, pick, scalars=0)[0]
    return call(
        functools.partial(expand_kernel, devices), "expand", [array(rows, W)],
        place, mine, theirs, first, pick, mode_coef, shapes, far,
        scratch=[pltpu.VMEM((W, half), BF)] * 2,
    )[0]


def solution(mesh):
    in_specs = (P(("cases", "frdm"), None), P("frdm", None), P(), P(), P(), P(), P(None, "frdm"))
    out_specs = P(("cases", "frdm"), None)
    body = functools.partial(shards, mesh.shape["frdm"])
    return jax.shard_map(body, mesh=mesh, in_specs=in_specs, out_specs=out_specs, check_vma=False)
```

```python
import functools

import jax
import jax.numpy as jnp
import numpy as np
from jax import lax
from jax.experimental import pallas as pl
from jax.experimental.pallas import tpu as pltpu
from jax.sharding import PartitionSpec as P

W = 256
LANES = 128
TILE = 512
EXTRA = 16
BF = jnp.bfloat16
F32 = jnp.float32
I32 = jnp.int32
NT = (((1,), (1,)), ((), ()))
NN = (((1,), (0,)), ((), ()))


def dot(a, b, dims=NN):
    return lax.dot_general(a, b, dims, preferred_element_type=F32)


def split(table):
    high = table.astype(BF)
    low = (table - high.astype(np.float64)).astype(BF)
    return high, low


def turns(half, n):
    odd = 2 * np.arange(half)[:, None] + 1
    angle = (odd * n[None, :]) % (4 * half) * (np.pi / (2 * half))
    return np.cos(angle), np.sin(angle)


def forward_table(hist):
    cos, sin = turns(hist // 2, np.arange(hist))
    return np.concatenate([cos, -sin]).astype(BF)


def tap_table(hist, taps):
    cos, sin = turns(hist // 2, np.arange(taps))
    table = np.concatenate([cos, -sin])
    last = np.repeat(table[:, -1:], LANES, axis=1).astype(BF)
    return np.concatenate(split(table[:, :-1]), axis=1), last


def phase_table(hist, delay):
    cos, sin = turns(hist // 2, np.arange(1, delay + 1))
    return np.concatenate(split(np.concatenate([cos - 1.0, sin])), axis=1)


def inverse_table(hist, taps):
    cos, sin = turns(hist // 2, np.arange(W) + taps - 1)
    return np.concatenate(split(np.concatenate([cos, -sin]).T * (2.0 / hist)), axis=1)


def call(kernel, name, out_shape, *args, scalars=1, far=(), scratch=(), limit=16, products=0):
    vmem = pl.BlockSpec(memory_space=pltpu.VMEM)
    smem = pl.BlockSpec(memory_space=pltpu.SMEM)
    hbm = pl.BlockSpec(memory_space=pltpu.HBM)
    places = [smem] * scalars + [vmem] * (len(args) - scalars)
    args = list(args)
    for i in far:
        places[i] = hbm
        args[i] = pltpu.with_memory_space_constraint(jnp.asarray(args[i]), pltpu.HBM)
    return pl.pallas_call(
        kernel,
        in_specs=places,
        out_specs=[vmem] * len(out_shape),
        out_shape=out_shape,
        scratch_shapes=list(scratch),
        cost_estimate=pl.CostEstimate(flops=2 * products, bytes_accessed=0, transcendentals=0) if products else None,
        compiler_params=pltpu.CompilerParams(vmem_limit_bytes=limit * 1024 * 1024),
        name=name,
    )(*args)


def array(*shape, dtype=BF):
    return jax.ShapeDtypeStruct(shape, dtype)


def near(*shape, dtype=BF):
    return pltpu.VMEM(shape, dtype)


def block(start, size):
    return pl.ds(pl.multiple_of(start, LANES), size)


def hot(mask):
    return mask.astype(F32).astype(BF)


def fetch(pairs, sems):
    return [pltpu.make_async_copy(a, b, sems.at[i]) for i, (a, b) in enumerate(pairs)]


def project_kernel(
    place, loads_far, forward_far, shapes_far, taps_far, offsets_far, coef_far,
    sent, lft, shapes, stack, coef, loads, forward, taps, offsets, sems,
):
    rows, half = shapes.shape
    hist, width = lft.shape[0], sent.shape[1]
    start, later = quarter_start(place, 1, 2 * half), quarter_start(place, 0, 2 * half)
    base = (1 - (place[0] & 1)) * half
    step = TILE
    pairs = [(forward_far, forward), (loads_far, loads)]
    first = len(pairs)
    pairs += [
        (coef_far, coef),
        (offsets_far, offsets),
        (shapes_far.at[:, block(base + start, width)], shapes.at[:, block(start, width)]),
        (taps_far, taps),
        (shapes_far.at[:, block(base + later, width)], shapes.at[:, block(later, width)]),
    ]
    copies = fetch(pairs, sems)
    for copy in copies[:first]:
        copy.start()
    copies[0].wait()
    for copy in copies[1:first]:
        copy.wait()
    for copy in copies[first:]:
        copy.start()

    @pl.loop(0, rows // step)
    def _(j):
        here = block(j * step, step)
        lft[:, here] = dot(forward[...], loads[here, :], NT).astype(BF)

    for copy in copies[first : first + 3]:
        copy.wait()
    count = taps.shape[0] - 1
    for c in range(0, width, step):
        sent[:hist, c : c + step] = dot(lft[...], shapes[:, block(start + c, step)]).astype(BF)
    sent[hist:, :] = jnp.zeros((EXTRA, width), BF)
    sent[hist : hist + 2, : coef.shape[1]] = coef[...]
    copies[first + 3].wait()
    for r in range(0, count, 64):
        stack[r : r + 64, :] = taps[r : r + 64, :].astype(BF)
    index = lax.broadcasted_iota(I32, (EXTRA, taps.shape[1]), 0)
    end = taps[count : count + 1, :]
    tail = jnp.where(index == 0, end, jnp.where(index == 1, offsets[...].astype(F32), 0.0))
    stack[count:, :] = tail.astype(BF)
    copies[first + 4].wait()


def project_rest_kernel(place, lft, shapes, after, sent):
    width = sent.shape[1]
    later = quarter_start(place, 0, 4 * width)
    for c in range(0, width, TILE):
        sent[:, c : c + TILE] = dot(lft[...], shapes[:, block(later + c, TILE)]).astype(BF)


def quarter_start(place, which, modes):
    return (((place[0] >> 1) & 1) ^ which) * (modes // 4)


def gather_taps(base, stack, order):
    count = stack.shape[0] - EXTRA
    mode = lax.broadcasted_iota(I32, (TILE, stack.shape[1]), 0) + base
    picked = dot(stack[...], hot(mode == order[...]), NT)
    tail = picked[count:]
    return picked[:count].astype(BF), tail[0:1], tail[1:2].astype(I32)


def spectrum_of(main, end, offset, table, last, phase):
    half = table.shape[0] // 2
    delay = phase.shape[1] // 2
    resp = dot(table[...], jnp.concatenate([main, main], axis=0))
    resp = resp + jnp.tile(last[...].astype(F32), (1, TILE // LANES)) * end
    which = hot(lax.broadcasted_iota(I32, (delay, TILE), 0) + 1 == offset)
    turn = dot(phase[...], jnp.concatenate([which, which], axis=0))
    cos, sin = turn[:half] + 1.0, turn[half:]
    re, im = resp[:half], resp[half:]
    return cos * re - sin * im, sin * re + cos * im


def spectrum_tiles(base, stack, order, table, last, phase, spec):
    half = spec.shape[0] // 2
    for c in range(0, spec.shape[1], TILE):
        parts = spectrum_of(*gather_taps(base + c, stack, order), table, last, phase)
        spec[:half, c : c + TILE], spec[half:, c : c + TILE] = parts


def spectrum_kernel(
    place, stack, order, shapes_far, table_far, last_far, phase_far, inverse_far,
    spec, shapes, table, last, phase, inverse, sems,
):
    half, modes = shapes.shape[1], shapes_far.shape[1]
    near = (place[0] & 1) * half
    copies = fetch(
        [
            (table_far, table),
            (last_far, last),
            (phase_far, phase),
            (shapes_far.at[:, block(near, half)], shapes),
            (inverse_far, inverse),
        ],
        sems,
    )
    for copy in copies:
        copy.start()
    width = spec.shape[1]
    start = near + quarter_start(place, 1, modes)
    tiles = range(0, width, TILE)
    picked = [gather_taps(start + c, stack, order) for c in tiles]
    for copy in copies[:3]:
        copy.wait()
    top = spec.shape[0] // 2
    for c, parts in zip(tiles, picked):
        spec[:top, c : c + TILE], spec[top:, c : c + TILE] = spectrum_of(*parts, table, last, phase)
    for copy in copies[3:]:
        copy.wait()


def spectrum_rest_kernel(place, stack, order, table, last, phase, after, spec):
    modes = order.shape[1]
    start = (place[0] & 1) * (modes // 2) + quarter_start(place, 0, modes)
    spectrum_tiles(start, stack, order, table, last, phase, spec)


def impose(total, tre, tim, inverse):
    half = tre.shape[0]
    re, im = total[:half], total[half:]
    product = jnp.concatenate([re * tre - im * tim, re * tim + im * tre], axis=0)
    high = product.astype(BF)
    low = (product - high.astype(F32)).astype(BF)
    both = dot(inverse[...], jnp.concatenate([high, high], axis=0))
    return both + dot(inverse[:, : 2 * half], low)


def respond_kernel(which, place, lft, shapes, other, spec, inverse, coef, out):
    hist, width = spec.shape
    half = hist // 2
    start = quarter_start(place, which, 4 * width)
    for c in range(0, width, TILE):
        total = dot(lft[...], shapes[:, block(start + c, TILE)]) + other[:hist, c : c + TILE].astype(F32)
        result = impose(total, spec[:half, c : c + TILE], spec[half:, c : c + TILE], inverse)
        out[:W, c : c + TILE] = result.astype(out.dtype)
    if out.shape[0] > W:
        out[W:, :] = jnp.zeros((EXTRA, width), BF)
        out[W : W + 2, : coef.shape[1]] = coef[...]
        out[W + 2 : W + 4, :LANES] = other[hist : hist + 2, :LANES]


def fold_kernel(place, own, got, coef, other, keep, known, first, second, third):
    z = place[0] >> 2
    size = keep.shape[1]
    hist = other.shape[0] - EXTRA
    known[...] = jnp.zeros(known.shape, BF)
    known[0:2, :] = coef[...]
    known[2:4, :] = other[hist : hist + 2, :LANES]
    known[4:8, :] = got[W : W + 4, :LANES]
    for d, out in enumerate((keep, first, second, third)):
        where = block((z ^ d) * size, size)
        total = own[:, where] + got[:W, where].astype(F32)
        out[:W, :] = total.astype(out.dtype)
        if d:
            out[W:, :] = known[...]


def settle_kernel(keep, first, second, third, out):
    total = keep[...]
    for got in (first, second, third):
        total = total + got[:W, :].astype(F32)
    out[...] = total.astype(BF)


def mask_of(place, devices, modes):
    me = place[0]
    if devices == 16:
        return ((me & 1) * 8 + (me & 2) * 2 + (me >> 2)) * (modes // 16)
    return (me & 1) * (modes // 2)


def pick_kernel(devices, place, partner, after, pick):
    modes = partner.shape[1]
    mask = mask_of(place, devices, modes)
    mates = [partner[:, block(c ^ mask, LANES)] ^ mask for c in range(0, modes, LANES)]
    mates = jnp.concatenate(mates, axis=1)
    for c in range(0, modes, 256):
        pick[c : c + 256, :] = hot(lax.broadcasted_iota(I32, (256, modes), 0) + c == mates)


def mixers_kernel(place, order, known, first, second, third, after, coef, held):
    me = place[0]
    held[...] = jnp.zeros(held.shape, F32)
    for z, rows in enumerate((known, first, second, third)):
        top = rows.shape[0] - EXTRA
        for low in range(4):
            where = block((me ^ (4 * z + low)) * LANES, LANES)
            held[0:2, where] = rows[top : top + EXTRA, :].astype(F32)[2 * low : 2 * low + 2]
    mixers(order, mask_of(place, 16, order.shape[1]), held, coef)


def mixers(order, mask, held, coef):
    modes = order.shape[1]
    table = held[...].astype(BF)
    slots = order[...] ^ mask
    for c in range(0, modes, TILE):
        coef[:, c : c + TILE] = dot(table, hot(lax.broadcasted_iota(I32, (TILE, modes), 0) + c == slots), NT)


def plain_mixers_kernel(devices, place, order, every, coef, held):
    held[...] = jnp.zeros(held.shape, F32)
    held[0:2, :] = every[...].astype(F32)
    mixers(order, mask_of(place, devices, order.shape[1]), held, coef)


def join_kernel(*refs):
    *parts, out = refs
    start = 0
    for part in parts:
        out[:, start : start + part.shape[1]] = part[...]
        start += part.shape[1]


def join(*parts, after=None):
    width = sum(part.shape[1] for part in parts)
    kernel = join_kernel if after is None else lambda _, *refs: join_kernel(*refs)
    first = () if after is None else (after,)
    return call(kernel, "join", [array(parts[0].shape[0], width)], *first, *parts, scalars=0)[0]


def mate_kernel(mine, pick, out):
    half = mine.shape[1]
    for c in range(0, 2 * half, TILE):
        out[:, c : c + TILE] = dot(mine[...], pick[:half, c : c + TILE])


def expand_kernel(devices, place, mine, theirs, mates, pick, coef, near, far, out, near_pair, far_pair):
    half = mine.shape[1]
    mask = mask_of(place, devices, 2 * half)
    for q, (direct, pair) in enumerate(((mine, near_pair), (theirs, far_pair))):
        for c in range(0, half, TILE):
            k = q * half + c
            here = slice(k, k + TILE)
            across = mates[:, here] + dot(theirs[...], pick[half:, here])
            mixed = coef[0:1, here] * direct[:, c : c + TILE].astype(F32) + coef[1:2, here] * across
            for d in range(0, TILE, LANES):
                pair[:, block((mask ^ (k + d)) & (half - 1), LANES)] = mixed[:, d : d + LANES].astype(BF)
    rows = out.shape[0]
    for r in range(0, rows, TILE):
        total = dot(near[r : r + TILE, :], near_pair[...], NT) + dot(far[r : r + TILE, :], far_pair[...], NT)
        out[r : r + TILE, :] = total.astype(BF)


def swap(x, devices, bits):
    return lax.ppermute(x, "frdm", [(i, i ^ bits) for i in range(devices)])


def shards(devices, loads, shapes, mode_order, partner, taps, offsets, coef):
    rows, modes = shapes.shape
    hist, count = loads.shape[1], taps.shape[1]
    half, quarter = modes // 2, modes // 4
    place = lax.axis_index("frdm").astype(I32).reshape(1)
    forward = forward_table(hist)
    tap_forward, last = tap_table(hist, count)
    phase = phase_table(hist, hist - W - count + 1)
    inverse = inverse_table(hist, count)
    order, mates, offsets, taps = mode_order[None], partner[None], offsets[None], taps.T

    sent, lft, far, stack, coef_near = call(
        project_kernel, "project",
        [near(hist + EXTRA, quarter), near(hist, rows), near(rows, half), near(count - 1 + EXTRA, modes), near(*coef.shape)],
        place, loads, forward, shapes, taps, offsets, coef, far=range(1, 7),
        scratch=[
            pltpu.VMEM(loads.shape, BF), pltpu.VMEM(forward.shape, BF), pltpu.VMEM(taps.shape, F32),
            pltpu.VMEM(offsets.shape, I32), pltpu.SemaphoreType.DMA((7,)),
        ],
        limit=24,
    )
    got = swap(sent, devices, 1)
    spec, shapes, *held = call(
        spectrum_kernel, "spectrum",
        [near(hist, quarter, dtype=F32), near(rows, half)] + [near(*t.shape) for t in (tap_forward, last, phase, inverse)],
        place, stack, order, shapes, tap_forward, last, phase, inverse, far=range(3, 8),
        scratch=[pltpu.SemaphoreType.DMA((5,))],
    )
    inverse = held.pop()

    def respond(which, got, spec, out):
        kernel = functools.partial(respond_kernel, which)
        return call(kernel, "respond", [out], place, lft, shapes, got, spec, inverse, coef_near)[0]

    away = respond(1, got, spec, array(W + EXTRA, quarter))
    sent = call(project_rest_kernel, "project_rest", [array(hist, quarter)], place, lft, far, away, products=4 * hist * rows * quarter)[0]
    rest = swap(sent, devices, 1)
    spec = call(
        spectrum_rest_kernel, "spectrum_rest", [array(hist, quarter, dtype=F32)], place, stack, order, *held, sent
    )[0]
    own = respond(0, rest, spec, array(W, quarter, dtype=F32))

    def pair(after):
        kernel = functools.partial(pick_kernel, devices)
        return call(kernel, "pick", [near(modes, modes)], place, mates, after)[0]

    if devices == 16:
        size = modes // devices
        away = swap(away, devices, 2)
        keep, known, *parts = call(
            fold_kernel, "fold", [array(W, size, dtype=F32), array(EXTRA, LANES)] + [array(W + EXTRA, size)] * 3,
            place, own, away, coef_near, got,
        )
        parts = [swap(part, devices, 4 * d) for d, part in zip((1, 2, 3), parts)]
        total = call(settle_kernel, "settle", [array(W, size)], keep, *parts, scalars=0)[0]
        spread = [swap(total, devices, 4 * d) for d in (1, 2, 3)]
        resp = join(total, *spread)
        mode_coef = call(
            mixers_kernel, "mixers", [array(8, modes, dtype=F32)],
            place, order, known, *parts, resp, scratch=[pltpu.VMEM((8, modes), F32)],
        )[0]
        pick = pair(mode_coef)
        mine = join(resp, swap(resp, devices, 2), after=pick)
    else:
        pick = pair(mates)
        mode_coef = call(
            functools.partial(plain_mixers_kernel, devices), "mixers", [array(8, modes, dtype=F32)],
            place, order, lax.all_gather(coef, "frdm", axis=1, tiled=True), scratch=[pltpu.VMEM((8, modes), F32)],
        )[0]
        away = away[:W].astype(F32)
        resp = jnp.where(place[0] & 2, jnp.concatenate([away, own], axis=1), jnp.concatenate([own, away], axis=1))
        groups = [list(range(c, devices, 2)) for c in range(2)]
        mine = lax.psum(resp, "frdm", axis_index_groups=groups).astype(BF)
    theirs = swap(mine, devices, 1)
    first = call(mate_kernel, "mate", [array(W, modes, dtype=F32)], mine, pick, scalars=0)[0]
    return call(
        functools.partial(expand_kernel, devices), "expand", [array(rows, W)],
        place, mine, theirs, first, pick, mode_coef, shapes, far,
        scratch=[pltpu.VMEM((W, half), BF)] * 2,
    )[0]


def solution(mesh):
    in_specs = (P(("cases", "frdm"), None), P("frdm", None), P(), P(), P(), P(), P(None, "frdm"))
    out_specs = P(("cases", "frdm"), None)
    body = functools.partial(shards, mesh.shape["frdm"])
    return jax.shard_map(body, mesh=mesh, in_specs=in_specs, out_specs=out_specs, check_vma=False)
```

```python
import functools

import jax
import jax.numpy as jnp
import numpy as np
from jax import lax
from jax.experimental import pallas as pl
from jax.experimental.pallas import tpu as pltpu
from jax.sharding import PartitionSpec as P

W = 256
LANES = 128
TILE = 512
EXTRA = 16
BF = jnp.bfloat16
F32 = jnp.float32
I32 = jnp.int32
NT = (((1,), (1,)), ((), ()))
NN = (((1,), (0,)), ((), ()))


def dot(a, b, dims=NN):
    return lax.dot_general(a, b, dims, preferred_element_type=F32)


def split(table):
    high = table.astype(BF)
    low = (table - high.astype(np.float64)).astype(BF)
    return high, low


def turns(half, n):
    odd = 2 * np.arange(half)[:, None] + 1
    angle = (odd * n[None, :]) % (4 * half) * (np.pi / (2 * half))
    return np.cos(angle), np.sin(angle)


def forward_table(hist):
    cos, sin = turns(hist // 2, np.arange(hist))
    return np.concatenate([cos, -sin]).astype(BF)


def tap_table(hist, taps):
    cos, sin = turns(hist // 2, np.arange(taps))
    table = np.concatenate([cos, -sin])
    last = np.repeat(table[:, -1:], LANES, axis=1).astype(BF)
    return np.concatenate(split(table[:, :-1]), axis=1), last


def phase_table(hist, delay):
    cos, sin = turns(hist // 2, np.arange(1, delay + 1))
    return np.concatenate(split(np.concatenate([cos - 1.0, sin])), axis=1)


def inverse_table(hist, taps):
    cos, sin = turns(hist // 2, np.arange(W) + taps - 1)
    return np.concatenate(split(np.concatenate([cos, -sin]).T * (2.0 / hist)), axis=1)


def call(kernel, name, out_shape, *args, scalars=1, far=(), scratch=(), limit=16, products=0):
    vmem = pl.BlockSpec(memory_space=pltpu.VMEM)
    smem = pl.BlockSpec(memory_space=pltpu.SMEM)
    hbm = pl.BlockSpec(memory_space=pltpu.HBM)
    places = [smem] * scalars + [vmem] * (len(args) - scalars)
    args = list(args)
    for i in far:
        places[i] = hbm
        args[i] = pltpu.with_memory_space_constraint(jnp.asarray(args[i]), pltpu.HBM)
    return pl.pallas_call(
        kernel,
        in_specs=places,
        out_specs=[vmem] * len(out_shape),
        out_shape=out_shape,
        scratch_shapes=list(scratch),
        cost_estimate=pl.CostEstimate(flops=2 * products, bytes_accessed=0, transcendentals=0) if products else None,
        compiler_params=pltpu.CompilerParams(vmem_limit_bytes=limit * 1024 * 1024),
        name=name,
    )(*args)


def array(*shape, dtype=BF):
    return jax.ShapeDtypeStruct(shape, dtype)


def near(*shape, dtype=BF):
    return pltpu.VMEM(shape, dtype)


def block(start, size):
    return pl.ds(pl.multiple_of(start, LANES), size)


def hot(mask):
    return mask.astype(F32).astype(BF)


def fetch(pairs, sems):
    return [pltpu.make_async_copy(a, b, sems.at[i]) for i, (a, b) in enumerate(pairs)]


def project_kernel(
    place, loads_far, forward_far, shapes_far, taps_far, offsets_far, coef_far,
    sent, lft, shapes, stack, coef, loads, forward, taps, offsets, sems,
):
    rows, half = shapes.shape
    hist, width = lft.shape[0], sent.shape[1]
    start, later = quarter_start(place, 1, 2 * half), quarter_start(place, 0, 2 * half)
    base = (1 - (place[0] & 1)) * half
    step = TILE
    pairs = [(forward_far, forward), (loads_far, loads)]
    first = len(pairs)
    pairs += [
        (coef_far, coef),
        (offsets_far, offsets),
        (shapes_far.at[:, block(base + start, width)], shapes.at[:, block(start, width)]),
        (taps_far, taps),
        (shapes_far.at[:, block(base + later, width)], shapes.at[:, block(later, width)]),
    ]
    copies = fetch(pairs, sems)
    for copy in copies[:first]:
        copy.start()
    copies[0].wait()
    for copy in copies[1:first]:
        copy.wait()
    for copy in copies[first:]:
        copy.start()

    @pl.loop(0, rows // step)
    def _(j):
        here = block(j * step, step)
        lft[:, here] = dot(forward[...], loads[here, :], NT).astype(BF)

    for copy in copies[first : first + 3]:
        copy.wait()
    count = taps.shape[0] - 1
    for c in range(0, width, step):
        sent[:hist, c : c + step] = dot(lft[...], shapes[:, block(start + c, step)]).astype(BF)
    sent[hist:, :] = jnp.zeros((EXTRA, width), BF)
    sent[hist : hist + 2, : coef.shape[1]] = coef[...]
    copies[first + 3].wait()
    for r in range(0, count, 64):
        stack[r : r + 64, :] = taps[r : r + 64, :].astype(BF)
    index = lax.broadcasted_iota(I32, (EXTRA, taps.shape[1]), 0)
    end = taps[count : count + 1, :]
    tail = jnp.where(index == 0, end, jnp.where(index == 1, offsets[...].astype(F32), 0.0))
    stack[count:, :] = tail.astype(BF)
    copies[first + 4].wait()


def project_rest_kernel(place, lft, shapes, after, sent):
    width = sent.shape[1]
    later = quarter_start(place, 0, 4 * width)
    for c in range(0, width, TILE):
        sent[:, c : c + TILE] = dot(lft[...], shapes[:, block(later + c, TILE)]).astype(BF)


def quarter_start(place, which, modes):
    return (((place[0] >> 1) & 1) ^ which) * (modes // 4)


def gather_taps(base, stack, order):
    count = stack.shape[0] - EXTRA
    mode = lax.broadcasted_iota(I32, (TILE, stack.shape[1]), 0) + base
    picked = dot(stack[...], hot(mode == order[...]), NT)
    tail = picked[count:]
    return picked[:count].astype(BF), tail[0:1], tail[1:2].astype(I32)


def spectrum_of(main, end, offset, table, last, phase):
    half = table.shape[0] // 2
    delay = phase.shape[1] // 2
    resp = dot(table[...], jnp.concatenate([main, main], axis=0))
    resp = resp + jnp.tile(last[...].astype(F32), (1, TILE // LANES)) * end
    which = hot(lax.broadcasted_iota(I32, (delay, TILE), 0) + 1 == offset)
    turn = dot(phase[...], jnp.concatenate([which, which], axis=0))
    cos, sin = turn[:half] + 1.0, turn[half:]
    re, im = resp[:half], resp[half:]
    return cos * re - sin * im, sin * re + cos * im


def spectrum_tiles(base, stack, order, table, last, phase, spec):
    half = spec.shape[0] // 2
    for c in range(0, spec.shape[1], TILE):
        parts = spectrum_of(*gather_taps(base + c, stack, order), table, last, phase)
        spec[:half, c : c + TILE], spec[half:, c : c + TILE] = parts


def spectrum_kernel(
    place, stack, order, shapes_far, table_far, last_far, phase_far, inverse_far,
    spec, shapes, table, last, phase, inverse, sems,
):
    half, modes = shapes.shape[1], shapes_far.shape[1]
    near = (place[0] & 1) * half
    copies = fetch(
        [
            (table_far, table),
            (last_far, last),
            (phase_far, phase),
            (shapes_far.at[:, block(near, half)], shapes),
            (inverse_far, inverse),
        ],
        sems,
    )
    for copy in copies:
        copy.start()
    width = spec.shape[1]
    start = near + quarter_start(place, 1, modes)
    tiles = range(0, width, TILE)
    picked = [gather_taps(start + c, stack, order) for c in tiles]
    for copy in copies[:3]:
        copy.wait()
    top = spec.shape[0] // 2
    for c, parts in zip(tiles, picked):
        spec[:top, c : c + TILE], spec[top:, c : c + TILE] = spectrum_of(*parts, table, last, phase)
    for copy in copies[3:]:
        copy.wait()


def spectrum_rest_kernel(place, stack, order, table, last, phase, after, spec):
    modes = order.shape[1]
    start = (place[0] & 1) * (modes // 2) + quarter_start(place, 0, modes)
    spectrum_tiles(start, stack, order, table, last, phase, spec)


def impose(total, tre, tim, inverse):
    half = tre.shape[0]
    re, im = total[:half], total[half:]
    product = jnp.concatenate([re * tre - im * tim, re * tim + im * tre], axis=0)
    high = product.astype(BF)
    low = (product - high.astype(F32)).astype(BF)
    both = dot(inverse[...], jnp.concatenate([high, high], axis=0))
    return both + dot(inverse[:, : 2 * half], low)


def respond_kernel(which, place, lft, shapes, other, spec, inverse, coef, out):
    hist, width = spec.shape
    half = hist // 2
    start = quarter_start(place, which, 4 * width)
    for c in range(0, width, TILE):
        total = dot(lft[...], shapes[:, block(start + c, TILE)]) + other[:hist, c : c + TILE].astype(F32)
        result = impose(total, spec[:half, c : c + TILE], spec[half:, c : c + TILE], inverse)
        out[:W, c : c + TILE] = result.astype(out.dtype)
    if out.shape[0] > W:
        out[W:, :] = jnp.zeros((EXTRA, width), BF)
        out[W : W + 2, : coef.shape[1]] = coef[...]
        out[W + 2 : W + 4, :LANES] = other[hist : hist + 2, :LANES]


def turns_of(core):
    return 3 - 2 * core, 2, 1 + 2 * core


def fold_kernel(place, own, got, coef, other, keep, known, first, second, third):
    z = place[0] >> 2
    size = keep.shape[1]
    hist = other.shape[0] - EXTRA
    known[...] = jnp.zeros(known.shape, BF)
    known[0:2, :] = coef[...]
    known[2:4, :] = other[hist : hist + 2, :LANES]
    known[4:8, :] = got[W : W + 4, :LANES]
    for d, out in zip((0, *turns_of(place[0] & 1)), (keep, first, second, third)):
        where = block((z ^ d) * size, size)
        total = own[:, where] + got[:W, where].astype(F32)
        out[:W, :] = total.astype(out.dtype)
        if out.shape[0] > W:
            out[W:, :] = known[...]


def settle_kernel(keep, first, second, third, out):
    total = keep[...]
    for got in (first, second, third):
        total = total + got[:W, :].astype(F32)
    out[...] = total.astype(BF)


def mask_of(place, devices, modes):
    me = place[0]
    if devices == 16:
        return ((me & 1) * 8 + (me & 2) * 2 + (me >> 2)) * (modes // 16)
    return (me & 1) * (modes // 2)


def pick_kernel(devices, place, partner, after, pick):
    modes = partner.shape[1]
    mask = mask_of(place, devices, modes)
    mates = [partner[:, block(c ^ mask, LANES)] ^ mask for c in range(0, modes, LANES)]
    mates = jnp.concatenate(mates, axis=1)
    for c in range(0, modes, 256):
        pick[c : c + 256, :] = hot(lax.broadcasted_iota(I32, (256, modes), 0) + c == mates)


def mixers_kernel(place, order, known, first, second, third, after, coef, held):
    me = place[0]
    held[...] = jnp.zeros(held.shape, F32)
    for z, rows in zip((0, *turns_of(me & 1)), (known, first, second, third)):
        top = rows.shape[0] - EXTRA
        for low in range(4):
            where = block((me ^ (4 * z + low)) * LANES, LANES)
            held[0:2, where] = rows[top : top + EXTRA, :].astype(F32)[2 * low : 2 * low + 2]
    mixers(order, mask_of(place, 16, order.shape[1]), held, coef)


def mixers(order, mask, held, coef):
    modes = order.shape[1]
    table = held[...].astype(BF)
    slots = order[...] ^ mask
    for c in range(0, modes, TILE):
        coef[:, c : c + TILE] = dot(table, hot(lax.broadcasted_iota(I32, (TILE, modes), 0) + c == slots), NT)


def plain_mixers_kernel(devices, place, order, every, coef, held):
    held[...] = jnp.zeros(held.shape, F32)
    held[0:2, :] = every[...].astype(F32)
    mixers(order, mask_of(place, devices, order.shape[1]), held, coef)


def join_kernel(*refs):
    *parts, out = refs
    start = 0
    for part in parts:
        out[:, start : start + part.shape[1]] = part[...]
        start += part.shape[1]


def join(*parts, after=None):
    width = sum(part.shape[1] for part in parts)
    kernel = join_kernel if after is None else lambda _, *refs: join_kernel(*refs)
    first = () if after is None else (after,)
    return call(kernel, "join", [array(parts[0].shape[0], width)], *first, *parts, scalars=0)[0]


def mate_kernel(mine, pick, out):
    half = mine.shape[1]
    for c in range(0, 2 * half, TILE):
        out[:, c : c + TILE] = dot(mine[...], pick[:half, c : c + TILE])


def expand_kernel(devices, place, mine, theirs, mates, pick, coef, near, far, out, near_pair, far_pair):
    half = mine.shape[1]
    mask = mask_of(place, devices, 2 * half)
    for q, (direct, pair) in enumerate(((mine, near_pair), (theirs, far_pair))):
        for c in range(0, half, TILE):
            k = q * half + c
            here = slice(k, k + TILE)
            across = mates[:, here] + dot(theirs[...], pick[half:, here])
            mixed = coef[0:1, here] * direct[:, c : c + TILE].astype(F32) + coef[1:2, here] * across
            for d in range(0, TILE, LANES):
                pair[:, block((mask ^ (k + d)) & (half - 1), LANES)] = mixed[:, d : d + LANES].astype(BF)
    rows = out.shape[0]
    for r in range(0, rows, TILE):
        total = dot(near[r : r + TILE, :], near_pair[...], NT) + dot(far[r : r + TILE, :], far_pair[...], NT)
        out[r : r + TILE, :] = total.astype(BF)


def swap(x, devices, bits, odd=None):
    odd = bits if odd is None else odd
    return lax.ppermute(x, "frdm", [(i, i ^ (odd if i & 1 else bits)) for i in range(devices)])


def shards(devices, loads, shapes, mode_order, partner, taps, offsets, coef):
    rows, modes = shapes.shape
    hist, count = loads.shape[1], taps.shape[1]
    half, quarter = modes // 2, modes // 4
    place = lax.axis_index("frdm").astype(I32).reshape(1)
    forward = forward_table(hist)
    tap_forward, last = tap_table(hist, count)
    phase = phase_table(hist, hist - W - count + 1)
    inverse = inverse_table(hist, count)
    order, mates, offsets, taps = mode_order[None], partner[None], offsets[None], taps.T

    sent, lft, far, stack, coef_near = call(
        project_kernel, "project",
        [near(hist + EXTRA, quarter), near(hist, rows), near(rows, half), near(count - 1 + EXTRA, modes), near(*coef.shape)],
        place, loads, forward, shapes, taps, offsets, coef, far=range(1, 7),
        scratch=[
            pltpu.VMEM(loads.shape, BF), pltpu.VMEM(forward.shape, BF), pltpu.VMEM(taps.shape, F32),
            pltpu.VMEM(offsets.shape, I32), pltpu.SemaphoreType.DMA((7,)),
        ],
        limit=24,
    )
    got = swap(sent, devices, 1)
    spec, shapes, *held = call(
        spectrum_kernel, "spectrum",
        [near(hist, quarter, dtype=F32), near(rows, half)] + [near(*t.shape) for t in (tap_forward, last, phase, inverse)],
        place, stack, order, shapes, tap_forward, last, phase, inverse, far=range(3, 8),
        scratch=[pltpu.SemaphoreType.DMA((5,))],
    )
    inverse = held.pop()

    def respond(which, got, spec, out):
        kernel = functools.partial(respond_kernel, which)
        return call(kernel, "respond", [out], place, lft, shapes, got, spec, inverse, coef_near)[0]

    away = respond(1, got, spec, array(W + EXTRA, quarter))
    sent = call(project_rest_kernel, "project_rest", [array(hist, quarter)], place, lft, far, away, products=4 * hist * rows * quarter)[0]
    rest = swap(sent, devices, 1)
    spec = call(
        spectrum_rest_kernel, "spectrum_rest", [array(hist, quarter, dtype=F32)], place, stack, order, *held, sent
    )[0]
    own = respond(0, rest, spec, array(W, quarter, dtype=F32))

    def pair(after):
        kernel = functools.partial(pick_kernel, devices)
        return call(kernel, "pick", [near(modes, modes)], place, mates, after)[0]

    if devices == 16:
        size = modes // devices
        away = swap(away, devices, 2)
        keep, known, *parts = call(
            fold_kernel, "fold", [array(W, size, dtype=F32), array(EXTRA, LANES)] + [array(W + EXTRA, size)] * 3,
            place, own, away, coef_near, got,
        )
        ways = zip(turns_of(0), turns_of(1))
        parts = [swap(part, devices, 4 * even, 4 * odd) for part, (even, odd) in zip(parts, ways)]
        total = call(settle_kernel, "settle", [array(W, size)], keep, *parts, scalars=0)[0]
        spread = [swap(total, devices, 4 * d) for d in (1, 2, 3)]
        resp = join(total, *spread)
        mode_coef = call(
            mixers_kernel, "mixers", [array(8, modes, dtype=F32)],
            place, order, known, *parts, resp, scratch=[pltpu.VMEM((8, modes), F32)],
        )[0]
        pick = pair(mode_coef)
        mine = join(resp, swap(resp, devices, 2), after=pick)
    else:
        pick = pair(mates)
        mode_coef = call(
            functools.partial(plain_mixers_kernel, devices), "mixers", [array(8, modes, dtype=F32)],
            place, order, lax.all_gather(coef, "frdm", axis=1, tiled=True), scratch=[pltpu.VMEM((8, modes), F32)],
        )[0]
        away = away[:W].astype(F32)
        resp = jnp.where(place[0] & 2, jnp.concatenate([away, own], axis=1), jnp.concatenate([own, away], axis=1))
        groups = [list(range(c, devices, 2)) for c in range(2)]
        mine = lax.psum(resp, "frdm", axis_index_groups=groups).astype(BF)
    theirs = swap(mine, devices, 1)
    first = call(mate_kernel, "mate", [array(W, modes, dtype=F32)], mine, pick, scalars=0)[0]
    return call(
        functools.partial(expand_kernel, devices), "expand", [array(rows, W)],
        place, mine, theirs, first, pick, mode_coef, shapes, far,
        scratch=[pltpu.VMEM((W, half), BF)] * 2,
    )[0]


def solution(mesh):
    in_specs = (P(("cases", "frdm"), None), P("frdm", None), P(), P(), P(), P(), P(None, "frdm"))
    out_specs = P(("cases", "frdm"), None)
    body = functools.partial(shards, mesh.shape["frdm"])
    return jax.shard_map(body, mesh=mesh, in_specs=in_specs, out_specs=out_specs, check_vma=False)
```

```python
import functools

import jax
import jax.numpy as jnp
import numpy as np
from jax import lax
from jax.experimental import pallas as pl
from jax.experimental.pallas import tpu as pltpu
from jax.sharding import PartitionSpec as P

W = 256
LANES = 128
TILE = 512
EXTRA = 16
BF = jnp.bfloat16
F32 = jnp.float32
I32 = jnp.int32
NT = (((1,), (1,)), ((), ()))
NN = (((1,), (0,)), ((), ()))


def dot(a, b, dims=NN):
    return lax.dot_general(a, b, dims, preferred_element_type=F32)


def split(table):
    high = table.astype(BF)
    low = (table - high.astype(np.float64)).astype(BF)
    return high, low


def turns(half, n):
    odd = 2 * np.arange(half)[:, None] + 1
    angle = (odd * n[None, :]) % (4 * half) * (np.pi / (2 * half))
    return np.cos(angle), np.sin(angle)


def forward_table(hist):
    cos, sin = turns(hist // 2, np.arange(hist))
    return np.concatenate([cos, -sin]).astype(BF)


def tap_table(hist, taps):
    cos, sin = turns(hist // 2, np.arange(taps))
    table = np.concatenate([cos, -sin])
    last = np.repeat(table[:, -1:], LANES, axis=1).astype(BF)
    return np.concatenate(split(table[:, :-1]), axis=1), last


def phase_table(hist, delay):
    cos, sin = turns(hist // 2, np.arange(1, delay + 1))
    return np.concatenate(split(np.concatenate([cos - 1.0, sin])), axis=1)


def inverse_table(hist, taps):
    cos, sin = turns(hist // 2, np.arange(W) + taps - 1)
    return np.concatenate(split(np.concatenate([cos, -sin]).T * (2.0 / hist)), axis=1)


def call(kernel, name, out_shape, *args, scalars=1, far=(), scratch=(), limit=16, products=0):
    vmem = pl.BlockSpec(memory_space=pltpu.VMEM)
    smem = pl.BlockSpec(memory_space=pltpu.SMEM)
    hbm = pl.BlockSpec(memory_space=pltpu.HBM)
    places = [smem] * scalars + [vmem] * (len(args) - scalars)
    args = list(args)
    for i in far:
        places[i] = hbm
        args[i] = pltpu.with_memory_space_constraint(jnp.asarray(args[i]), pltpu.HBM)
    return pl.pallas_call(
        kernel,
        in_specs=places,
        out_specs=[vmem] * len(out_shape),
        out_shape=out_shape,
        scratch_shapes=list(scratch),
        cost_estimate=pl.CostEstimate(flops=2 * products, bytes_accessed=0, transcendentals=0) if products else None,
        compiler_params=pltpu.CompilerParams(vmem_limit_bytes=limit * 1024 * 1024),
        name=name,
    )(*args)


def array(*shape, dtype=BF):
    return jax.ShapeDtypeStruct(shape, dtype)


def near(*shape, dtype=BF):
    return pltpu.VMEM(shape, dtype)


def block(start, size):
    return pl.ds(pl.multiple_of(start, LANES), size)


def hot(mask):
    return mask.astype(F32).astype(BF)


def fetch(pairs, sems):
    return [pltpu.make_async_copy(a, b, sems.at[i]) for i, (a, b) in enumerate(pairs)]


def project_kernel(
    place, loads_far, forward_far, shapes_far, taps_far, offsets_far, coef_far,
    sent, lft, shapes, stack, coef, loads, forward, taps, offsets, sems,
):
    rows, half = shapes.shape
    hist, width = lft.shape[0], sent.shape[1]
    start, later = quarter_start(place, 1, 2 * half), quarter_start(place, 0, 2 * half)
    base = (1 - (place[0] & 1)) * half
    step = TILE
    pairs = [(forward_far, forward), (loads_far, loads)]
    first = len(pairs)
    pairs += [
        (coef_far, coef),
        (offsets_far, offsets),
        (shapes_far.at[:, block(base + start, width)], shapes.at[:, block(start, width)]),
        (taps_far, taps),
        (shapes_far.at[:, block(base + later, width)], shapes.at[:, block(later, width)]),
    ]
    copies = fetch(pairs, sems)
    for copy in copies[:first]:
        copy.start()
    copies[0].wait()
    for copy in copies[1:first]:
        copy.wait()
    for copy in copies[first:]:
        copy.start()

    @pl.loop(0, rows // step)
    def _(j):
        here = block(j * step, step)
        lft[:, here] = dot(forward[...], loads[here, :], NT).astype(BF)

    for copy in copies[first : first + 3]:
        copy.wait()
    count = taps.shape[0] - 1
    for c in range(0, width, step):
        sent[:hist, c : c + step] = dot(lft[...], shapes[:, block(start + c, step)]).astype(BF)
    sent[hist:, :] = jnp.zeros((EXTRA, width), BF)
    sent[hist : hist + 2, : coef.shape[1]] = coef[...]
    copies[first + 3].wait()
    for r in range(0, count, 64):
        stack[r : r + 64, :] = taps[r : r + 64, :].astype(BF)
    index = lax.broadcasted_iota(I32, (EXTRA, taps.shape[1]), 0)
    end = taps[count : count + 1, :]
    tail = jnp.where(index == 0, end, jnp.where(index == 1, offsets[...].astype(F32), 0.0))
    stack[count:, :] = tail.astype(BF)
    copies[first + 4].wait()


def project_rest_kernel(place, lft, shapes, after, sent):
    width = sent.shape[1]
    later = quarter_start(place, 0, 4 * width)
    for c in range(0, width, TILE):
        sent[:, c : c + TILE] = dot(lft[...], shapes[:, block(later + c, TILE)]).astype(BF)


def quarter_start(place, which, modes):
    return (((place[0] >> 1) & 1) ^ which) * (modes // 4)


def gather_taps(base, stack, order):
    count = stack.shape[0] - EXTRA
    mode = lax.broadcasted_iota(I32, (TILE, stack.shape[1]), 0) + base
    picked = dot(stack[...], hot(mode == order[...]), NT)
    tail = picked[count:]
    return picked[:count].astype(BF), tail[0:1], tail[1:2].astype(I32)


def spectrum_of(main, end, offset, table, last, phase):
    half = table.shape[0] // 2
    delay = phase.shape[1] // 2
    resp = dot(table[...], jnp.concatenate([main, main], axis=0))
    resp = resp + jnp.tile(last[...].astype(F32), (1, TILE // LANES)) * end
    which = hot(lax.broadcasted_iota(I32, (delay, TILE), 0) + 1 == offset)
    turn = dot(phase[...], jnp.concatenate([which, which], axis=0))
    cos, sin = turn[:half] + 1.0, turn[half:]
    re, im = resp[:half], resp[half:]
    return cos * re - sin * im, sin * re + cos * im


def spectrum_tiles(base, stack, order, table, last, phase, spec):
    half = spec.shape[0] // 2
    for c in range(0, spec.shape[1], TILE):
        parts = spectrum_of(*gather_taps(base + c, stack, order), table, last, phase)
        spec[:half, c : c + TILE], spec[half:, c : c + TILE] = parts


def spectrum_kernel(
    place, stack, order, shapes_far, table_far, last_far, phase_far, inverse_far,
    spec, shapes, table, last, phase, inverse, sems,
):
    half, modes = shapes.shape[1], shapes_far.shape[1]
    near = (place[0] & 1) * half
    copies = fetch(
        [
            (table_far, table),
            (last_far, last),
            (phase_far, phase),
            (shapes_far.at[:, block(near, half)], shapes),
            (inverse_far, inverse),
        ],
        sems,
    )
    for copy in copies:
        copy.start()
    width = spec.shape[1]
    start = near + quarter_start(place, 1, modes)
    tiles = range(0, width, TILE)
    picked = [gather_taps(start + c, stack, order) for c in tiles]
    for copy in copies[:3]:
        copy.wait()
    top = spec.shape[0] // 2
    for c, parts in zip(tiles, picked):
        spec[:top, c : c + TILE], spec[top:, c : c + TILE] = spectrum_of(*parts, table, last, phase)
    for copy in copies[3:]:
        copy.wait()


def spectrum_rest_kernel(place, stack, order, table, last, phase, after, spec):
    modes = order.shape[1]
    start = (place[0] & 1) * (modes // 2) + quarter_start(place, 0, modes)
    spectrum_tiles(start, stack, order, table, last, phase, spec)


def impose(total, tre, tim, inverse):
    half = tre.shape[0]
    re, im = total[:half], total[half:]
    product = jnp.concatenate([re * tre - im * tim, re * tim + im * tre], axis=0)
    high = product.astype(BF)
    low = (product - high.astype(F32)).astype(BF)
    both = dot(inverse[...], jnp.concatenate([high, high], axis=0))
    return both + dot(inverse[:, : 2 * half], low)


def respond_kernel(which, place, lft, shapes, other, spec, inverse, coef, out):
    hist, width = spec.shape
    half = hist // 2
    start = quarter_start(place, which, 4 * width)
    for c in range(0, width, TILE):
        total = dot(lft[...], shapes[:, block(start + c, TILE)]) + other[:hist, c : c + TILE].astype(F32)
        result = impose(total, spec[:half, c : c + TILE], spec[half:, c : c + TILE], inverse)
        out[:W, c : c + TILE] = result.astype(out.dtype)
    if out.shape[0] > W:
        out[W:, :] = jnp.zeros((EXTRA, width), BF)
        out[W : W + 2, : coef.shape[1]] = coef[...]
        out[W + 2 : W + 4, :LANES] = other[hist : hist + 2, :LANES]


def turns_of(core):
    return 3 - 2 * core, 2, 1 + 2 * core


def fold_kernel(place, own, got, coef, other, keep, known, first, second, third):
    z = place[0] >> 2
    size = keep.shape[1]
    hist = other.shape[0] - EXTRA
    known[...] = jnp.zeros(known.shape, BF)
    known[0:2, :] = coef[...]
    known[2:4, :] = other[hist : hist + 2, :LANES]
    known[4:8, :] = got[W : W + 4, :LANES]
    for d, out in zip((0, *turns_of(place[0] & 1)), (keep, first, second, third)):
        where = block((z ^ d) * size, size)
        total = own[:, where] + got[:W, where].astype(F32)
        out[:W, :] = total.astype(out.dtype)
        if out.shape[0] > W:
            out[W:, :] = known[...]


def settle_kernel(keep, first, second, third, out):
    total = keep[...]
    for got in (first, second, third):
        total = total + got[:W, :].astype(F32)
    out[...] = total.astype(BF)


def mask_of(place, devices, modes):
    me = place[0]
    if devices == 16:
        return ((me & 1) * 8 + (me & 2) * 2 + (me >> 2)) * (modes // 16)
    return (me & 1) * (modes // 2)


def pick_kernel(devices, place, partner, after, pick):
    modes = partner.shape[1]
    mask = mask_of(place, devices, modes)
    mates = [partner[:, block(c ^ mask, LANES)] ^ mask for c in range(0, modes, LANES)]
    mates = jnp.concatenate(mates, axis=1)
    for c in range(0, modes, 256):
        pick[c : c + 256, :] = hot(lax.broadcasted_iota(I32, (256, modes), 0) + c == mates)


def mixers_kernel(place, order, known, first, second, third, after, coef, held):
    me = place[0]
    held[...] = jnp.zeros(held.shape, F32)
    for z, rows in zip((0, *turns_of(me & 1)), (known, first, second, third)):
        top = rows.shape[0] - EXTRA
        for low in range(4):
            where = block((me ^ (4 * z + low)) * LANES, LANES)
            held[0:2, where] = rows[top : top + EXTRA, :].astype(F32)[2 * low : 2 * low + 2]
    mixers(order, mask_of(place, 16, order.shape[1]), held, coef)


def mixers(order, mask, held, coef):
    modes = order.shape[1]
    table = held[...].astype(BF)
    slots = order[...] ^ mask
    for c in range(0, modes, TILE):
        coef[:, c : c + TILE] = dot(table, hot(lax.broadcasted_iota(I32, (TILE, modes), 0) + c == slots), NT)


def plain_mixers_kernel(devices, place, order, every, coef, held):
    held[...] = jnp.zeros(held.shape, F32)
    held[0:2, :] = every[...].astype(F32)
    mixers(order, mask_of(place, devices, order.shape[1]), held, coef)


def join_kernel(*refs):
    *parts, out = refs
    start = 0
    for part in parts:
        out[:, start : start + part.shape[1]] = part[...]
        start += part.shape[1]


def join(*parts, after=None):
    width = sum(part.shape[1] for part in parts)
    kernel = join_kernel if after is None else lambda _, *refs: join_kernel(*refs)
    first = () if after is None else (after,)
    return call(kernel, "join", [array(parts[0].shape[0], width)], *first, *parts, scalars=0)[0]


def mate_kernel(mine, pick, out):
    half = mine.shape[1]
    for c in range(0, 2 * half, TILE):
        out[:, c : c + TILE] = dot(mine[...], pick[:half, c : c + TILE])


def expand_kernel(devices, place, mine, theirs, mates, pick, coef, near, far, out, near_pair, far_pair):
    half = mine.shape[1]
    mask = mask_of(place, devices, 2 * half)
    for q, (direct, pair) in enumerate(((mine, near_pair), (theirs, far_pair))):
        for c in range(0, half, TILE):
            k = q * half + c
            here = slice(k, k + TILE)
            across = mates[:, here] + dot(theirs[...], pick[half:, here])
            mixed = coef[0:1, here] * direct[:, c : c + TILE].astype(F32) + coef[1:2, here] * across
            for d in range(0, TILE, LANES):
                pair[:, block((mask ^ (k + d)) & (half - 1), LANES)] = mixed[:, d : d + LANES].astype(BF)
    rows = out.shape[0]
    for r in range(0, rows, TILE):
        total = dot(near[r : r + TILE, :], near_pair[...], NT) + dot(far[r : r + TILE, :], far_pair[...], NT)
        out[r : r + TILE, :] = total.astype(BF)


def swap(x, devices, bits, odd=None):
    odd = bits if odd is None else odd
    return lax.ppermute(x, "frdm", [(i, i ^ (odd if i & 1 else bits)) for i in range(devices)])


def shards(devices, loads, shapes, mode_order, partner, taps, offsets, coef):
    rows, modes = shapes.shape
    hist, count = loads.shape[1], taps.shape[1]
    half, quarter = modes // 2, modes // 4
    place = lax.axis_index("frdm").astype(I32).reshape(1)
    forward = forward_table(hist)
    tap_forward, last = tap_table(hist, count)
    phase = phase_table(hist, hist - W - count + 1)
    inverse = inverse_table(hist, count)
    order, mates, offsets, taps = mode_order[None], partner[None], offsets[None], taps.T

    sent, lft, far, stack, coef_near = call(
        project_kernel, "project",
        [near(hist + EXTRA, quarter), near(hist, rows), near(rows, half), near(count - 1 + EXTRA, modes), near(*coef.shape)],
        place, loads, forward, shapes, taps, offsets, coef, far=range(1, 7),
        scratch=[
            pltpu.VMEM(loads.shape, BF), pltpu.VMEM(forward.shape, BF), pltpu.VMEM(taps.shape, F32),
            pltpu.VMEM(offsets.shape, I32), pltpu.SemaphoreType.DMA((7,)),
        ],
        limit=24,
    )
    got = swap(sent, devices, 1)
    spec, shapes, *held = call(
        spectrum_kernel, "spectrum",
        [near(hist, quarter, dtype=F32), near(rows, half)] + [near(*t.shape) for t in (tap_forward, last, phase, inverse)],
        place, stack, order, shapes, tap_forward, last, phase, inverse, far=range(3, 8),
        scratch=[pltpu.SemaphoreType.DMA((5,))],
    )
    inverse = held.pop()

    def respond(which, got, spec, out):
        kernel = functools.partial(respond_kernel, which)
        return call(kernel, "respond", [out], place, lft, shapes, got, spec, inverse, coef_near)[0]

    away = respond(1, got, spec, array(W + EXTRA, quarter))
    sent = call(project_rest_kernel, "project_rest", [array(hist, quarter)], place, lft, far, away, products=4 * hist * rows * quarter)[0]
    rest = swap(sent, devices, 1)
    spec = call(
        spectrum_rest_kernel, "spectrum_rest", [array(hist, quarter, dtype=F32)], place, stack, order, *held, away, products=10**10
    )[0]
    own = respond(0, rest, spec, array(W, quarter, dtype=F32))

    def pair(after):
        kernel = functools.partial(pick_kernel, devices)
        return call(kernel, "pick", [near(modes, modes)], place, mates, after)[0]

    if devices == 16:
        size = modes // devices
        away = swap(away, devices, 2)
        keep, known, *parts = call(
            fold_kernel, "fold", [array(W, size, dtype=F32), array(EXTRA, LANES)] + [array(W + EXTRA, size)] * 3,
            place, own, away, coef_near, got,
        )
        ways = zip(turns_of(0), turns_of(1))
        parts = [swap(part, devices, 4 * even, 4 * odd) for part, (even, odd) in zip(parts, ways)]
        total = call(settle_kernel, "settle", [array(W, size)], keep, *parts, scalars=0)[0]
        spread = [swap(total, devices, 4 * d) for d in (1, 2, 3)]
        resp = join(total, *spread)
        mode_coef = call(
            mixers_kernel, "mixers", [array(8, modes, dtype=F32)],
            place, order, known, *parts, resp, scratch=[pltpu.VMEM((8, modes), F32)],
        )[0]
        pick = pair(mode_coef)
        mine = join(resp, swap(resp, devices, 2), after=pick)
    else:
        pick = pair(mates)
        mode_coef = call(
            functools.partial(plain_mixers_kernel, devices), "mixers", [array(8, modes, dtype=F32)],
            place, order, lax.all_gather(coef, "frdm", axis=1, tiled=True), scratch=[pltpu.VMEM((8, modes), F32)],
        )[0]
        away = away[:W].astype(F32)
        resp = jnp.where(place[0] & 2, jnp.concatenate([away, own], axis=1), jnp.concatenate([own, away], axis=1))
        groups = [list(range(c, devices, 2)) for c in range(2)]
        mine = lax.psum(resp, "frdm", axis_index_groups=groups).astype(BF)
    theirs = swap(mine, devices, 1)
    first = call(mate_kernel, "mate", [array(W, modes, dtype=F32)], mine, pick, scalars=0)[0]
    return call(
        functools.partial(expand_kernel, devices), "expand", [array(rows, W)],
        place, mine, theirs, first, pick, mode_coef, shapes, far,
        scratch=[pltpu.VMEM((W, half), BF)] * 2,
    )[0]


def solution(mesh):
    in_specs = (P(("cases", "frdm"), None), P("frdm", None), P(), P(), P(), P(), P(None, "frdm"))
    out_specs = P(("cases", "frdm"), None)
    body = functools.partial(shards, mesh.shape["frdm"])
    return jax.shard_map(body, mesh=mesh, in_specs=in_specs, out_specs=out_specs, check_vma=False)
```

```python
import functools

import jax
import jax.numpy as jnp
import numpy as np
from jax import lax
from jax.experimental import pallas as pl
from jax.experimental.pallas import tpu as pltpu
from jax.sharding import PartitionSpec as P

W = 256
LANES = 128
TILE = 512
EXTRA = 16
BF = jnp.bfloat16
F32 = jnp.float32
I32 = jnp.int32
NT = (((1,), (1,)), ((), ()))
NN = (((1,), (0,)), ((), ()))


def dot(a, b, dims=NN):
    return lax.dot_general(a, b, dims, preferred_element_type=F32)


def split(table):
    high = table.astype(BF)
    low = (table - high.astype(np.float64)).astype(BF)
    return high, low


def turns(half, n):
    odd = 2 * np.arange(half)[:, None] + 1
    angle = (odd * n[None, :]) % (4 * half) * (np.pi / (2 * half))
    return np.cos(angle), np.sin(angle)


def forward_table(hist):
    cos, sin = turns(hist // 2, np.arange(hist))
    return np.concatenate([cos, -sin]).astype(BF)


def tap_table(hist, taps):
    cos, sin = turns(hist // 2, np.arange(taps))
    table = np.concatenate([cos, -sin])
    last = np.repeat(table[:, -1:], LANES, axis=1).astype(BF)
    return np.concatenate(split(table[:, :-1]), axis=1), last


def phase_table(hist, delay):
    cos, sin = turns(hist // 2, np.arange(1, delay + 1))
    return np.concatenate(split(np.concatenate([cos - 1.0, sin])), axis=1)


def inverse_table(hist, taps):
    cos, sin = turns(hist // 2, np.arange(W) + taps - 1)
    return np.concatenate(split(np.concatenate([cos, -sin]).T * (2.0 / hist)), axis=1)


def call(kernel, name, out_shape, *args, scalars=1, far=(), scratch=(), limit=16, products=0):
    vmem = pl.BlockSpec(memory_space=pltpu.VMEM)
    smem = pl.BlockSpec(memory_space=pltpu.SMEM)
    hbm = pl.BlockSpec(memory_space=pltpu.HBM)
    places = [smem] * scalars + [vmem] * (len(args) - scalars)
    args = list(args)
    for i in far:
        places[i] = hbm
        args[i] = pltpu.with_memory_space_constraint(jnp.asarray(args[i]), pltpu.HBM)
    return pl.pallas_call(
        kernel,
        in_specs=places,
        out_specs=[vmem] * len(out_shape),
        out_shape=out_shape,
        scratch_shapes=list(scratch),
        cost_estimate=pl.CostEstimate(flops=2 * products, bytes_accessed=0, transcendentals=0) if products else None,
        compiler_params=pltpu.CompilerParams(vmem_limit_bytes=limit * 1024 * 1024),
        name=name,
    )(*args)


def array(*shape, dtype=BF):
    return jax.ShapeDtypeStruct(shape, dtype)


def near(*shape, dtype=BF):
    return pltpu.VMEM(shape, dtype)


def block(start, size):
    return pl.ds(pl.multiple_of(start, LANES), size)


def hot(mask):
    return mask.astype(F32).astype(BF)


def fetch(pairs, sems):
    return [pltpu.make_async_copy(a, b, sems.at[i]) for i, (a, b) in enumerate(pairs)]


def project_kernel(
    place, loads_far, forward_far, shapes_far, taps_far, offsets_far, coef_far,
    sent, lft, shapes, stack, coef, loads, forward, taps, offsets, sems,
):
    rows, half = shapes.shape
    hist, width = lft.shape[0], sent.shape[1]
    start, later = quarter_start(place, 1, 2 * half), quarter_start(place, 0, 2 * half)
    base = (1 - (place[0] & 1)) * half
    step = TILE
    top, left = slice(0, hist // 2), slice(0, step)
    low, right = slice(hist // 2, hist), slice(step, rows)
    pairs = [
        (forward_far.at[top, :], forward.at[top, :]),
        (loads_far.at[left, :], loads.at[left, :]),
        (loads_far.at[right, :], loads.at[right, :]),
        (forward_far.at[low, :], forward.at[low, :]),
    ]
    first = len(pairs)
    pairs += [
        (coef_far, coef),
        (offsets_far, offsets),
        (shapes_far.at[:, block(base + start, width)], shapes.at[:, block(start, width)]),
        (taps_far, taps),
        (shapes_far.at[:, block(base + later, width)], shapes.at[:, block(later, width)]),
    ]
    copies = fetch(pairs, sems)
    for copy in copies[:first]:
        copy.start()
    copies[0].wait()
    copies[1].wait()
    lft[top, left] = dot(forward[top, :], loads[left, :], NT).astype(BF)
    copies[2].wait()
    for copy in copies[first:]:
        copy.start()
    lft[top, right] = dot(forward[top, :], loads[right, :], NT).astype(BF)
    copies[3].wait()
    for part in (left, right):
        lft[low, part] = dot(forward[low, :], loads[part, :], NT).astype(BF)
    for copy in copies[first : first + 3]:
        copy.wait()
    count = taps.shape[0] - 1
    for c in range(0, width, step):
        sent[:hist, c : c + step] = dot(lft[...], shapes[:, block(start + c, step)]).astype(BF)
    sent[hist:, :] = jnp.zeros((EXTRA, width), BF)
    sent[hist : hist + 2, : coef.shape[1]] = coef[...]
    copies[first + 3].wait()
    for r in range(0, count, 64):
        stack[r : r + 64, :] = taps[r : r + 64, :].astype(BF)
    index = lax.broadcasted_iota(I32, (EXTRA, taps.shape[1]), 0)
    end = taps[count : count + 1, :]
    tail = jnp.where(index == 0, end, jnp.where(index == 1, offsets[...].astype(F32), 0.0))
    stack[count:, :] = tail.astype(BF)
    copies[first + 4].wait()


def project_rest_kernel(place, lft, shapes, after, sent):
    width = sent.shape[1]
    later = quarter_start(place, 0, 4 * width)
    for c in range(0, width, TILE):
        sent[:, c : c + TILE] = dot(lft[...], shapes[:, block(later + c, TILE)]).astype(BF)


def quarter_start(place, which, modes):
    return (((place[0] >> 1) & 1) ^ which) * (modes // 4)


def gather_taps(base, stack, order):
    count = stack.shape[0] - EXTRA
    mode = lax.broadcasted_iota(I32, (TILE, stack.shape[1]), 0) + base
    picked = dot(stack[...], hot(mode == order[...]), NT)
    tail = picked[count:]
    return picked[:count].astype(BF), tail[0:1], tail[1:2].astype(I32)


def spectrum_of(main, end, offset, table, last, phase):
    half = table.shape[0] // 2
    delay = phase.shape[1] // 2
    resp = dot(table[...], jnp.concatenate([main, main], axis=0))
    resp = resp + jnp.tile(last[...].astype(F32), (1, TILE // LANES)) * end
    which = hot(lax.broadcasted_iota(I32, (delay, TILE), 0) + 1 == offset)
    turn = dot(phase[...], jnp.concatenate([which, which], axis=0))
    cos, sin = turn[:half] + 1.0, turn[half:]
    re, im = resp[:half], resp[half:]
    return cos * re - sin * im, sin * re + cos * im


def spectrum_tiles(base, stack, order, table, last, phase, spec):
    half = spec.shape[0] // 2
    for c in range(0, spec.shape[1], TILE):
        parts = spectrum_of(*gather_taps(base + c, stack, order), table, last, phase)
        spec[:half, c : c + TILE], spec[half:, c : c + TILE] = parts


def spectrum_kernel(
    place, stack, order, shapes_far, table_far, last_far, phase_far, inverse_far,
    spec, shapes, table, last, phase, inverse, sems,
):
    half, modes = shapes.shape[1], shapes_far.shape[1]
    near = (place[0] & 1) * half
    copies = fetch(
        [
            (table_far, table),
            (last_far, last),
            (phase_far, phase),
            (shapes_far.at[:, block(near, half)], shapes),
            (inverse_far, inverse),
        ],
        sems,
    )
    for copy in copies:
        copy.start()
    width = spec.shape[1]
    start = near + quarter_start(place, 1, modes)
    tiles = range(0, width, TILE)
    picked = [gather_taps(start + c, stack, order) for c in tiles]
    for copy in copies[:3]:
        copy.wait()
    top = spec.shape[0] // 2
    for c, parts in zip(tiles, picked):
        spec[:top, c : c + TILE], spec[top:, c : c + TILE] = spectrum_of(*parts, table, last, phase)
    for copy in copies[3:]:
        copy.wait()


def spectrum_rest_kernel(place, stack, order, table, last, phase, after, spec):
    modes = order.shape[1]
    start = (place[0] & 1) * (modes // 2) + quarter_start(place, 0, modes)
    spectrum_tiles(start, stack, order, table, last, phase, spec)


def impose(total, tre, tim, inverse):
    half = tre.shape[0]
    re, im = total[:half], total[half:]
    product = jnp.concatenate([re * tre - im * tim, re * tim + im * tre], axis=0)
    high = product.astype(BF)
    low = (product - high.astype(F32)).astype(BF)
    both = dot(inverse[...], jnp.concatenate([high, high], axis=0))
    return both + dot(inverse[:, : 2 * half], low)


def respond_kernel(which, place, lft, shapes, other, spec, inverse, coef, out):
    hist, width = spec.shape
    half = hist // 2
    start = quarter_start(place, which, 4 * width)
    for c in range(0, width, TILE):
        total = dot(lft[...], shapes[:, block(start + c, TILE)]) + other[:hist, c : c + TILE].astype(F32)
        result = impose(total, spec[:half, c : c + TILE], spec[half:, c : c + TILE], inverse)
        out[:W, c : c + TILE] = result.astype(out.dtype)
    if out.shape[0] > W:
        out[W:, :] = jnp.zeros((EXTRA, width), BF)
        out[W : W + 2, : coef.shape[1]] = coef[...]
        out[W + 2 : W + 4, :LANES] = other[hist : hist + 2, :LANES]


def turns_of(core):
    return 3 - 2 * core, 2, 1 + 2 * core


def fold_kernel(place, own, got, coef, other, keep, known, first, second, third):
    z = place[0] >> 2
    size = keep.shape[1]
    hist = other.shape[0] - EXTRA
    known[...] = jnp.zeros(known.shape, BF)
    known[0:2, :] = coef[...]
    known[2:4, :] = other[hist : hist + 2, :LANES]
    known[4:8, :] = got[W : W + 4, :LANES]
    for d, out in zip((0, *turns_of(place[0] & 1)), (keep, first, second, third)):
        where = block((z ^ d) * size, size)
        total = own[:, where] + got[:W, where].astype(F32)
        out[:W, :] = total.astype(out.dtype)
        if out.shape[0] > W:
            out[W:, :] = known[...]


def settle_kernel(keep, first, second, third, out):
    total = keep[...]
    for got in (first, second, third):
        total = total + got[:W, :].astype(F32)
    out[...] = total.astype(BF)


def mask_of(place, devices, modes):
    me = place[0]
    if devices == 16:
        return ((me & 1) * 8 + (me & 2) * 2 + (me >> 2)) * (modes // 16)
    return (me & 1) * (modes // 2)


def pick_kernel(devices, place, partner, after, pick):
    modes = partner.shape[1]
    mask = mask_of(place, devices, modes)
    mates = [partner[:, block(c ^ mask, LANES)] ^ mask for c in range(0, modes, LANES)]
    mates = jnp.concatenate(mates, axis=1)
    for c in range(0, modes, 256):
        pick[c : c + 256, :] = hot(lax.broadcasted_iota(I32, (256, modes), 0) + c == mates)


def mixers_kernel(place, order, known, first, second, third, after, coef, held):
    me = place[0]
    held[...] = jnp.zeros(held.shape, F32)
    for z, rows in zip((0, *turns_of(me & 1)), (known, first, second, third)):
        top = rows.shape[0] - EXTRA
        for low in range(4):
            where = block((me ^ (4 * z + low)) * LANES, LANES)
            held[0:2, where] = rows[top : top + EXTRA, :].astype(F32)[2 * low : 2 * low + 2]
    mixers(order, mask_of(place, 16, order.shape[1]), held, coef)


def mixers(order, mask, held, coef):
    modes = order.shape[1]
    table = held[...].astype(BF)
    slots = order[...] ^ mask
    for c in range(0, modes, TILE):
        coef[:, c : c + TILE] = dot(table, hot(lax.broadcasted_iota(I32, (TILE, modes), 0) + c == slots), NT)


def plain_mixers_kernel(devices, place, order, every, coef, held):
    held[...] = jnp.zeros(held.shape, F32)
    held[0:2, :] = every[...].astype(F32)
    mixers(order, mask_of(place, devices, order.shape[1]), held, coef)


def line_kernel(place, total, first, second, third, out):
    size = total.shape[1]
    for d, part in zip((0, *turns_of(place[0] & 1)), (total, first, second, third)):
        out[:, block(d * size, size)] = part[...]


def join_kernel(*refs):
    *parts, out = refs
    start = 0
    for part in parts:
        out[:, start : start + part.shape[1]] = part[...]
        start += part.shape[1]


def join(*parts, after=None):
    width = sum(part.shape[1] for part in parts)
    kernel = join_kernel if after is None else lambda _, *refs: join_kernel(*refs)
    first = () if after is None else (after,)
    return call(kernel, "join", [array(parts[0].shape[0], width)], *first, *parts, scalars=0)[0]


def mate_kernel(mine, pick, out):
    half = mine.shape[1]
    for c in range(0, 2 * half, TILE):
        out[:, c : c + TILE] = dot(mine[...], pick[:half, c : c + TILE])


def expand_kernel(devices, place, mine, theirs, mates, pick, coef, near, far, out, near_pair, far_pair):
    half = mine.shape[1]
    mask = mask_of(place, devices, 2 * half)
    for q, (direct, pair) in enumerate(((mine, near_pair), (theirs, far_pair))):
        for c in range(0, half, TILE):
            k = q * half + c
            here = slice(k, k + TILE)
            across = mates[:, here] + dot(theirs[...], pick[half:, here])
            mixed = coef[0:1, here] * direct[:, c : c + TILE].astype(F32) + coef[1:2, here] * across
            for d in range(0, TILE, LANES):
                pair[:, block((mask ^ (k + d)) & (half - 1), LANES)] = mixed[:, d : d + LANES].astype(BF)
    rows = out.shape[0]
    for r in range(0, rows, TILE):
        total = dot(near[r : r + TILE, :], near_pair[...], NT) + dot(far[r : r + TILE, :], far_pair[...], NT)
        out[r : r + TILE, :] = total.astype(BF)


def swap(x, devices, bits, odd=None):
    odd = bits if odd is None else odd
    return lax.ppermute(x, "frdm", [(i, i ^ (odd if i & 1 else bits)) for i in range(devices)])


def shards(devices, loads, shapes, mode_order, partner, taps, offsets, coef):
    rows, modes = shapes.shape
    hist, count = loads.shape[1], taps.shape[1]
    half, quarter = modes // 2, modes // 4
    place = lax.axis_index("frdm").astype(I32).reshape(1)
    forward = forward_table(hist)
    tap_forward, last = tap_table(hist, count)
    phase = phase_table(hist, hist - W - count + 1)
    inverse = inverse_table(hist, count)
    order, mates, offsets, taps = mode_order[None], partner[None], offsets[None], taps.T

    sent, lft, far, stack, coef_near = call(
        project_kernel, "project",
        [near(hist + EXTRA, quarter), near(hist, rows), near(rows, half), near(count - 1 + EXTRA, modes), near(*coef.shape)],
        place, loads, forward, shapes, taps, offsets, coef, far=range(1, 7),
        scratch=[
            pltpu.VMEM(loads.shape, BF), pltpu.VMEM(forward.shape, BF), pltpu.VMEM(taps.shape, F32),
            pltpu.VMEM(offsets.shape, I32), pltpu.SemaphoreType.DMA((9,)),
        ],
        limit=24,
    )
    got = swap(sent, devices, 1)
    spec, shapes, *held = call(
        spectrum_kernel, "spectrum",
        [near(hist, quarter, dtype=F32), near(rows, half)] + [near(*t.shape) for t in (tap_forward, last, phase, inverse)],
        place, stack, order, shapes, tap_forward, last, phase, inverse, far=range(3, 8),
        scratch=[pltpu.SemaphoreType.DMA((5,))],
    )
    inverse = held.pop()

    def respond(which, got, spec, out):
        kernel = functools.partial(respond_kernel, which)
        return call(kernel, "respond", [out], place, lft, shapes, got, spec, inverse, coef_near)[0]

    away = respond(1, got, spec, array(W + EXTRA, quarter))
    sent = call(project_rest_kernel, "project_rest", [array(hist, quarter)], place, lft, far, away, products=4 * hist * rows * quarter)[0]
    rest = swap(sent, devices, 1)
    spec = call(
        spectrum_rest_kernel, "spectrum_rest", [array(hist, quarter, dtype=F32)], place, stack, order, *held, away, products=10**10
    )[0]
    own = respond(0, rest, spec, array(W, quarter, dtype=F32))

    def pair(after):
        kernel = functools.partial(pick_kernel, devices)
        return call(kernel, "pick", [near(modes, modes)], place, mates, after)[0]

    if devices == 16:
        size = modes // devices
        away = swap(away, devices, 2)
        keep, known, *parts = call(
            fold_kernel, "fold", [array(W, size, dtype=F32), array(EXTRA, LANES)] + [array(W + EXTRA, size)] * 3,
            place, own, away, coef_near, got,
        )
        ways = zip(turns_of(0), turns_of(1))
        parts = [swap(part, devices, 4 * even, 4 * odd) for part, (even, odd) in zip(parts, ways)]
        total = call(settle_kernel, "settle", [array(W, size)], keep, *parts, scalars=0)[0]
        spread = [swap(total, devices, 4 * even, 4 * odd) for even, odd in reversed(list(zip(turns_of(0), turns_of(1))))]
        resp = call(line_kernel, "line", [array(W, quarter)], place, total, *reversed(spread))[0]
        mode_coef = call(
            mixers_kernel, "mixers", [array(8, modes, dtype=F32)],
            place, order, known, *parts, resp, scratch=[pltpu.VMEM((8, modes), F32)],
        )[0]
        pick = pair(mode_coef)
        mine = join(resp, swap(resp, devices, 2), after=pick)
    else:
        pick = pair(mates)
        mode_coef = call(
            functools.partial(plain_mixers_kernel, devices), "mixers", [array(8, modes, dtype=F32)],
            place, order, lax.all_gather(coef, "frdm", axis=1, tiled=True), scratch=[pltpu.VMEM((8, modes), F32)],
        )[0]
        away = away[:W].astype(F32)
        resp = jnp.where(place[0] & 2, jnp.concatenate([away, own], axis=1), jnp.concatenate([own, away], axis=1))
        groups = [list(range(c, devices, 2)) for c in range(2)]
        mine = lax.psum(resp, "frdm", axis_index_groups=groups).astype(BF)
    theirs = swap(mine, devices, 1)
    first = call(mate_kernel, "mate", [array(W, modes, dtype=F32)], mine, pick, scalars=0)[0]
    return call(
        functools.partial(expand_kernel, devices), "expand", [array(rows, W)],
        place, mine, theirs, first, pick, mode_coef, shapes, far,
        scratch=[pltpu.VMEM((W, half), BF)] * 2,
    )[0]


def solution(mesh):
    in_specs = (P(("cases", "frdm"), None), P("frdm", None), P(), P(), P(), P(), P(None, "frdm"))
    out_specs = P(("cases", "frdm"), None)
    body = functools.partial(shards, mesh.shape["frdm"])
    return jax.shard_map(body, mesh=mesh, in_specs=in_specs, out_specs=out_specs, check_vma=False)
```

```python
import functools

import jax
import jax.numpy as jnp
import numpy as np
from jax import lax
from jax.experimental import pallas as pl
from jax.experimental.pallas import tpu as pltpu
from jax.sharding import PartitionSpec as P

W = 256
LANES = 128
TILE = 512
EXTRA = 16
BF = jnp.bfloat16
F32 = jnp.float32
I32 = jnp.int32
NT = (((1,), (1,)), ((), ()))
NN = (((1,), (0,)), ((), ()))


def dot(a, b, dims=NN):
    return lax.dot_general(a, b, dims, preferred_element_type=F32)


def split(table):
    high = table.astype(BF)
    low = (table - high.astype(np.float64)).astype(BF)
    return high, low


def turns(half, n):
    odd = 2 * np.arange(half)[:, None] + 1
    angle = (odd * n[None, :]) % (4 * half) * (np.pi / (2 * half))
    return np.cos(angle), np.sin(angle)


def forward_table(hist):
    cos, sin = turns(hist // 2, np.arange(hist))
    return np.concatenate([cos, -sin]).astype(BF)


def tap_table(hist, taps):
    cos, sin = turns(hist // 2, np.arange(taps))
    table = np.concatenate([cos, -sin])
    last = np.repeat(table[:, -1:], LANES, axis=1).astype(BF)
    return np.concatenate(split(table[:, :-1]), axis=1), last


def phase_table(hist, delay):
    cos, sin = turns(hist // 2, np.arange(1, delay + 1))
    return np.concatenate(split(np.concatenate([cos - 1.0, sin])), axis=1)


def inverse_table(hist, taps):
    cos, sin = turns(hist // 2, np.arange(W) + taps - 1)
    return np.concatenate(split(np.concatenate([cos, -sin]).T * (2.0 / hist)), axis=1)


def call(kernel, name, out_shape, *args, scalars=1, far=(), scratch=(), limit=16, products=0):
    vmem = pl.BlockSpec(memory_space=pltpu.VMEM)
    smem = pl.BlockSpec(memory_space=pltpu.SMEM)
    hbm = pl.BlockSpec(memory_space=pltpu.HBM)
    places = [smem] * scalars + [vmem] * (len(args) - scalars)
    args = list(args)
    for i in far:
        places[i] = hbm
        args[i] = pltpu.with_memory_space_constraint(jnp.asarray(args[i]), pltpu.HBM)
    return pl.pallas_call(
        kernel,
        in_specs=places,
        out_specs=[vmem] * len(out_shape),
        out_shape=out_shape,
        scratch_shapes=list(scratch),
        cost_estimate=pl.CostEstimate(flops=2 * products, bytes_accessed=0, transcendentals=0) if products else None,
        compiler_params=pltpu.CompilerParams(vmem_limit_bytes=limit * 1024 * 1024),
        name=name,
    )(*args)


def array(*shape, dtype=BF):
    return jax.ShapeDtypeStruct(shape, dtype)


def near(*shape, dtype=BF):
    return pltpu.VMEM(shape, dtype)


def block(start, size):
    return pl.ds(pl.multiple_of(start, LANES), size)


def hot(mask):
    return mask.astype(F32).astype(BF)


def fetch(pairs, sems):
    return [pltpu.make_async_copy(a, b, sems.at[i]) for i, (a, b) in enumerate(pairs)]


def project_kernel(
    place, loads_far, forward_far, shapes_far, taps_far, offsets_far, coef_far,
    sent, lft, shapes, stack, coef, loads, forward, taps, offsets, sems,
):
    rows, half = shapes.shape
    hist, width = lft.shape[0], sent.shape[1]
    start, later = quarter_start(place, 1, 2 * half), quarter_start(place, 0, 2 * half)
    base = (1 - (place[0] & 1)) * half
    step = TILE
    top, left = slice(0, hist // 2), slice(0, step)
    low, right = slice(hist // 2, hist), slice(step, rows)
    pairs = [
        (forward_far.at[top, :], forward.at[top, :]),
        (loads_far.at[left, :], loads.at[left, :]),
        (loads_far.at[right, :], loads.at[right, :]),
        (forward_far.at[low, :], forward.at[low, :]),
    ]
    first = len(pairs)
    pairs += [
        (coef_far, coef),
        (offsets_far, offsets),
        (shapes_far.at[:, block(base + start, width)], shapes.at[:, block(start, width)]),
        (taps_far, taps),
        (shapes_far.at[:, block(base + later, width)], shapes.at[:, block(later, width)]),
    ]
    copies = fetch(pairs, sems)
    for copy in copies[:first]:
        copy.start()
    copies[0].wait()
    copies[1].wait()
    lft[top, left] = dot(forward[top, :], loads[left, :], NT).astype(BF)
    copies[2].wait()
    for copy in copies[first:]:
        copy.start()
    lft[top, right] = dot(forward[top, :], loads[right, :], NT).astype(BF)
    copies[3].wait()
    for part in (left, right):
        lft[low, part] = dot(forward[low, :], loads[part, :], NT).astype(BF)
    for copy in copies[first : first + 3]:
        copy.wait()
    count = taps.shape[0] - 1
    for c in range(0, width, step):
        sent[:hist, c : c + step] = dot(lft[...], shapes[:, block(start + c, step)]).astype(BF)
    sent[hist:, :] = jnp.zeros((EXTRA, width), BF)
    sent[hist : hist + 2, : coef.shape[1]] = coef[...]
    copies[first + 3].wait()
    for r in range(0, count, 64):
        stack[r : r + 64, :] = taps[r : r + 64, :].astype(BF)
    index = lax.broadcasted_iota(I32, (EXTRA, taps.shape[1]), 0)
    end = taps[count : count + 1, :]
    tail = jnp.where(index == 0, end, jnp.where(index == 1, offsets[...].astype(F32), 0.0))
    stack[count:, :] = tail.astype(BF)
    copies[first + 4].wait()


def project_rest_kernel(place, lft, shapes, after, sent):
    width = sent.shape[1]
    later = quarter_start(place, 0, 4 * width)
    for c in range(0, width, TILE):
        sent[:, c : c + TILE] = dot(lft[...], shapes[:, block(later + c, TILE)]).astype(BF)


def quarter_start(place, which, modes):
    return (((place[0] >> 1) & 1) ^ which) * (modes // 4)


def gather_taps(base, stack, order):
    count = stack.shape[0] - EXTRA
    mode = lax.broadcasted_iota(I32, (TILE, stack.shape[1]), 0) + base
    picked = dot(stack[...], hot(mode == order[...]), NT)
    tail = picked[count:]
    return picked[:count].astype(BF), tail[0:1], tail[1:2].astype(I32)


def spectrum_of(main, end, offset, table, last, phase):
    half = table.shape[0] // 2
    delay = phase.shape[1] // 2
    resp = dot(table[...], jnp.concatenate([main, main], axis=0))
    resp = resp + jnp.tile(last[...].astype(F32), (1, TILE // LANES)) * end
    which = hot(lax.broadcasted_iota(I32, (delay, TILE), 0) + 1 == offset)
    turn = dot(phase[...], jnp.concatenate([which, which], axis=0))
    cos, sin = turn[:half] + 1.0, turn[half:]
    re, im = resp[:half], resp[half:]
    return cos * re - sin * im, sin * re + cos * im


def spectrum_tiles(base, stack, order, table, last, phase, spec):
    half = spec.shape[0] // 2
    for c in range(0, spec.shape[1], TILE):
        parts = spectrum_of(*gather_taps(base + c, stack, order), table, last, phase)
        spec[:half, c : c + TILE], spec[half:, c : c + TILE] = parts


def spectrum_kernel(
    place, stack, order, shapes_far, table_far, last_far, phase_far, inverse_far,
    spec, shapes, table, last, phase, inverse, sems,
):
    half, modes = shapes.shape[1], shapes_far.shape[1]
    near = (place[0] & 1) * half
    copies = fetch(
        [
            (table_far, table),
            (last_far, last),
            (phase_far, phase),
            (shapes_far.at[:, block(near, half)], shapes),
            (inverse_far, inverse),
        ],
        sems,
    )
    for copy in copies:
        copy.start()
    width = spec.shape[1]
    start = near + quarter_start(place, 1, modes)
    tiles = range(0, width, TILE)
    picked = [gather_taps(start + c, stack, order) for c in tiles]
    for copy in copies[:3]:
        copy.wait()
    top = spec.shape[0] // 2
    for c, parts in zip(tiles, picked):
        spec[:top, c : c + TILE], spec[top:, c : c + TILE] = spectrum_of(*parts, table, last, phase)
    for copy in copies[3:]:
        copy.wait()


def spectrum_rest_kernel(place, stack, order, table, last, phase, after, spec):
    modes = order.shape[1]
    start = (place[0] & 1) * (modes // 2) + quarter_start(place, 0, modes)
    spectrum_tiles(start, stack, order, table, last, phase, spec)


def impose(total, tre, tim, inverse):
    half = tre.shape[0]
    re, im = total[:half], total[half:]
    product = jnp.concatenate([re * tre - im * tim, re * tim + im * tre], axis=0)
    high = product.astype(BF)
    low = (product - high.astype(F32)).astype(BF)
    both = dot(inverse[...], jnp.concatenate([high, high], axis=0))
    return both + dot(inverse[:, : 2 * half], low)


def respond_kernel(which, place, lft, shapes, other, spec, inverse, coef, out):
    hist, width = spec.shape
    half = hist // 2
    start = quarter_start(place, which, 4 * width)
    for c in range(0, width, TILE):
        total = dot(lft[...], shapes[:, block(start + c, TILE)]) + other[:hist, c : c + TILE].astype(F32)
        result = impose(total, spec[:half, c : c + TILE], spec[half:, c : c + TILE], inverse)
        out[:W, c : c + TILE] = result.astype(out.dtype)
    if out.shape[0] > W:
        out[W:, :] = jnp.zeros((EXTRA, width), BF)
        out[W : W + 2, : coef.shape[1]] = coef[...]
        out[W + 2 : W + 4, :LANES] = other[hist : hist + 2, :LANES]


def turns_of(core):
    return 3 - 2 * core, 2, 1 + 2 * core


def fold_kernel(place, own, got, coef, other, keep, known, first, second, third):
    z = place[0] >> 2
    size = keep.shape[1]
    hist = other.shape[0] - EXTRA
    known[...] = jnp.zeros(known.shape, BF)
    known[0:2, :] = coef[...]
    known[2:4, :] = other[hist : hist + 2, :LANES]
    known[4:8, :] = got[W : W + 4, :LANES]
    for d, out in zip((0, *turns_of(place[0] & 1)), (keep, first, second, third)):
        where = block((z ^ d) * size, size)
        total = own[:, where] + got[:W, where].astype(F32)
        out[:W, :] = total.astype(out.dtype)
        if out.shape[0] > W:
            out[W:, :] = known[...]


def settle_kernel(keep, first, second, third, out):
    total = keep[...]
    for got in (first, second, third):
        total = total + got[:W, :].astype(F32)
    out[...] = total.astype(BF)


def mask_of(place, devices, modes):
    me = place[0]
    if devices == 16:
        return ((me & 1) * 8 + (me & 2) * 2 + (me >> 2)) * (modes // 16)
    return (me & 1) * (modes // 2)


def pick_kernel(devices, place, partner, after, pick):
    modes = partner.shape[1]
    mask = mask_of(place, devices, modes)
    mates = [partner[:, block(c ^ mask, LANES)] ^ mask for c in range(0, modes, LANES)]
    mates = jnp.concatenate(mates, axis=1)
    for c in range(0, modes, 256):
        pick[c : c + 256, :] = hot(lax.broadcasted_iota(I32, (256, modes), 0) + c == mates)


def mixers_kernel(place, order, known, first, second, third, after, coef, held):
    me = place[0]
    held[...] = jnp.zeros(held.shape, F32)
    for z, rows in zip((0, *turns_of(me & 1)), (known, first, second, third)):
        top = rows.shape[0] - EXTRA
        for low in range(4):
            where = block((me ^ (4 * z + low)) * LANES, LANES)
            held[0:2, where] = rows[top : top + EXTRA, :].astype(F32)[2 * low : 2 * low + 2]
    mixers(order, mask_of(place, 16, order.shape[1]), held, coef)


def mixers(order, mask, held, coef):
    modes = order.shape[1]
    table = held[...].astype(BF)
    slots = order[...] ^ mask
    for c in range(0, modes, TILE):
        coef[:, c : c + TILE] = dot(table, hot(lax.broadcasted_iota(I32, (TILE, modes), 0) + c == slots), NT)


def plain_mixers_kernel(devices, place, order, every, coef, held):
    held[...] = jnp.zeros(held.shape, F32)
    held[0:2, :] = every[...].astype(F32)
    mixers(order, mask_of(place, devices, order.shape[1]), held, coef)


def line_kernel(place, total, third, second, first, out):
    size = total.shape[1]
    for d, part in zip((0, *turns_of(place[0] & 1)), (total, first, second, third)):
        out[:, block(d * size, size)] = part[...]


def join_kernel(*refs):
    *parts, out = refs
    start = 0
    for part in parts:
        out[:, start : start + part.shape[1]] = part[...]
        start += part.shape[1]


def join(*parts, after=None):
    width = sum(part.shape[1] for part in parts)
    kernel = join_kernel if after is None else lambda _, *refs: join_kernel(*refs)
    first = () if after is None else (after,)
    return call(kernel, "join", [array(parts[0].shape[0], width)], *first, *parts, scalars=0)[0]


def mate_kernel(mine, pick, out):
    half = mine.shape[1]
    for c in range(0, 2 * half, TILE):
        out[:, c : c + TILE] = dot(mine[...], pick[:half, c : c + TILE])


def expand_kernel(devices, place, mine, theirs, mates, pick, coef, near, far, out, near_pair, far_pair):
    half = mine.shape[1]
    mask = mask_of(place, devices, 2 * half)
    for q, (direct, pair) in enumerate(((mine, near_pair), (theirs, far_pair))):
        for c in range(0, half, TILE):
            k = q * half + c
            here = slice(k, k + TILE)
            across = mates[:, here] + dot(theirs[...], pick[half:, here])
            mixed = coef[0:1, here] * direct[:, c : c + TILE].astype(F32) + coef[1:2, here] * across
            for d in range(0, TILE, LANES):
                pair[:, block((mask ^ (k + d)) & (half - 1), LANES)] = mixed[:, d : d + LANES].astype(BF)
    rows = out.shape[0]
    for r in range(0, rows, TILE):
        total = dot(near[r : r + TILE, :], near_pair[...], NT) + dot(far[r : r + TILE, :], far_pair[...], NT)
        out[r : r + TILE, :] = total.astype(BF)


def swap(x, devices, bits, odd=None):
    odd = bits if odd is None else odd
    return lax.ppermute(x, "frdm", [(i, i ^ (odd if i & 1 else bits)) for i in range(devices)])


def shards(devices, loads, shapes, mode_order, partner, taps, offsets, coef):
    rows, modes = shapes.shape
    hist, count = loads.shape[1], taps.shape[1]
    half, quarter = modes // 2, modes // 4
    place = lax.axis_index("frdm").astype(I32).reshape(1)
    forward = forward_table(hist)
    tap_forward, last = tap_table(hist, count)
    phase = phase_table(hist, hist - W - count + 1)
    inverse = inverse_table(hist, count)
    order, mates, offsets, taps = mode_order[None], partner[None], offsets[None], taps.T

    sent, lft, far, stack, coef_near = call(
        project_kernel, "project",
        [near(hist + EXTRA, quarter), near(hist, rows), near(rows, half), near(count - 1 + EXTRA, modes), near(*coef.shape)],
        place, loads, forward, shapes, taps, offsets, coef, far=range(1, 7),
        scratch=[
            pltpu.VMEM(loads.shape, BF), pltpu.VMEM(forward.shape, BF), pltpu.VMEM(taps.shape, F32),
            pltpu.VMEM(offsets.shape, I32), pltpu.SemaphoreType.DMA((9,)),
        ],
        limit=24,
    )
    got = swap(sent, devices, 1)
    spec, shapes, *held = call(
        spectrum_kernel, "spectrum",
        [near(hist, quarter, dtype=F32), near(rows, half)] + [near(*t.shape) for t in (tap_forward, last, phase, inverse)],
        place, stack, order, shapes, tap_forward, last, phase, inverse, far=range(3, 8),
        scratch=[pltpu.SemaphoreType.DMA((5,))],
    )
    inverse = held.pop()

    def respond(which, got, spec, out):
        kernel = functools.partial(respond_kernel, which)
        return call(kernel, "respond", [out], place, lft, shapes, got, spec, inverse, coef_near)[0]

    away = respond(1, got, spec, array(W + EXTRA, quarter))
    sent = call(project_rest_kernel, "project_rest", [array(hist, quarter)], place, lft, far, away, products=4 * hist * rows * quarter)[0]
    rest = swap(sent, devices, 1)
    spec = call(
        spectrum_rest_kernel, "spectrum_rest", [array(hist, quarter, dtype=F32)], place, stack, order, *held, away, products=10**10
    )[0]
    own = respond(0, rest, spec, array(W, quarter, dtype=F32))

    def pair(after):
        kernel = functools.partial(pick_kernel, devices)
        return call(kernel, "pick", [near(modes, modes)], place, mates, after)[0]

    if devices == 16:
        size = modes // devices
        away = swap(away, devices, 2)
        keep, known, *parts = call(
            fold_kernel, "fold", [array(W, size, dtype=F32), array(EXTRA, LANES)] + [array(W + EXTRA, size)] * 3,
            place, own, away, coef_near, got,
        )
        ways = zip(turns_of(0), turns_of(1))
        parts = [swap(part, devices, 4 * even, 4 * odd) for part, (even, odd) in zip(parts, ways)]
        total = call(settle_kernel, "settle", [array(W, size)], keep, *parts, scalars=0)[0]
        spread = [swap(total, devices, 4 * even, 4 * odd) for even, odd in zip(turns_of(0), turns_of(1))]
        resp = call(line_kernel, "line", [array(W, quarter)], place, total, *reversed(spread))[0]
        mode_coef = call(
            mixers_kernel, "mixers", [array(8, modes, dtype=F32)],
            place, order, known, *parts, resp, scratch=[pltpu.VMEM((8, modes), F32)],
        )[0]
        pick = pair(mode_coef)
        mine = join(resp, swap(resp, devices, 2), after=pick)
    else:
        pick = pair(mates)
        mode_coef = call(
            functools.partial(plain_mixers_kernel, devices), "mixers", [array(8, modes, dtype=F32)],
            place, order, lax.all_gather(coef, "frdm", axis=1, tiled=True), scratch=[pltpu.VMEM((8, modes), F32)],
        )[0]
        away = away[:W].astype(F32)
        resp = jnp.where(place[0] & 2, jnp.concatenate([away, own], axis=1), jnp.concatenate([own, away], axis=1))
        groups = [list(range(c, devices, 2)) for c in range(2)]
        mine = lax.psum(resp, "frdm", axis_index_groups=groups).astype(BF)
    theirs = swap(mine, devices, 1)
    first = call(mate_kernel, "mate", [array(W, modes, dtype=F32)], mine, pick, scalars=0)[0]
    return call(
        functools.partial(expand_kernel, devices), "expand", [array(rows, W)],
        place, mine, theirs, first, pick, mode_coef, shapes, far,
        scratch=[pltpu.VMEM((W, half), BF)] * 2,
    )[0]


def solution(mesh):
    in_specs = (P(("cases", "frdm"), None), P("frdm", None), P(), P(), P(), P(), P(None, "frdm"))
    out_specs = P(("cases", "frdm"), None)
    body = functools.partial(shards, mesh.shape["frdm"])
    return jax.shard_map(body, mesh=mesh, in_specs=in_specs, out_specs=out_specs, check_vma=False)
```

```python
import functools

import jax
import jax.numpy as jnp
import numpy as np
from jax import lax
from jax.experimental import pallas as pl
from jax.experimental.pallas import tpu as pltpu
from jax.sharding import PartitionSpec as P

W = 256
LANES = 128
TILE = 512
EXTRA = 16
BF = jnp.bfloat16
F32 = jnp.float32
I32 = jnp.int32
NT = (((1,), (1,)), ((), ()))
NN = (((1,), (0,)), ((), ()))


def dot(a, b, dims=NN):
    return lax.dot_general(a, b, dims, preferred_element_type=F32)


def split(table):
    high = table.astype(BF)
    low = (table - high.astype(np.float64)).astype(BF)
    return high, low


def turns(half, n):
    odd = 2 * np.arange(half)[:, None] + 1
    angle = (odd * n[None, :]) % (4 * half) * (np.pi / (2 * half))
    return np.cos(angle), np.sin(angle)


def forward_table(hist):
    cos, sin = turns(hist // 2, np.arange(hist))
    return np.concatenate([cos, -sin]).astype(BF)


def tap_table(hist, taps):
    cos, sin = turns(hist // 2, np.arange(taps))
    table = np.concatenate([cos, -sin])
    last = np.repeat(table[:, -1:], LANES, axis=1).astype(BF)
    return np.concatenate(split(table[:, :-1]), axis=1), last


def phase_table(hist, delay):
    cos, sin = turns(hist // 2, np.arange(1, delay + 1))
    return np.concatenate(split(np.concatenate([cos - 1.0, sin])), axis=1)


def inverse_table(hist, taps):
    cos, sin = turns(hist // 2, np.arange(W) + taps - 1)
    return np.concatenate(split(np.concatenate([cos, -sin]).T * (2.0 / hist)), axis=1)


def call(kernel, name, out_shape, *args, scalars=1, far=(), scratch=(), limit=16, products=0):
    vmem = pl.BlockSpec(memory_space=pltpu.VMEM)
    smem = pl.BlockSpec(memory_space=pltpu.SMEM)
    hbm = pl.BlockSpec(memory_space=pltpu.HBM)
    places = [smem] * scalars + [vmem] * (len(args) - scalars)
    args = list(args)
    for i in far:
        places[i] = hbm
        args[i] = pltpu.with_memory_space_constraint(jnp.asarray(args[i]), pltpu.HBM)
    return pl.pallas_call(
        kernel,
        in_specs=places,
        out_specs=[vmem] * len(out_shape),
        out_shape=out_shape,
        scratch_shapes=list(scratch),
        cost_estimate=pl.CostEstimate(flops=2 * products, bytes_accessed=0, transcendentals=0) if products else None,
        compiler_params=pltpu.CompilerParams(vmem_limit_bytes=limit * 1024 * 1024),
        name=name,
    )(*args)


def array(*shape, dtype=BF):
    return jax.ShapeDtypeStruct(shape, dtype)


def near(*shape, dtype=BF):
    return pltpu.VMEM(shape, dtype)


def block(start, size):
    return pl.ds(pl.multiple_of(start, LANES), size)


def hot(mask):
    return mask.astype(F32).astype(BF)


def fetch(pairs, sems):
    return [pltpu.make_async_copy(a, b, sems.at[i]) for i, (a, b) in enumerate(pairs)]


def project_kernel(
    place, loads_far, forward_far, shapes_far, taps_far, offsets_far, coef_far,
    sent, lft, shapes, stack, coef, loads, forward, taps, offsets, sems,
):
    rows, half = shapes.shape
    hist, width = lft.shape[0], sent.shape[1]
    start, later = quarter_start(place, 1, 2 * half), quarter_start(place, 0, 2 * half)
    base = (1 - (place[0] & 1)) * half
    step = TILE
    top, left = slice(0, hist // 2), slice(0, step)
    low, right = slice(hist // 2, hist), slice(step, rows)
    pairs = [
        (forward_far.at[top, :], forward.at[top, :]),
        (loads_far.at[left, :], loads.at[left, :]),
        (loads_far.at[right, :], loads.at[right, :]),
        (forward_far.at[low, :], forward.at[low, :]),
    ]
    first = len(pairs)
    pairs += [
        (coef_far, coef),
        (offsets_far, offsets),
        (shapes_far.at[:, block(base + start, width)], shapes.at[:, block(start, width)]),
        (taps_far, taps),
        (shapes_far.at[:, block(base + later, width)], shapes.at[:, block(later, width)]),
    ]
    copies = fetch(pairs, sems)
    for copy in copies[:first]:
        copy.start()
    copies[0].wait()
    copies[1].wait()
    lft[top, left] = dot(forward[top, :], loads[left, :], NT).astype(BF)
    copies[2].wait()
    for copy in copies[first:]:
        copy.start()
    lft[top, right] = dot(forward[top, :], loads[right, :], NT).astype(BF)
    copies[3].wait()
    for part in (left, right):
        lft[low, part] = dot(forward[low, :], loads[part, :], NT).astype(BF)
    for copy in copies[first : first + 3]:
        copy.wait()
    count = taps.shape[0] - 1
    for c in range(0, width, step):
        sent[:hist, c : c + step] = dot(lft[...], shapes[:, block(start + c, step)]).astype(BF)
    sent[hist:, :] = jnp.zeros((EXTRA, width), BF)
    sent[hist : hist + 2, : coef.shape[1]] = coef[...]
    copies[first + 3].wait()
    for r in range(0, count, 64):
        stack[r : r + 64, :] = taps[r : r + 64, :].astype(BF)
    index = lax.broadcasted_iota(I32, (EXTRA, taps.shape[1]), 0)
    end = taps[count : count + 1, :]
    tail = jnp.where(index == 0, end, jnp.where(index == 1, offsets[...].astype(F32), 0.0))
    stack[count:, :] = tail.astype(BF)
    copies[first + 4].wait()


def project_rest_kernel(place, lft, shapes, after, sent):
    width = sent.shape[1]
    later = quarter_start(place, 0, 4 * width)
    for c in range(0, width, TILE):
        sent[:, c : c + TILE] = dot(lft[...], shapes[:, block(later + c, TILE)]).astype(BF)


def quarter_start(place, which, modes):
    return (((place[0] >> 1) & 1) ^ which) * (modes // 4)


def gather_taps(base, stack, order):
    count = stack.shape[0] - EXTRA
    mode = lax.broadcasted_iota(I32, (TILE, stack.shape[1]), 0) + base
    picked = dot(stack[...], hot(mode == order[...]), NT)
    tail = picked[count:]
    return picked[:count].astype(BF), tail[0:1], tail[1:2].astype(I32)


def spectrum_of(main, end, offset, table, last, phase):
    half = table.shape[0] // 2
    delay = phase.shape[1] // 2
    resp = dot(table[...], jnp.concatenate([main, main], axis=0))
    resp = resp + jnp.tile(last[...].astype(F32), (1, TILE // LANES)) * end
    which = hot(lax.broadcasted_iota(I32, (delay, TILE), 0) + 1 == offset)
    turn = dot(phase[...], jnp.concatenate([which, which], axis=0))
    cos, sin = turn[:half] + 1.0, turn[half:]
    re, im = resp[:half], resp[half:]
    return cos * re - sin * im, sin * re + cos * im


def spectrum_tiles(base, stack, order, table, last, phase, spec):
    half = spec.shape[0] // 2
    for c in range(0, spec.shape[1], TILE):
        parts = spectrum_of(*gather_taps(base + c, stack, order), table, last, phase)
        spec[:half, c : c + TILE], spec[half:, c : c + TILE] = parts


def spectrum_kernel(
    place, stack, order, shapes_far, table_far, last_far, phase_far, inverse_far,
    spec, shapes, table, last, phase, inverse, sems,
):
    half, modes = shapes.shape[1], shapes_far.shape[1]
    near = (place[0] & 1) * half
    copies = fetch(
        [
            (table_far, table),
            (last_far, last),
            (phase_far, phase),
            (shapes_far.at[:, block(near, half)], shapes),
            (inverse_far, inverse),
        ],
        sems,
    )
    for copy in copies:
        copy.start()
    width = spec.shape[1]
    start = near + quarter_start(place, 1, modes)
    tiles = range(0, width, TILE)
    picked = [gather_taps(start + c, stack, order) for c in tiles]
    for copy in copies[:3]:
        copy.wait()
    top = spec.shape[0] // 2
    for c, parts in zip(tiles, picked):
        spec[:top, c : c + TILE], spec[top:, c : c + TILE] = spectrum_of(*parts, table, last, phase)
    for copy in copies[3:]:
        copy.wait()


def spectrum_rest_kernel(place, stack, order, table, last, phase, after, spec):
    modes = order.shape[1]
    start = (place[0] & 1) * (modes // 2) + quarter_start(place, 0, modes)
    spectrum_tiles(start, stack, order, table, last, phase, spec)


def impose(total, tre, tim, inverse):
    half = tre.shape[0]
    re, im = total[:half], total[half:]
    product = jnp.concatenate([re * tre - im * tim, re * tim + im * tre], axis=0)
    high = product.astype(BF)
    low = (product - high.astype(F32)).astype(BF)
    both = dot(inverse[...], jnp.concatenate([high, high], axis=0))
    return both + dot(inverse[:, : 2 * half], low)


def respond_kernel(which, place, lft, shapes, other, spec, inverse, coef, out):
    hist, width = spec.shape
    half = hist // 2
    start = quarter_start(place, which, 4 * width)
    for c in range(0, width, TILE):
        total = dot(lft[...], shapes[:, block(start + c, TILE)]) + other[:hist, c : c + TILE].astype(F32)
        result = impose(total, spec[:half, c : c + TILE], spec[half:, c : c + TILE], inverse)
        out[:W, c : c + TILE] = result.astype(out.dtype)
    if out.shape[0] > W:
        out[W:, :] = jnp.zeros((EXTRA, width), BF)
        out[W : W + 2, : coef.shape[1]] = coef[...]
        out[W + 2 : W + 4, :LANES] = other[hist : hist + 2, :LANES]


def turns_of(core):
    return 3 - 2 * core, 2, 1 + 2 * core


def fold_kernel(place, own, got, coef, other, keep, known, first, second, third):
    z = place[0] >> 2
    size = keep.shape[1]
    hist = other.shape[0] - EXTRA
    known[...] = jnp.zeros(known.shape, BF)
    known[0:2, :] = coef[...]
    known[2:4, :] = other[hist : hist + 2, :LANES]
    known[4:8, :] = got[W : W + 4, :LANES]
    for d, out in zip((0, *turns_of(place[0] & 1)), (keep, first, second, third)):
        where = block((z ^ d) * size, size)
        total = own[:, where] + got[:W, where].astype(F32)
        out[:W, :] = total.astype(out.dtype)
        if out.shape[0] > W:
            out[W:, :] = known[...]


def settle_kernel(keep, first, second, third, out):
    total = keep[...]
    for got in (first, second, third):
        total = total + got[:W, :].astype(F32)
    out[...] = total.astype(BF)


def mask_of(place, devices, modes):
    me = place[0]
    if devices == 16:
        return ((me & 1) * 8 + (me & 2) * 2 + (me >> 2)) * (modes // 16)
    return (me & 1) * (modes // 2)


def pick_kernel(devices, place, partner, after, pick):
    modes = partner.shape[1]
    mask = mask_of(place, devices, modes)
    mates = [partner[:, block(c ^ mask, LANES)] ^ mask for c in range(0, modes, LANES)]
    mates = jnp.concatenate(mates, axis=1)
    for c in range(0, modes, 256):
        pick[c : c + 256, :] = hot(lax.broadcasted_iota(I32, (256, modes), 0) + c == mates)


def mixers_kernel(place, order, known, first, second, third, after, coef, held):
    me = place[0]
    held[...] = jnp.zeros(held.shape, F32)
    for z, rows in zip((0, *turns_of(me & 1)), (known, first, second, third)):
        top = rows.shape[0] - EXTRA
        for low in range(4):
            where = block((me ^ (4 * z + low)) * LANES, LANES)
            held[0:2, where] = rows[top : top + EXTRA, :].astype(F32)[2 * low : 2 * low + 2]
    mixers(order, mask_of(place, 16, order.shape[1]), held, coef)


def mixers(order, mask, held, coef):
    modes = order.shape[1]
    table = held[...].astype(BF)
    slots = order[...] ^ mask
    for c in range(0, modes, TILE):
        coef[:, c : c + TILE] = dot(table, hot(lax.broadcasted_iota(I32, (TILE, modes), 0) + c == slots), NT)


def plain_mixers_kernel(devices, place, order, every, coef, held):
    held[...] = jnp.zeros(held.shape, F32)
    held[0:2, :] = every[...].astype(F32)
    mixers(order, mask_of(place, devices, order.shape[1]), held, coef)


def join_kernel(*refs):
    *parts, out = refs
    start = 0
    for part in parts:
        out[:, start : start + part.shape[1]] = part[...]
        start += part.shape[1]


def join(*parts, after=None):
    width = sum(part.shape[1] for part in parts)
    kernel = join_kernel if after is None else lambda _, *refs: join_kernel(*refs)
    first = () if after is None else (after,)
    return call(kernel, "join", [array(parts[0].shape[0], width)], *first, *parts, scalars=0)[0]


def mate_kernel(mine, pick, out):
    half = mine.shape[1]
    for c in range(0, 2 * half, TILE):
        out[:, c : c + TILE] = dot(mine[...], pick[:half, c : c + TILE])


def expand_kernel(devices, place, mine, theirs, mates, pick, coef, near, far, out, near_pair, far_pair):
    half = mine.shape[1]
    mask = mask_of(place, devices, 2 * half)
    for q, (direct, pair) in enumerate(((mine, near_pair), (theirs, far_pair))):
        for c in range(0, half, TILE):
            k = q * half + c
            here = slice(k, k + TILE)
            across = mates[:, here] + dot(theirs[...], pick[half:, here])
            mixed = coef[0:1, here] * direct[:, c : c + TILE].astype(F32) + coef[1:2, here] * across
            for d in range(0, TILE, LANES):
                pair[:, block((mask ^ (k + d)) & (half - 1), LANES)] = mixed[:, d : d + LANES].astype(BF)
    rows = out.shape[0]
    for r in range(0, rows, TILE):
        total = dot(near[r : r + TILE, :], near_pair[...], NT) + dot(far[r : r + TILE, :], far_pair[...], NT)
        out[r : r + TILE, :] = total.astype(BF)


def swap(x, devices, bits, odd=None):
    odd = bits if odd is None else odd
    return lax.ppermute(x, "frdm", [(i, i ^ (odd if i & 1 else bits)) for i in range(devices)])


def shards(devices, loads, shapes, mode_order, partner, taps, offsets, coef):
    rows, modes = shapes.shape
    hist, count = loads.shape[1], taps.shape[1]
    half, quarter = modes // 2, modes // 4
    place = lax.axis_index("frdm").astype(I32).reshape(1)
    forward = forward_table(hist)
    tap_forward, last = tap_table(hist, count)
    phase = phase_table(hist, hist - W - count + 1)
    inverse = inverse_table(hist, count)
    order, mates, offsets, taps = mode_order[None], partner[None], offsets[None], taps.T

    sent, lft, far, stack, coef_near = call(
        project_kernel, "project",
        [near(hist + EXTRA, quarter), near(hist, rows), near(rows, half), near(count - 1 + EXTRA, modes), near(*coef.shape)],
        place, loads, forward, shapes, taps, offsets, coef, far=range(1, 7),
        scratch=[
            pltpu.VMEM(loads.shape, BF), pltpu.VMEM(forward.shape, BF), pltpu.VMEM(taps.shape, F32),
            pltpu.VMEM(offsets.shape, I32), pltpu.SemaphoreType.DMA((9,)),
        ],
        limit=24,
    )
    got = swap(sent, devices, 1)
    spec, shapes, *held = call(
        spectrum_kernel, "spectrum",
        [near(hist, quarter, dtype=F32), near(rows, half)] + [near(*t.shape) for t in (tap_forward, last, phase, inverse)],
        place, stack, order, shapes, tap_forward, last, phase, inverse, far=range(3, 8),
        scratch=[pltpu.SemaphoreType.DMA((5,))],
    )
    inverse = held.pop()

    def respond(which, got, spec, out):
        kernel = functools.partial(respond_kernel, which)
        return call(kernel, "respond", [out], place, lft, shapes, got, spec, inverse, coef_near)[0]

    away = respond(1, got, spec, array(W + EXTRA, quarter))
    sent = call(project_rest_kernel, "project_rest", [array(hist, quarter)], place, lft, far, away, products=4 * hist * rows * quarter)[0]
    rest = swap(sent, devices, 1)
    spec = call(
        spectrum_rest_kernel, "spectrum_rest", [array(hist, quarter, dtype=F32)], place, stack, order, *held, away, products=10**10
    )[0]
    own = respond(0, rest, spec, array(W, quarter, dtype=F32))

    def pair(after):
        kernel = functools.partial(pick_kernel, devices)
        return call(kernel, "pick", [near(modes, modes)], place, mates, after)[0]

    if devices == 16:
        size = modes // devices
        away = swap(away, devices, 2)
        keep, known, *parts = call(
            fold_kernel, "fold", [array(W, size, dtype=F32), array(EXTRA, LANES)] + [array(W + EXTRA, size)] * 3,
            place, own, away, coef_near, got,
        )
        ways = zip(turns_of(0), turns_of(1))
        parts = [swap(part, devices, 4 * even, 4 * odd) for part, (even, odd) in zip(parts, ways)]
        total = call(settle_kernel, "settle", [array(W, size)], keep, *parts, scalars=0)[0]
        spread = [swap(total, devices, 4 * d) for d in (1, 2, 3)]
        resp = join(total, *spread)
        mode_coef = call(
            mixers_kernel, "mixers", [array(8, modes, dtype=F32)],
            place, order, known, *parts, resp, scratch=[pltpu.VMEM((8, modes), F32)],
        )[0]
        pick = pair(mode_coef)
        mine = join(resp, swap(resp, devices, 2), after=pick)
    else:
        pick = pair(mates)
        mode_coef = call(
            functools.partial(plain_mixers_kernel, devices), "mixers", [array(8, modes, dtype=F32)],
            place, order, lax.all_gather(coef, "frdm", axis=1, tiled=True), scratch=[pltpu.VMEM((8, modes), F32)],
        )[0]
        away = away[:W].astype(F32)
        resp = jnp.where(place[0] & 2, jnp.concatenate([away, own], axis=1), jnp.concatenate([own, away], axis=1))
        groups = [list(range(c, devices, 2)) for c in range(2)]
        mine = lax.psum(resp, "frdm", axis_index_groups=groups).astype(BF)
    theirs = swap(mine, devices, 1)
    first = call(mate_kernel, "mate", [array(W, modes, dtype=F32)], mine, pick, scalars=0)[0]
    return call(
        functools.partial(expand_kernel, devices), "expand", [array(rows, W)],
        place, mine, theirs, first, pick, mode_coef, shapes, far,
        scratch=[pltpu.VMEM((W, half), BF)] * 2,
    )[0]


def solution(mesh):
    in_specs = (P(("cases", "frdm"), None), P("frdm", None), P(), P(), P(), P(), P(None, "frdm"))
    out_specs = P(("cases", "frdm"), None)
    body = functools.partial(shards, mesh.shape["frdm"])
    return jax.shard_map(body, mesh=mesh, in_specs=in_specs, out_specs=out_specs, check_vma=False)
```

```python
import functools

import jax
import jax.numpy as jnp
import numpy as np
from jax import lax
from jax.experimental import pallas as pl
from jax.experimental.pallas import tpu as pltpu
from jax.sharding import PartitionSpec as P

W = 256
LANES = 128
TILE = 512
EXTRA = 16
BF = jnp.bfloat16
F32 = jnp.float32
I32 = jnp.int32
NT = (((1,), (1,)), ((), ()))
NN = (((1,), (0,)), ((), ()))


def dot(a, b, dims=NN):
    return lax.dot_general(a, b, dims, preferred_element_type=F32)


def split(table):
    high = table.astype(BF)
    low = (table - high.astype(np.float64)).astype(BF)
    return high, low


def turns(half, n):
    odd = 2 * np.arange(half)[:, None] + 1
    angle = (odd * n[None, :]) % (4 * half) * (np.pi / (2 * half))
    return np.cos(angle), np.sin(angle)


def forward_table(hist):
    cos, sin = turns(hist // 2, np.arange(hist))
    return np.concatenate([cos, -sin]).astype(BF)


def tap_table(hist, taps):
    cos, sin = turns(hist // 2, np.arange(taps))
    table = np.concatenate([cos, -sin])
    last = np.repeat(table[:, -1:], LANES, axis=1).astype(BF)
    return np.concatenate(split(table[:, :-1]), axis=1), last


def phase_table(hist, delay):
    cos, sin = turns(hist // 2, np.arange(1, delay + 1))
    return np.concatenate(split(np.concatenate([cos - 1.0, sin])), axis=1)


def inverse_table(hist, taps):
    cos, sin = turns(hist // 2, np.arange(W) + taps - 1)
    return np.concatenate(split(np.concatenate([cos, -sin]).T * (2.0 / hist)), axis=1)


def call(kernel, name, out_shape, *args, scalars=1, far=(), scratch=(), limit=16, products=0):
    vmem = pl.BlockSpec(memory_space=pltpu.VMEM)
    smem = pl.BlockSpec(memory_space=pltpu.SMEM)
    hbm = pl.BlockSpec(memory_space=pltpu.HBM)
    places = [smem] * scalars + [vmem] * (len(args) - scalars)
    args = list(args)
    for i in far:
        places[i] = hbm
        args[i] = pltpu.with_memory_space_constraint(jnp.asarray(args[i]), pltpu.HBM)
    return pl.pallas_call(
        kernel,
        in_specs=places,
        out_specs=[vmem] * len(out_shape),
        out_shape=out_shape,
        scratch_shapes=list(scratch),
        cost_estimate=pl.CostEstimate(flops=2 * products, bytes_accessed=0, transcendentals=0) if products else None,
        compiler_params=pltpu.CompilerParams(vmem_limit_bytes=limit * 1024 * 1024),
        name=name,
    )(*args)


def array(*shape, dtype=BF):
    return jax.ShapeDtypeStruct(shape, dtype)


def near(*shape, dtype=BF):
    return pltpu.VMEM(shape, dtype)


def block(start, size):
    return pl.ds(pl.multiple_of(start, LANES), size)


def hot(mask):
    return mask.astype(F32).astype(BF)


def fetch(pairs, sems):
    return [pltpu.make_async_copy(a, b, sems.at[i]) for i, (a, b) in enumerate(pairs)]


def project_kernel(
    place, loads_far, forward_far, shapes_far, taps_far, offsets_far, coef_far,
    sent, lft, shapes, stack, coef, loads, forward, taps, offsets, sems,
):
    rows, half = shapes.shape
    hist, width = lft.shape[0], sent.shape[1]
    start, later = quarter_start(place, 1, 2 * half), quarter_start(place, 0, 2 * half)
    base = (1 - (place[0] & 1)) * half
    step = TILE
    top, left = slice(0, hist // 2), slice(0, step)
    low, right = slice(hist // 2, hist), slice(step, rows)
    pairs = [
        (forward_far.at[top, :], forward.at[top, :]),
        (loads_far.at[left, :], loads.at[left, :]),
        (loads_far.at[right, :], loads.at[right, :]),
        (forward_far.at[low, :], forward.at[low, :]),
    ]
    first = len(pairs)
    pairs += [
        (coef_far, coef),
        (offsets_far, offsets),
        (shapes_far.at[:, block(base + start, width)], shapes.at[:, block(start, width)]),
        (taps_far, taps),
        (shapes_far.at[:, block(base + later, width)], shapes.at[:, block(later, width)]),
    ]
    copies = fetch(pairs, sems)
    for copy in copies[:first]:
        copy.start()
    copies[0].wait()
    copies[1].wait()
    lft[top, left] = dot(forward[top, :], loads[left, :], NT).astype(BF)
    copies[2].wait()
    for copy in copies[first:]:
        copy.start()
    lft[top, right] = dot(forward[top, :], loads[right, :], NT).astype(BF)
    copies[3].wait()
    for part in (left, right):
        lft[low, part] = dot(forward[low, :], loads[part, :], NT).astype(BF)
    for copy in copies[first : first + 3]:
        copy.wait()
    count = taps.shape[0] - 1
    for c in range(0, width, step):
        sent[:hist, c : c + step] = dot(lft[...], shapes[:, block(start + c, step)]).astype(BF)
    sent[hist:, :] = jnp.zeros((EXTRA, width), BF)
    sent[hist : hist + 2, : coef.shape[1]] = coef[...]
    copies[first + 3].wait()
    for r in range(0, count, 64):
        stack[r : r + 64, :] = taps[r : r + 64, :].astype(BF)
    index = lax.broadcasted_iota(I32, (EXTRA, taps.shape[1]), 0)
    end = taps[count : count + 1, :]
    tail = jnp.where(index == 0, end, jnp.where(index == 1, offsets[...].astype(F32), 0.0))
    stack[count:, :] = tail.astype(BF)
    copies[first + 4].wait()


def project_rest_kernel(place, lft, shapes, after, sent):
    width = sent.shape[1]
    later = quarter_start(place, 0, 4 * width)
    for c in range(0, width, TILE):
        sent[:, c : c + TILE] = dot(lft[...], shapes[:, block(later + c, TILE)]).astype(BF)


def quarter_start(place, which, modes):
    return (((place[0] >> 1) & 1) ^ which) * (modes // 4)


def gather_taps(base, stack, order):
    count = stack.shape[0] - EXTRA
    mode = lax.broadcasted_iota(I32, (TILE, stack.shape[1]), 0) + base
    picked = dot(stack[...], hot(mode == order[...]), NT)
    tail = picked[count:]
    return picked[:count].astype(BF), tail[0:1], tail[1:2].astype(I32)


def spectrum_of(main, end, offset, table, last, phase):
    half = table.shape[0] // 2
    delay = phase.shape[1] // 2
    resp = dot(table[...], jnp.concatenate([main, main], axis=0))
    resp = resp + jnp.tile(last[...].astype(F32), (1, TILE // LANES)) * end
    which = hot(lax.broadcasted_iota(I32, (delay, TILE), 0) + 1 == offset)
    turn = dot(phase[...], jnp.concatenate([which, which], axis=0))
    cos, sin = turn[:half] + 1.0, turn[half:]
    re, im = resp[:half], resp[half:]
    return cos * re - sin * im, sin * re + cos * im


def spectrum_tiles(base, stack, order, table, last, phase, spec):
    half = spec.shape[0] // 2
    for c in range(0, spec.shape[1], TILE):
        parts = spectrum_of(*gather_taps(base + c, stack, order), table, last, phase)
        spec[:half, c : c + TILE], spec[half:, c : c + TILE] = parts


def spectrum_kernel(
    place, stack, order, shapes_far, table_far, last_far, phase_far, inverse_far,
    spec, shapes, table, last, phase, inverse, sems,
):
    half, modes = shapes.shape[1], shapes_far.shape[1]
    near = (place[0] & 1) * half
    copies = fetch(
        [
            (table_far, table),
            (last_far, last),
            (phase_far, phase),
            (shapes_far.at[:, block(near, half)], shapes),
            (inverse_far, inverse),
        ],
        sems,
    )
    for copy in copies:
        copy.start()
    width = spec.shape[1]
    start = near + quarter_start(place, 1, modes)
    tiles = range(0, width, TILE)
    picked = [gather_taps(start + c, stack, order) for c in tiles]
    for copy in copies[:3]:
        copy.wait()
    top = spec.shape[0] // 2
    for c, parts in zip(tiles, picked):
        spec[:top, c : c + TILE], spec[top:, c : c + TILE] = spectrum_of(*parts, table, last, phase)
    for copy in copies[3:]:
        copy.wait()


def spectrum_rest_kernel(place, stack, order, table, last, phase, after, spec):
    modes = order.shape[1]
    start = (place[0] & 1) * (modes // 2) + quarter_start(place, 0, modes)
    spectrum_tiles(start, stack, order, table, last, phase, spec)


def impose(total, tre, tim, inverse):
    half = tre.shape[0]
    re, im = total[:half], total[half:]
    product = jnp.concatenate([re * tre - im * tim, re * tim + im * tre], axis=0)
    high = product.astype(BF)
    low = (product - high.astype(F32)).astype(BF)
    both = dot(inverse[...], jnp.concatenate([high, high], axis=0))
    return both + dot(inverse[:, : 2 * half], low)


def respond_kernel(which, place, lft, shapes, other, spec, inverse, coef, out):
    hist, width = spec.shape
    half = hist // 2
    start = quarter_start(place, which, 4 * width)
    for c in range(0, width, TILE):
        total = dot(lft[...], shapes[:, block(start + c, TILE)]) + other[:hist, c : c + TILE].astype(F32)
        result = impose(total, spec[:half, c : c + TILE], spec[half:, c : c + TILE], inverse)
        out[:W, c : c + TILE] = result.astype(out.dtype)
    if out.shape[0] > W:
        out[W:, :] = jnp.zeros((EXTRA, width), BF)
        out[W : W + 2, : coef.shape[1]] = coef[...]
        out[W + 2 : W + 4, :LANES] = other[hist : hist + 2, :LANES]


def turns_of(core):
    return 1, 2, 3


def fold_kernel(place, own, got, coef, other, keep, known, first, second, third):
    z = place[0] >> 2
    size = keep.shape[1]
    hist = other.shape[0] - EXTRA
    known[...] = jnp.zeros(known.shape, BF)
    known[0:2, :] = coef[...]
    known[2:4, :] = other[hist : hist + 2, :LANES]
    known[4:8, :] = got[W : W + 4, :LANES]
    for d, out in zip((0, *turns_of(place[0] & 1)), (keep, first, second, third)):
        where = block((z ^ d) * size, size)
        total = own[:, where] + got[:W, where].astype(F32)
        out[:W, :] = total.astype(out.dtype)
        if out.shape[0] > W:
            out[W:, :] = known[...]


def settle_kernel(keep, first, second, third, out):
    total = keep[...]
    for got in (first, second, third):
        total = total + got[:W, :].astype(F32)
    out[...] = total.astype(BF)


def mask_of(place, devices, modes):
    me = place[0]
    if devices == 16:
        return ((me & 1) * 8 + (me & 2) * 2 + (me >> 2)) * (modes // 16)
    return (me & 1) * (modes // 2)


def pick_kernel(devices, place, partner, after, pick):
    modes = partner.shape[1]
    mask = mask_of(place, devices, modes)
    mates = [partner[:, block(c ^ mask, LANES)] ^ mask for c in range(0, modes, LANES)]
    mates = jnp.concatenate(mates, axis=1)
    for c in range(0, modes, 256):
        pick[c : c + 256, :] = hot(lax.broadcasted_iota(I32, (256, modes), 0) + c == mates)


def mixers_kernel(place, order, known, first, second, third, after, coef, held):
    me = place[0]
    held[...] = jnp.zeros(held.shape, F32)
    for z, rows in zip((0, *turns_of(me & 1)), (known, first, second, third)):
        top = rows.shape[0] - EXTRA
        for low in range(4):
            where = block((me ^ (4 * z + low)) * LANES, LANES)
            held[0:2, where] = rows[top : top + EXTRA, :].astype(F32)[2 * low : 2 * low + 2]
    mixers(order, mask_of(place, 16, order.shape[1]), held, coef)


def mixers(order, mask, held, coef):
    modes = order.shape[1]
    table = held[...].astype(BF)
    slots = order[...] ^ mask
    for c in range(0, modes, TILE):
        coef[:, c : c + TILE] = dot(table, hot(lax.broadcasted_iota(I32, (TILE, modes), 0) + c == slots), NT)


def plain_mixers_kernel(devices, place, order, every, coef, held):
    held[...] = jnp.zeros(held.shape, F32)
    held[0:2, :] = every[...].astype(F32)
    mixers(order, mask_of(place, devices, order.shape[1]), held, coef)


def join_kernel(*refs):
    *parts, out = refs
    start = 0
    for part in parts:
        out[:, start : start + part.shape[1]] = part[...]
        start += part.shape[1]


def join(*parts, after=None):
    width = sum(part.shape[1] for part in parts)
    kernel = join_kernel if after is None else lambda _, *refs: join_kernel(*refs)
    first = () if after is None else (after,)
    return call(kernel, "join", [array(parts[0].shape[0], width)], *first, *parts, scalars=0)[0]


def mate_kernel(mine, pick, out):
    half = mine.shape[1]
    for c in range(0, 2 * half, TILE):
        out[:, c : c + TILE] = dot(mine[...], pick[:half, c : c + TILE])


def expand_kernel(devices, place, mine, theirs, mates, pick, coef, near, far, out, near_pair, far_pair):
    half = mine.shape[1]
    mask = mask_of(place, devices, 2 * half)
    for q, (direct, pair) in enumerate(((mine, near_pair), (theirs, far_pair))):
        for c in range(0, half, TILE):
            k = q * half + c
            here = slice(k, k + TILE)
            across = mates[:, here] + dot(theirs[...], pick[half:, here])
            mixed = coef[0:1, here] * direct[:, c : c + TILE].astype(F32) + coef[1:2, here] * across
            for d in range(0, TILE, LANES):
                pair[:, block((mask ^ (k + d)) & (half - 1), LANES)] = mixed[:, d : d + LANES].astype(BF)
    rows = out.shape[0]
    for r in range(0, rows, TILE):
        total = dot(near[r : r + TILE, :], near_pair[...], NT) + dot(far[r : r + TILE, :], far_pair[...], NT)
        out[r : r + TILE, :] = total.astype(BF)


def swap(x, devices, bits, odd=None):
    odd = bits if odd is None else odd
    return lax.ppermute(x, "frdm", [(i, i ^ (odd if i & 1 else bits)) for i in range(devices)])


def shards(devices, loads, shapes, mode_order, partner, taps, offsets, coef):
    rows, modes = shapes.shape
    hist, count = loads.shape[1], taps.shape[1]
    half, quarter = modes // 2, modes // 4
    place = lax.axis_index("frdm").astype(I32).reshape(1)
    forward = forward_table(hist)
    tap_forward, last = tap_table(hist, count)
    phase = phase_table(hist, hist - W - count + 1)
    inverse = inverse_table(hist, count)
    order, mates, offsets, taps = mode_order[None], partner[None], offsets[None], taps.T

    sent, lft, far, stack, coef_near = call(
        project_kernel, "project",
        [near(hist + EXTRA, quarter), near(hist, rows), near(rows, half), near(count - 1 + EXTRA, modes), near(*coef.shape)],
        place, loads, forward, shapes, taps, offsets, coef, far=range(1, 7),
        scratch=[
            pltpu.VMEM(loads.shape, BF), pltpu.VMEM(forward.shape, BF), pltpu.VMEM(taps.shape, F32),
            pltpu.VMEM(offsets.shape, I32), pltpu.SemaphoreType.DMA((9,)),
        ],
        limit=24,
    )
    got = swap(sent, devices, 1)
    spec, shapes, *held = call(
        spectrum_kernel, "spectrum",
        [near(hist, quarter, dtype=F32), near(rows, half)] + [near(*t.shape) for t in (tap_forward, last, phase, inverse)],
        place, stack, order, shapes, tap_forward, last, phase, inverse, far=range(3, 8),
        scratch=[pltpu.SemaphoreType.DMA((5,))],
    )
    inverse = held.pop()

    def respond(which, got, spec, out):
        kernel = functools.partial(respond_kernel, which)
        return call(kernel, "respond", [out], place, lft, shapes, got, spec, inverse, coef_near)[0]

    away = respond(1, got, spec, array(W + EXTRA, quarter))
    sent = call(project_rest_kernel, "project_rest", [array(hist, quarter)], place, lft, far, away, products=4 * hist * rows * quarter)[0]
    rest = swap(sent, devices, 1)
    spec = call(
        spectrum_rest_kernel, "spectrum_rest", [array(hist, quarter, dtype=F32)], place, stack, order, *held, away, products=10**10
    )[0]
    own = respond(0, rest, spec, array(W, quarter, dtype=F32))

    def pair(after):
        kernel = functools.partial(pick_kernel, devices)
        return call(kernel, "pick", [near(modes, modes)], place, mates, after)[0]

    if devices == 16:
        size = modes // devices
        away = swap(away, devices, 2)
        keep, known, *parts = call(
            fold_kernel, "fold", [array(W, size, dtype=F32), array(EXTRA, LANES)] + [array(W + EXTRA, size)] * 3,
            place, own, away, coef_near, got,
        )
        ways = zip(turns_of(0), turns_of(1))
        parts = [swap(part, devices, 4 * even, 4 * odd) for part, (even, odd) in zip(parts, ways)]
        total = call(settle_kernel, "settle", [array(W, size)], keep, *parts, scalars=0)[0]
        spread = [swap(total, devices, 4 * d) for d in (1, 2, 3)]
        resp = join(total, *spread)
        mode_coef = call(
            mixers_kernel, "mixers", [array(8, modes, dtype=F32)],
            place, order, known, *parts, resp, scratch=[pltpu.VMEM((8, modes), F32)],
        )[0]
        pick = pair(mode_coef)
        mine = join(resp, swap(resp, devices, 2), after=pick)
    else:
        pick = pair(mates)
        mode_coef = call(
            functools.partial(plain_mixers_kernel, devices), "mixers", [array(8, modes, dtype=F32)],
            place, order, lax.all_gather(coef, "frdm", axis=1, tiled=True), scratch=[pltpu.VMEM((8, modes), F32)],
        )[0]
        away = away[:W].astype(F32)
        resp = jnp.where(place[0] & 2, jnp.concatenate([away, own], axis=1), jnp.concatenate([own, away], axis=1))
        groups = [list(range(c, devices, 2)) for c in range(2)]
        mine = lax.psum(resp, "frdm", axis_index_groups=groups).astype(BF)
    theirs = swap(mine, devices, 1)
    first = call(mate_kernel, "mate", [array(W, modes, dtype=F32)], mine, pick, scalars=0)[0]
    return call(
        functools.partial(expand_kernel, devices), "expand", [array(rows, W)],
        place, mine, theirs, first, pick, mode_coef, shapes, far,
        scratch=[pltpu.VMEM((W, half), BF)] * 2,
    )[0]


def solution(mesh):
    in_specs = (P(("cases", "frdm"), None), P("frdm", None), P(), P(), P(), P(), P(None, "frdm"))
    out_specs = P(("cases", "frdm"), None)
    body = functools.partial(shards, mesh.shape["frdm"])
    return jax.shard_map(body, mesh=mesh, in_specs=in_specs, out_specs=out_specs, check_vma=False)
```

```python
import functools

import jax
import jax.numpy as jnp
import numpy as np
from jax import lax
from jax.experimental import pallas as pl
from jax.experimental.pallas import tpu as pltpu
from jax.sharding import PartitionSpec as P

W = 256
LANES = 128
TILE = 512
EXTRA = 16
BF = jnp.bfloat16
F32 = jnp.float32
I32 = jnp.int32
NT = (((1,), (1,)), ((), ()))
NN = (((1,), (0,)), ((), ()))


def dot(a, b, dims=NN):
    return lax.dot_general(a, b, dims, preferred_element_type=F32)


def split(table):
    high = table.astype(BF)
    low = (table - high.astype(np.float64)).astype(BF)
    return high, low


def turns(half, n):
    odd = 2 * np.arange(half)[:, None] + 1
    angle = (odd * n[None, :]) % (4 * half) * (np.pi / (2 * half))
    return np.cos(angle), np.sin(angle)


def forward_table(hist):
    cos, sin = turns(hist // 2, np.arange(hist))
    return np.concatenate([cos, -sin]).astype(BF)


def tap_table(hist, taps):
    cos, sin = turns(hist // 2, np.arange(taps))
    table = np.concatenate([cos, -sin])
    last = np.repeat(table[:, -1:], LANES, axis=1).astype(BF)
    return np.concatenate(split(table[:, :-1]), axis=1), last


def phase_table(hist, delay):
    cos, sin = turns(hist // 2, np.arange(1, delay + 1))
    return np.concatenate(split(np.concatenate([cos - 1.0, sin])), axis=1)


def inverse_table(hist, taps):
    cos, sin = turns(hist // 2, np.arange(W) + taps - 1)
    return np.concatenate(split(np.concatenate([cos, -sin]).T * (2.0 / hist)), axis=1)


def call(kernel, name, out_shape, *args, scalars=1, far=(), scratch=(), limit=16, products=0):
    vmem = pl.BlockSpec(memory_space=pltpu.VMEM)
    smem = pl.BlockSpec(memory_space=pltpu.SMEM)
    hbm = pl.BlockSpec(memory_space=pltpu.HBM)
    places = [smem] * scalars + [vmem] * (len(args) - scalars)
    args = list(args)
    for i in far:
        places[i] = hbm
        args[i] = pltpu.with_memory_space_constraint(jnp.asarray(args[i]), pltpu.HBM)
    return pl.pallas_call(
        kernel,
        in_specs=places,
        out_specs=[vmem] * len(out_shape),
        out_shape=out_shape,
        scratch_shapes=list(scratch),
        cost_estimate=pl.CostEstimate(flops=2 * products, bytes_accessed=0, transcendentals=0) if products else None,
        compiler_params=pltpu.CompilerParams(vmem_limit_bytes=limit * 1024 * 1024),
        name=name,
    )(*args)


def array(*shape, dtype=BF):
    return jax.ShapeDtypeStruct(shape, dtype)


def near(*shape, dtype=BF):
    return pltpu.VMEM(shape, dtype)


def block(start, size):
    return pl.ds(pl.multiple_of(start, LANES), size)


def hot(mask):
    return mask.astype(F32).astype(BF)


def fetch(pairs, sems):
    return [pltpu.make_async_copy(a, b, sems.at[i]) for i, (a, b) in enumerate(pairs)]


def project_kernel(
    place, loads_far, forward_far, shapes_far, taps_far, offsets_far, coef_far,
    sent, lft, shapes, stack, coef, loads, forward, taps, offsets, sems,
):
    rows, half = shapes.shape
    hist, width = lft.shape[0], sent.shape[1]
    start, later = quarter_start(place, 1, 2 * half), quarter_start(place, 0, 2 * half)
    base = (1 - (place[0] & 1)) * half
    step = TILE
    top, left = slice(0, hist // 2), slice(0, step)
    low, right = slice(hist // 2, hist), slice(step, rows)
    pairs = [
        (forward_far.at[top, :], forward.at[top, :]),
        (loads_far.at[left, :], loads.at[left, :]),
        (loads_far.at[right, :], loads.at[right, :]),
        (forward_far.at[low, :], forward.at[low, :]),
    ]
    first = len(pairs)
    pairs += [
        (coef_far, coef),
        (offsets_far, offsets),
        (shapes_far.at[:, block(base + start, width)], shapes.at[:, block(start, width)]),
        (taps_far, taps),
        (shapes_far.at[:, block(base + later, width)], shapes.at[:, block(later, width)]),
    ]
    copies = fetch(pairs, sems)
    for copy in copies[:first]:
        copy.start()
    copies[0].wait()
    copies[1].wait()
    lft[top, left] = dot(forward[top, :], loads[left, :], NT).astype(BF)
    copies[2].wait()
    for copy in copies[first:]:
        copy.start()
    lft[top, right] = dot(forward[top, :], loads[right, :], NT).astype(BF)
    copies[3].wait()
    for part in (left, right):
        lft[low, part] = dot(forward[low, :], loads[part, :], NT).astype(BF)
    for copy in copies[first : first + 3]:
        copy.wait()
    count = taps.shape[0] - 1
    for c in range(0, width, step):
        sent[:hist, c : c + step] = dot(lft[...], shapes[:, block(start + c, step)]).astype(BF)
    sent[hist:, :] = jnp.zeros((EXTRA, width), BF)
    sent[hist : hist + 2, : coef.shape[1]] = coef[...]
    copies[first + 3].wait()
    for r in range(0, count, 64):
        stack[r : r + 64, :] = taps[r : r + 64, :].astype(BF)
    index = lax.broadcasted_iota(I32, (EXTRA, taps.shape[1]), 0)
    end = taps[count : count + 1, :]
    tail = jnp.where(index == 0, end, jnp.where(index == 1, offsets[...].astype(F32), 0.0))
    stack[count:, :] = tail.astype(BF)
    copies[first + 4].wait()


def project_rest_kernel(place, lft, shapes, after, sent):
    width = sent.shape[1]
    later = quarter_start(place, 0, 4 * width)
    for c in range(0, width, TILE):
        sent[:, c : c + TILE] = dot(lft[...], shapes[:, block(later + c, TILE)]).astype(BF)


def quarter_start(place, which, modes):
    return (((place[0] >> 1) & 1) ^ which) * (modes // 4)


def gather_taps(base, stack, order):
    count = stack.shape[0] - EXTRA
    mode = lax.broadcasted_iota(I32, (TILE, stack.shape[1]), 0) + base
    picked = dot(stack[...], hot(mode == order[...]), NT)
    tail = picked[count:]
    return picked[:count].astype(BF), tail[0:1], tail[1:2].astype(I32)


def spectrum_of(main, end, offset, table, last, phase):
    half = table.shape[0] // 2
    delay = phase.shape[1] // 2
    resp = dot(table[...], jnp.concatenate([main, main], axis=0))
    resp = resp + jnp.tile(last[...].astype(F32), (1, TILE // LANES)) * end
    which = hot(lax.broadcasted_iota(I32, (delay, TILE), 0) + 1 == offset)
    turn = dot(phase[...], jnp.concatenate([which, which], axis=0))
    cos, sin = turn[:half] + 1.0, turn[half:]
    re, im = resp[:half], resp[half:]
    return cos * re - sin * im, sin * re + cos * im


def spectrum_tiles(base, stack, order, table, last, phase, spec):
    half = spec.shape[0] // 2
    for c in range(0, spec.shape[1], TILE):
        parts = spectrum_of(*gather_taps(base + c, stack, order), table, last, phase)
        spec[:half, c : c + TILE], spec[half:, c : c + TILE] = parts


def spectrum_kernel(
    place, stack, order, shapes_far, table_far, last_far, phase_far, inverse_far,
    spec, shapes, table, last, phase, inverse, sems,
):
    half, modes = shapes.shape[1], shapes_far.shape[1]
    near = (place[0] & 1) * half
    copies = fetch(
        [
            (table_far, table),
            (last_far, last),
            (phase_far, phase),
            (shapes_far.at[:, block(near, half)], shapes),
            (inverse_far, inverse),
        ],
        sems,
    )
    for copy in copies:
        copy.start()
    width = spec.shape[1]
    start = near + quarter_start(place, 1, modes)
    tiles = range(0, width, TILE)
    picked = [gather_taps(start + c, stack, order) for c in tiles]
    for copy in copies[:3]:
        copy.wait()
    top = spec.shape[0] // 2
    for c, parts in zip(tiles, picked):
        spec[:top, c : c + TILE], spec[top:, c : c + TILE] = spectrum_of(*parts, table, last, phase)
    for copy in copies[3:]:
        copy.wait()


def spectrum_rest_kernel(place, stack, order, table, last, phase, after, spec):
    modes = order.shape[1]
    start = (place[0] & 1) * (modes // 2) + quarter_start(place, 0, modes)
    spectrum_tiles(start, stack, order, table, last, phase, spec)


def impose(total, tre, tim, inverse):
    half = tre.shape[0]
    re, im = total[:half], total[half:]
    product = jnp.concatenate([re * tre - im * tim, re * tim + im * tre], axis=0)
    high = product.astype(BF)
    low = (product - high.astype(F32)).astype(BF)
    both = dot(inverse[...], jnp.concatenate([high, high], axis=0))
    return both + dot(inverse[:, : 2 * half], low)


def respond_kernel(which, place, lft, shapes, other, spec, inverse, coef, out):
    hist, width = spec.shape
    half = hist // 2
    start = quarter_start(place, which, 4 * width)
    for c in range(0, width, TILE):
        total = dot(lft[...], shapes[:, block(start + c, TILE)]) + other[:hist, c : c + TILE].astype(F32)
        result = impose(total, spec[:half, c : c + TILE], spec[half:, c : c + TILE], inverse)
        out[:W, c : c + TILE] = result.astype(out.dtype)
    if out.shape[0] > W:
        out[W:, :] = jnp.zeros((EXTRA, width), BF)
        out[W : W + 2, : coef.shape[1]] = coef[...]
        out[W + 2 : W + 4, :LANES] = other[hist : hist + 2, :LANES]


def turns_of(core):
    return 1, 2, 3


def fold_kernel(place, own, got, coef, other, keep, known, first, second, third):
    z = place[0] >> 2
    size = keep.shape[1]
    hist = other.shape[0] - EXTRA
    known[...] = jnp.zeros(known.shape, BF)
    known[0:2, :] = coef[...]
    known[2:4, :] = other[hist : hist + 2, :LANES]
    known[4:8, :] = got[W : W + 4, :LANES]
    for d, out in zip((0, *turns_of(place[0] & 1)), (keep, first, second, third)):
        where = block((z ^ d) * size, size)
        total = own[:, where] + got[:W, where].astype(F32)
        out[:W, :] = total.astype(out.dtype)
        if out.shape[0] > W:
            out[W:, :] = known[...]


def settle_kernel(keep, first, second, third, out):
    total = keep[...]
    for got in (first, second, third):
        total = total + got[:W, :].astype(F32)
    out[...] = total.astype(BF)


def mask_of(place, devices, modes):
    me = place[0]
    if devices == 16:
        return ((me & 1) * 8 + (me & 2) * 2 + (me >> 2)) * (modes // 16)
    return (me & 1) * (modes // 2)


def pick_kernel(devices, place, partner, after, pick):
    modes = partner.shape[1]
    mask = mask_of(place, devices, modes)
    mates = [partner[:, block(c ^ mask, LANES)] ^ mask for c in range(0, modes, LANES)]
    mates = jnp.concatenate(mates, axis=1)
    for c in range(0, modes, 256):
        pick[c : c + 256, :] = hot(lax.broadcasted_iota(I32, (256, modes), 0) + c == mates)


def mixers_kernel(place, order, known, first, second, third, after, coef, held):
    me = place[0]
    held[...] = jnp.zeros(held.shape, F32)
    for z, rows in zip((0, *turns_of(me & 1)), (known, first, second, third)):
        top = rows.shape[0] - EXTRA
        for low in range(4):
            where = block((me ^ (4 * z + low)) * LANES, LANES)
            held[0:2, where] = rows[top : top + EXTRA, :].astype(F32)[2 * low : 2 * low + 2]
    mixers(order, mask_of(place, 16, order.shape[1]), held, coef)


def mixers(order, mask, held, coef):
    modes = order.shape[1]
    table = held[...].astype(BF)
    slots = order[...] ^ mask
    for c in range(0, modes, TILE):
        coef[:, c : c + TILE] = dot(table, hot(lax.broadcasted_iota(I32, (TILE, modes), 0) + c == slots), NT)


def plain_mixers_kernel(devices, place, order, every, coef, held):
    held[...] = jnp.zeros(held.shape, F32)
    held[0:2, :] = every[...].astype(F32)
    mixers(order, mask_of(place, devices, order.shape[1]), held, coef)


def line_kernel(total, third, second, first, out):
    join_kernel(total, first, second, third, out)


def join_kernel(*refs):
    *parts, out = refs
    start = 0
    for part in parts:
        out[:, start : start + part.shape[1]] = part[...]
        start += part.shape[1]


def join(*parts, after=None):
    width = sum(part.shape[1] for part in parts)
    kernel = join_kernel if after is None else lambda _, *refs: join_kernel(*refs)
    first = () if after is None else (after,)
    return call(kernel, "join", [array(parts[0].shape[0], width)], *first, *parts, scalars=0)[0]


def mate_kernel(mine, pick, out):
    half = mine.shape[1]
    for c in range(0, 2 * half, TILE):
        out[:, c : c + TILE] = dot(mine[...], pick[:half, c : c + TILE])


def expand_kernel(devices, place, mine, theirs, mates, pick, coef, near, far, out, near_pair, far_pair):
    half = mine.shape[1]
    mask = mask_of(place, devices, 2 * half)
    for q, (direct, pair) in enumerate(((mine, near_pair), (theirs, far_pair))):
        for c in range(0, half, TILE):
            k = q * half + c
            here = slice(k, k + TILE)
            across = mates[:, here] + dot(theirs[...], pick[half:, here])
            mixed = coef[0:1, here] * direct[:, c : c + TILE].astype(F32) + coef[1:2, here] * across
            for d in range(0, TILE, LANES):
                pair[:, block((mask ^ (k + d)) & (half - 1), LANES)] = mixed[:, d : d + LANES].astype(BF)
    rows = out.shape[0]
    for r in range(0, rows, TILE):
        total = dot(near[r : r + TILE, :], near_pair[...], NT) + dot(far[r : r + TILE, :], far_pair[...], NT)
        out[r : r + TILE, :] = total.astype(BF)


def swap(x, devices, bits, odd=None):
    odd = bits if odd is None else odd
    return lax.ppermute(x, "frdm", [(i, i ^ (odd if i & 1 else bits)) for i in range(devices)])


def shards(devices, loads, shapes, mode_order, partner, taps, offsets, coef):
    rows, modes = shapes.shape
    hist, count = loads.shape[1], taps.shape[1]
    half, quarter = modes // 2, modes // 4
    place = lax.axis_index("frdm").astype(I32).reshape(1)
    forward = forward_table(hist)
    tap_forward, last = tap_table(hist, count)
    phase = phase_table(hist, hist - W - count + 1)
    inverse = inverse_table(hist, count)
    order, mates, offsets, taps = mode_order[None], partner[None], offsets[None], taps.T

    sent, lft, far, stack, coef_near = call(
        project_kernel, "project",
        [near(hist + EXTRA, quarter), near(hist, rows), near(rows, half), near(count - 1 + EXTRA, modes), near(*coef.shape)],
        place, loads, forward, shapes, taps, offsets, coef, far=range(1, 7),
        scratch=[
            pltpu.VMEM(loads.shape, BF), pltpu.VMEM(forward.shape, BF), pltpu.VMEM(taps.shape, F32),
            pltpu.VMEM(offsets.shape, I32), pltpu.SemaphoreType.DMA((9,)),
        ],
        limit=24,
    )
    got = swap(sent, devices, 1)
    spec, shapes, *held = call(
        spectrum_kernel, "spectrum",
        [near(hist, quarter, dtype=F32), near(rows, half)] + [near(*t.shape) for t in (tap_forward, last, phase, inverse)],
        place, stack, order, shapes, tap_forward, last, phase, inverse, far=range(3, 8),
        scratch=[pltpu.SemaphoreType.DMA((5,))],
    )
    inverse = held.pop()

    def respond(which, got, spec, out):
        kernel = functools.partial(respond_kernel, which)
        return call(kernel, "respond", [out], place, lft, shapes, got, spec, inverse, coef_near)[0]

    away = respond(1, got, spec, array(W + EXTRA, quarter))
    sent = call(project_rest_kernel, "project_rest", [array(hist, quarter)], place, lft, far, away, products=4 * hist * rows * quarter)[0]
    rest = swap(sent, devices, 1)
    spec = call(
        spectrum_rest_kernel, "spectrum_rest", [array(hist, quarter, dtype=F32)], place, stack, order, *held, away, products=10**10
    )[0]
    own = respond(0, rest, spec, array(W, quarter, dtype=F32))

    def pair(after):
        kernel = functools.partial(pick_kernel, devices)
        return call(kernel, "pick", [near(modes, modes)], place, mates, after)[0]

    if devices == 16:
        size = modes // devices
        away = swap(away, devices, 2)
        keep, known, *parts = call(
            fold_kernel, "fold", [array(W, size, dtype=F32), array(EXTRA, LANES)] + [array(W + EXTRA, size)] * 3,
            place, own, away, coef_near, got,
        )
        ways = zip(turns_of(0), turns_of(1))
        parts = [swap(part, devices, 4 * even, 4 * odd) for part, (even, odd) in zip(parts, ways)]
        total = call(settle_kernel, "settle", [array(W, size)], keep, *parts, scalars=0)[0]
        spread = [swap(total, devices, 4 * d) for d in (3, 2, 1)]
        resp = call(line_kernel, "line", [array(W, quarter)], total, *spread, scalars=0)[0]
        mode_coef = call(
            mixers_kernel, "mixers", [array(8, modes, dtype=F32)],
            place, order, known, *parts, resp, scratch=[pltpu.VMEM((8, modes), F32)],
        )[0]
        pick = pair(mode_coef)
        mine = join(resp, swap(resp, devices, 2), after=pick)
    else:
        pick = pair(mates)
        mode_coef = call(
            functools.partial(plain_mixers_kernel, devices), "mixers", [array(8, modes, dtype=F32)],
            place, order, lax.all_gather(coef, "frdm", axis=1, tiled=True), scratch=[pltpu.VMEM((8, modes), F32)],
        )[0]
        away = away[:W].astype(F32)
        resp = jnp.where(place[0] & 2, jnp.concatenate([away, own], axis=1), jnp.concatenate([own, away], axis=1))
        groups = [list(range(c, devices, 2)) for c in range(2)]
        mine = lax.psum(resp, "frdm", axis_index_groups=groups).astype(BF)
    theirs = swap(mine, devices, 1)
    first = call(mate_kernel, "mate", [array(W, modes, dtype=F32)], mine, pick, scalars=0)[0]
    return call(
        functools.partial(expand_kernel, devices), "expand", [array(rows, W)],
        place, mine, theirs, first, pick, mode_coef, shapes, far,
        scratch=[pltpu.VMEM((W, half), BF)] * 2,
    )[0]


def solution(mesh):
    in_specs = (P(("cases", "frdm"), None), P("frdm", None), P(), P(), P(), P(), P(None, "frdm"))
    out_specs = P(("cases", "frdm"), None)
    body = functools.partial(shards, mesh.shape["frdm"])
    return jax.shard_map(body, mesh=mesh, in_specs=in_specs, out_specs=out_specs, check_vma=False)
```
